128 devices in a mesh: dp: 16 (over z_hi, x, core), space: 8 (over y, z_lo).
Axes of the slice: x: 4, y: 4, z: 4 (z_hi: 2, z_lo: 2; z = z_hi * 2 + z_lo), core: 2. Of those that a mesh axis runs over, the one named last changes fastest.
Arguments:
- inputs: bfloat16 [16, 8, 4, 8, 8, 128], P('dp', 'space'), may hold values from -6 to 6
- pre_act: bfloat16 [16, 8, 16, 8, 8, 128], P('dp', 'space'), may hold values from -6 to 6
- out_grad: bfloat16 [16, 8, 32, 16, 512], P('dp', 'space'), may hold values from -6 to 6
- conv1_weight: bfloat16 [27, 4, 16], replicated, may hold values from -0.3125 to 0.3125
- conv2_weight: bfloat16 [27, 16, 32], replicated, may hold values from -0.21875 to 0.21875
Outputs:
- input_grad: bfloat16 [16, 8, 4, 8, 8, 128], P('dp', 'space')
- conv1_grad: float32 [27, 4, 16], replicated
- conv2_grad: float32 [27, 16, 32], replicated
The draws below stay inside these ranges and needn't reach their ends.
All inputs are finite; a program needn't handle non-finite values.
Results may differ from the reference program's by a relative error of at most 0.0049.
Values may be sent and summed in bfloat16 or wider, within the bound.
No kernel may reach another device: no remote copies, remote signals or barrier semaphores. Data moves between devices by JAX's collectives and lax.ppermute only.
A program may use at most 64 MiB of HBM per device.

```python
import jax
import jax.numpy as jnp
from jax import lax

C0 = 4
C1 = 16
C2 = 32
DZ = 8
TH = 8
TW = 128
TILES = 8
H = 16
W = 512
VOLUMES = 16
N_SPACE = 8


def levels(own_key, dims, pieces, smallest, largest):
    def one(position, shards_of):
        draws = jax.random.uniform(jax.random.fold_in(jax.random.fold_in(own_key, 6), position), (shards_of,), jnp.float32, smallest / len(pieces), largest / len(pieces))
        return jnp.repeat(jnp.exp(draws), dims[position] // shards_of).reshape((-1,) + (1,) * (len(dims) - position - 1))

    gain = one(*pieces[0])
    for cut in pieces[1:]:
        gain = gain * one(*cut)
    return gain


def gaussian(stream_key, shape, spread, reach, pieces=(), kind=jnp.bfloat16):
    values = spread * jax.random.normal(stream_key, shape, jnp.float32)
    if pieces:
        values = values * levels(stream_key, shape, pieces, -0.22, 0.18)
    return jnp.clip(values, -reach, reach).astype(kind)


def setup_inputs(seed: int = 0) -> dict:
    key_of = jax.random.split(jax.random.key(seed), 6)
    return {
        "inputs": gaussian(key_of[0], (VOLUMES, TILES, C0, DZ, TH, TW), 1.0, 6.0, ((0, 16), (1, 8))),
        "pre_act": gaussian(key_of[1], (VOLUMES, TILES, C1, DZ, TH, TW), 1.0, 6.0, ((0, 16), (1, 8))),
        "out_grad": gaussian(key_of[2], (VOLUMES, DZ, C2, H, W), 1.0, 6.0, ((0, 16), (1, 8))),
        "conv1_weight": gaussian(key_of[3], (27, C0, C1), (27 * C1) ** -0.5, 0.3125),
        "conv2_weight": gaussian(key_of[4], (27, C1, C2), (27 * C2) ** -0.5, 0.21875),
    }


leak = 0.3
numbers = ('NCDHW', 'OIDHW', 'NCDHW')

def whole_volume(tiles):
    tile_cols = N_SPACE // 2
    chans = tiles.shape[1]
    shaped = tiles.reshape(tile_cols, 2, chans, DZ, TH, TW)
    return shaped.transpose(2, 3, 1, 4, 0, 5).reshape(chans, DZ, 2 * TH, tile_cols * TW)

def split_tiles(volume):
    tile_cols = N_SPACE // 2
    chans = volume.shape[0]
    shaped = volume.reshape(chans, DZ, 2, TH, tile_cols, TW)
    return shaped.transpose(4, 2, 0, 1, 3, 5).reshape(2 * tile_cols, chans, DZ, TH, TW)

def flipped(weights):
    ins, outs = (weights.shape[1], weights.shape[2])
    return weights[::-1].reshape(3, 3, 3, ins, outs).transpose(3, 4, 0, 1, 2)

def transposed_conv(grads, weights):
    padded = jnp.pad(grads, ((0, 0), (1, 1), (1, 1), (1, 1)))
    kernel = flipped(weights).astype(jnp.float32)
    result = lax.conv_general_dilated(padded[None], kernel, (1, 1, 1), 'VALID', dimension_numbers=numbers, precision=lax.Precision.HIGHEST, preferred_element_type=jnp.float32)
    return result[0]

def weight_grad(sources, grads):
    padded = jnp.pad(sources, ((0, 0), (1, 1), (1, 1), (1, 1)))
    depth, rows, width = (grads.shape[1], grads.shape[2], grads.shape[3])
    terms = []
    for kz in range(3):
        for ky in range(3):
            for kx in range(3):
                window = padded[:, kz:kz + depth, ky:ky + rows, kx:kx + width]
                terms.append(jnp.einsum('cdhw,odhw->co', window, grads, precision=lax.Precision.HIGHEST))
    return jnp.stack(terms)

def reference(inputs, pre_act, out_grad, conv1_weight, conv2_weight):

    def one_volume(items):
        input_tiles, act_tiles, slab = items
        volume_in = whole_volume(input_tiles).astype(jnp.float32)
        volume_act = whole_volume(act_tiles).astype(jnp.float32)
        hidden = jnp.where(volume_act > 0, volume_act, leak * volume_act).astype(jnp.bfloat16)
        hidden = lax.optimization_barrier(hidden).astype(jnp.float32)
        grads = slab.transpose(1, 0, 2, 3).astype(jnp.float32)
        hidden_grad = transposed_conv(grads, conv2_weight)
        act_grad = (hidden_grad * jnp.where(volume_act > 0, 1.0, leak)).astype(jnp.bfloat16)
        act_grad = lax.optimization_barrier(act_grad).astype(jnp.float32)
        input_grad = transposed_conv(act_grad, conv1_weight).astype(jnp.bfloat16)
        return (split_tiles(input_grad), weight_grad(hidden, grads), weight_grad(volume_in, act_grad))
    input_grad, second, first = lax.map(one_volume, (inputs, pre_act, out_grad))
    scale = 1.0 / jnp.sqrt(jnp.float32(VOLUMES * DZ * H * W))
    return (input_grad, lax.optimization_barrier(jnp.sum(first, axis=0)) * scale, lax.optimization_barrier(jnp.sum(second, axis=0)) * scale)
```

```python
import itertools

import jax
import jax.numpy as jnp
from jax import lax
from jax.experimental import pallas as pl
from jax.experimental.pallas import tpu as pltpu
from jax.sharding import PartitionSpec as P

LEAK = 0.3
STRIP = 64
WIDE = 72
PAD = 80
ROWS = 8 * PAD
ALL = ("dp", "space")
F32 = jnp.float32
BF16 = jnp.bfloat16


def iota(shape, dim):
    return lax.broadcasted_iota(jnp.int32, shape, dim)


def one_hot(flags):
    return jnp.where(flags, 1.0, 0.0).astype(BF16)


def dot(a, b):
    return jnp.dot(a, b, preferred_element_type=F32)


def dot_t(a, b):
    return lax.dot_general(a, b, (((1,), (1,)), ((), ())), preferred_element_type=F32)


def call(kernel, name, outs, scratch, args, flops=1e8, size=4e6):
    return pl.pallas_call(
        kernel,
        name=name,
        out_shape=outs,
        in_specs=[pl.BlockSpec(memory_space=pltpu.VMEM)] * len(args),
        out_specs=jax.tree.map(lambda _: pl.BlockSpec(memory_space=pltpu.VMEM), outs),
        scratch_shapes=scratch,
        compiler_params=pltpu.CompilerParams(vmem_limit_bytes=40 << 20),
        cost_estimate=pl.CostEstimate(flops=int(flops), bytes_accessed=int(size), transcendentals=0),
    )(*args)


def cut_kernel(slab_ref, out_ref, wide_ref, turned_ref):
    for b in range(4):
        wide_ref[b] = slab_ref[:, :, 128 * b : 128 * b + 128].astype(F32).reshape(512, 128)
    for y in range(16):
        for b in range(4):
            turned_ref[32 * y : 32 * y + 32, 128 * b : 128 * b + 128] = wide_ref[
                b, pl.ds(y, 32, stride=16), :
            ].astype(BF16)
    p, x = iota((WIDE, 512), 0), iota((WIDE, 512), 1)
    gap = jnp.where(p < STRIP + 4, x - p, -9999)
    pick = jnp.concatenate([jnp.where(gap == STRIP * t - 2, 1.0, 0.0) for t in range(8)], axis=0)
    cut = dot_t(pick.astype(BF16), turned_ref[...])
    for t in range(8):
        out_ref[t] = cut[WIDE * t : WIDE * t + WIDE].astype(BF16)


def turn_kernel(pre_ref, in_ref, keep_ref, send_ref, edge_ref):
    r = lax.rem(lax.axis_index("space"), 2)
    a, x = iota((WIDE, 128), 0), iota((WIDE, 128), 1)
    gap = jnp.where(a < STRIP + 2, x - a, -9999)
    first, x1 = iota((8, 128), 0) == 0, iota((8, 128), 1)
    pick = jnp.concatenate(
        [
            jnp.where(gap == STRIP * r - 1, 1.0, 0.0),
            jnp.where(gap == STRIP * (1 - r) - 1, 1.0, 0.0),
            jnp.where(first & (x1 == 127 * (1 - r)), 1.0, 0.0),
            jnp.where(first & (x1 == 127 * r), 1.0, 0.0),
        ],
        axis=0,
    ).astype(BF16)
    src, dst = iota((128, 128), 0), iota((128, 128), 1)
    order = one_hot((src // 8 == dst % 16) & (src % 8 == dst // 16))
    for z in range(8):
        rows = pre_ref[:, z].astype(F32).reshape(128, 128).astype(BF16)
        got = dot(dot_t(pick, rows).astype(BF16), order).astype(BF16).astype(F32)
        keep_ref[z] = got[:WIDE].astype(BF16)
        send_ref[z] = got[WIDE : 2 * WIDE].astype(BF16)
        edge_ref[0, z] = got[2 * WIDE : 2 * WIDE + 8].astype(BF16)
        edge_ref[1, z] = got[2 * WIDE + 8 :].astype(BF16)
    gap = jnp.where(a < STRIP, x - a, -9999)
    pick = jnp.concatenate(
        [jnp.where(gap == STRIP * r, 1.0, 0.0), jnp.where(gap == STRIP * (1 - r), 1.0, 0.0)], axis=0
    ).astype(BF16)
    src, dst = iota((256, 256), 0), iota((256, 256), 1)
    same = (src // 64 == dst // 8 % 4) & (src // 8 % 8 == dst // 32) & (src % 8 == dst % 8)
    rows = in_ref[...].astype(F32).reshape(256, 128).astype(BF16)
    got = dot(dot_t(pick, rows).astype(BF16), one_hot(same))
    for half in range(2):
        keep_ref[8 + half] = got[:WIDE, 128 * half : 128 * half + 128].astype(BF16)
        send_ref[8 + half] = got[WIDE:, 128 * half : 128 * half + 128].astype(BF16)


def join_kernel(keep_ref, recv_ref, near_ref, far_ref, pre_ref, hid_ref, ins_ref, wide_ref, thin_ref):
    r = lax.rem(lax.axis_index("space"), 2)
    left = r == 0
    row = iota((WIDE, 128), 0)
    edge = row == jnp.where(left, 0, STRIP + 1)
    lane = iota((PAD, 128), 1)
    tail = jnp.zeros((PAD - WIDE, 128), F32)
    own = (iota((PAD, 128), 0) >= 1) & (iota((PAD, 128), 0) <= STRIP)
    for z in range(8):
        mine = jnp.where(edge, near_ref[z].astype(F32)[:1], keep_ref[z].astype(F32))
        other = jnp.where(edge, far_ref[z].astype(F32)[:1], recv_ref[z].astype(F32))
        mine = jnp.concatenate([mine, tail], axis=0)
        other = jnp.concatenate([other, tail], axis=0)
        for part in range(2):
            value = jnp.where(left, mine, other) if part == 0 else jnp.where(left, other, mine)
            pre_ref[z, :, 128 * part : 128 * part + 128] = value.astype(BF16)
            hidden = jnp.where(value > 0, value, LEAK * value)
            wide_ref[PAD * z : PAD * z + PAD, 128 * part : 128 * part + 128] = jnp.where(own, hidden, 0.0)
        mine = jnp.concatenate([keep_ref[8 + z // 4].astype(F32), tail], axis=0)
        other = jnp.concatenate([recv_ref[8 + z // 4].astype(F32), tail], axis=0)
        low, high = jnp.where(left, mine, other), jnp.where(left, other, mine)
        low = pltpu.roll(low, (128 - 32 * (z % 4)) % 128, 1)
        high = pltpu.roll(high, (160 - 32 * (z % 4)) % 128, 1)
        value = jnp.where(lane < 32, low, jnp.where(lane < 64, high, 0.0))
        thin_ref[PAD * z : PAD * z + PAD, :] = value
    for part in range(2):
        turned = wide_ref[:, 128 * part : 128 * part + 128].T
        for kx in range(3):
            shifted = pltpu.roll(turned, 2 - kx, 1) if kx < 2 else turned
            hid_ref[256 * kx + 128 * part : 256 * kx + 128 * part + 128, :] = shifted.astype(BF16)
    turned = thin_ref[...].T[:64]
    for kx in range(3):
        shifted = pltpu.roll(turned, 2 - kx, 1) if kx < 2 else turned
        ins_ref[64 * kx : 64 * kx + 64, :] = shifted.astype(BF16)


def band_kernel(two_ref, one_ref, wide_ref, thin_ref):
    spread = one_hot(iota((16, 256), 1) % 16 == iota((16, 256), 0))
    two = dot(two_ref[...], spread)
    group = iota((32, 256), 1) // 16
    for kz in range(3):
        for kx in range(3):
            terms = [two[32 * (9 * kz + 3 * ky + kx) :][:32] for ky in range(3)]
            for y in range(16):
                block = jnp.zeros((32, 256), F32)
                for ky in range(3):
                    block = jnp.where(group == y + ky - 1, terms[ky], block)
                wide_ref[512 * kz + 32 * y : 512 * kz + 32 * y + 32, 256 * kx : 256 * kx + 256] = block.astype(BF16)
    lane = iota((4, 128), 1)
    spread = one_hot((lane < 64) & (lane // 8 % 4 == iota((4, 128), 0)))
    one = dot(one_ref[...], spread)
    lane = iota((16, 128), 1)
    group = 8 * (lane // 32) + lane % 8
    for kz in range(3):
        for kx in range(3):
            terms = [one[16 * (9 * kz + 3 * ky + kx) :][:16] for ky in range(3)]
            for y in range(16):
                block = jnp.zeros((16, 128), F32)
                for ky in range(3):
                    block = jnp.where(group == y + ky - 1, terms[ky], block)
                thin_ref[256 * kz + 16 * y : 256 * kz + 16 * y + 16, 128 * kx : 128 * kx + 128] = block.astype(BF16)


def planes(ref, kz):
    return ref[(2 - kz) * PAD : (2 - kz) * PAD + ROWS, :]


def grads_kernel(
    grad_ref, pre_ref, hid_ref, ins_ref, wide_ref, thin_ref,
    own_ref, give_ref, mine_ref, rest_ref, grad_s, act_s, out_s, terms_s,
):
    space = lax.axis_index("space")
    left = lax.rem(space, 2) == 0
    for block in (0, 9):
        grad_s[PAD * block : PAD * block + PAD, :] = jnp.zeros((PAD, 512), BF16)
        act_s[PAD * block : PAD * block + PAD, :] = jnp.zeros((PAD, 256), BF16)
    for z in range(8):
        plane = jnp.concatenate([grad_ref[z].astype(F32), jnp.zeros((PAD - WIDE, 512), F32)], axis=0)
        grad_s[PAD * (z + 1) : PAD * (z + 2), :] = plane.astype(BF16)

    lane = iota((16, 128), 1)
    taps = [None] * 28
    for kz in range(3):
        terms_s[...] = dot(hid_ref[...], planes(grad_s, kz))
        for kx in range(3):
            for ky in range(3):
                total = jnp.zeros((16, 128), F32)
                for y in range(16):
                    at = y + ky - 1
                    if 0 <= at < 16:
                        piece = terms_s[256 * kx + 16 * at : 256 * kx + 16 * at + 16, 128 * (y // 4) : 128 * (y // 4) + 128]
                        total = total + jnp.where(lane // 32 == y % 4, piece, 0.0)
                total = total + pltpu.roll(total, 64, 1)
                taps[9 * kz + 3 * ky + kx] = total + pltpu.roll(total, 32, 1)

    left_side = jnp.concatenate([planes(grad_s, kz) for kz in range(3)], axis=1)
    sums = dot(left_side, wide_ref[...])
    act = sums[:, 512:] + pltpu.roll(sums[:, 256:512], ROWS - 1, 0) + pltpu.roll(sums[:, :256], ROWS - 2, 0)
    act = act.reshape(8, PAD, 256)
    at = STRIP * space - 1 + iota((8, PAD, 256), 1)
    inside = (iota((8, PAD, 256), 1) < STRIP + 2) & (at >= 0) & (at < 512)
    act = act * jnp.where(pre_ref[...].astype(F32) > 0, 1.0, LEAK)
    act_s[PAD : PAD + ROWS, :] = jnp.where(inside, act, 0.0).reshape(ROWS, 256).astype(BF16)

    left_side = jnp.concatenate([planes(act_s, kz) for kz in range(3)], axis=1)
    sums = dot(left_side, thin_ref[...])
    out_s[...] = sums[:, 256:] + pltpu.roll(sums[:, 128:256], ROWS - 1, 0) + pltpu.roll(sums[:, :128], ROWS - 2, 0)
    for z in range(4):
        pair = jnp.concatenate([out_s[PAD * z : PAD * z + STRIP], out_s[PAD * (z + 4) : PAD * (z + 4) + STRIP]], axis=0).T
        own_ref[z] = jnp.where(left, pair[:32], pair[32:64]).astype(BF16)
        give_ref[z] = jnp.where(left, pair[32:64], pair[:32]).astype(BF16)

    row, col = iota((64, 256), 0), iota((64, 256), 1)
    gap = 8 * (row // 32) + row % 8 - col // 16
    packed = jnp.zeros((12, 128), F32)
    for kz in range(3):
        terms = dot(ins_ref[...], planes(act_s, kz)).reshape(3, 64, 256)
        for ky in range(3):
            part = jnp.where((gap == ky - 1)[None], terms, 0.0)
            part = (part[:, :, :128] + part[:, :, 128:]).reshape(3, 2, 4, 8, 128)
            part = jnp.sum(part[:, 0] + part[:, 1], axis=2).reshape(12, 128)
            for by in (64, 32, 16):
                part = part + pltpu.roll(part, by, 1)
            if 3 * kz + ky < 8:
                packed = jnp.where(iota((12, 128), 1) // 16 == 3 * kz + ky, part, packed)
            else:
                last = part
    filler = jnp.zeros((4, 128), F32)
    taps[27] = jnp.concatenate([last, filler], axis=0)
    blocks = []
    for q in range(7):
        block = taps[4 * q]
        for g in range(1, 4):
            block = jnp.where(lane // 32 == g, taps[4 * q + g], block)
        blocks.append(block)
    blocks.append(jnp.concatenate([packed, filler], axis=0))
    first = lax.rem(lax.axis_index("dp"), 2) == 0
    cells = 16 * 8 * 16 * 512
    scale = cells**-0.5
    for q in range(4):
        low, high = blocks[q] * scale, blocks[q + 4] * scale
        mine_ref[16 * q : 16 * q + 16, :] = jnp.where(first, low, high)
        rest_ref[16 * q : 16 * q + 16, :] = jnp.where(first, high, low)


def tile_kernel(own_ref, recv_ref, out_ref):
    left = lax.rem(lax.axis_index("space"), 2) == 0
    low_lanes = iota((32, 128), 1) < STRIP
    for z in range(4):
        own, recv = own_ref[z].astype(F32), recv_ref[z].astype(F32)
        a, b = jnp.where(left, own, recv), jnp.where(left, recv, own)
        near = jnp.where(low_lanes, a, pltpu.roll(b, STRIP, 1))
        far = jnp.where(low_lanes, pltpu.roll(a, STRIP, 1), b)
        out_ref[:, z] = near.reshape(4, 8, 128).astype(BF16)
        out_ref[:, z + 4] = far.reshape(4, 8, 128).astype(BF16)


def unpack_kernel(mine_ref, rest_ref, one_ref, two_ref):
    first = lax.rem(lax.axis_index("dp"), 2) == 0
    mine, rest = mine_ref[...], rest_ref[...]
    low, high = jnp.where(first, mine, rest), jnp.where(first, rest, mine)
    blocks = [low[16 * q : 16 * q + 16] for q in range(4)] + [high[16 * q : 16 * q + 16] for q in range(4)]
    for k in range(27):
        two_ref[k] = blocks[k // 4][:, 32 * (k % 4) : 32 * (k % 4) + 32]
    for pair in range(9):
        for kx in range(3):
            source, lane = (blocks[7], 16 * pair) if pair < 8 else (blocks[6], 96)
            one_ref[3 * pair + kx] = source[4 * kx : 4 * kx + 4, lane : lane + 16]


def routes():
    def number(zh, x, core, y, zl):
        return ((zh * 4 + x) * 2 + core) * 8 + y * 2 + zl

    every = list(itertools.product(range(2), range(4), range(2), range(4), range(2)))
    cores = [(number(*d), number(d[0], d[1], 1 - d[2], d[3], d[4])) for d in every]
    along_x = [[(number(*d), number(d[0], (d[1] + j) % 4, *d[2:])) for d in every] for j in (1, 3, 2)]
    along_y = [[(number(*d), number(*d[:3], (d[3] + j) % 4, d[4])) for d in every] for j in (1, 3, 2)]
    along_z = []
    for j in (1, 3, 2):
        pairs = []
        for d in every:
            z = (2 * d[0] + d[4] + j) % 4
            pairs.append((number(*d), number(z // 2, d[1], d[2], d[3], z % 2)))
        along_z.append(pairs)
    return cores, [along_x, along_y, along_z]


def body(inputs, pre_act, out_grad, conv1_weight, conv2_weight):
    shape = jax.ShapeDtypeStruct
    cores, stages = routes()
    strips = call(
        cut_kernel, "cut", shape((8, WIDE, 512), BF16),
        [pltpu.VMEM((4, 512, 128), F32), pltpu.VMEM((512, 512), BF16)], [out_grad[0, 0]], 3e8, 1.2e6,
    )
    strips = lax.all_to_all(strips, "space", 0, 0, tiled=True)
    keep, send, edges = call(
        turn_kernel, "turn",
        [shape((10, WIDE, 128), BF16), shape((10, WIDE, 128), BF16), shape((2, 8, 8, 128), BF16)],
        [], [pre_act[0, 0], inputs[0, 0]], 1e8, 1e6,
    )
    swap = [(i, i ^ 1) for i in range(8)]
    recv = lax.ppermute(send, "space", swap)
    near = [(i, i + 2) for i in (0, 2, 4)] + [(i, i - 2) for i in (3, 5, 7)]
    far = [(i, i + 1) for i in (1, 3, 5)] + [(i, i - 1) for i in (2, 4, 6)]
    near = lax.ppermute(edges[0], "space", near)
    far = lax.ppermute(edges[1], "space", far)
    pre, hid, ins = call(
        join_kernel, "join",
        [shape((8, PAD, 256), BF16), shape((768, ROWS), BF16), shape((192, ROWS), BF16)],
        [pltpu.VMEM((ROWS, 256), F32), pltpu.VMEM((ROWS, 128), F32)], [keep, recv, near, far], 1e7, 2e6,
    )
    wide, thin = call(
        band_kernel, "band", [shape((1536, 768), BF16), shape((768, 384), BF16)], [],
        [conv2_weight.transpose(0, 2, 1).reshape(864, 16), conv1_weight.transpose(0, 2, 1).reshape(432, 4)], 1e7, 3e6,
    )
    own, give, mine, rest = call(
        grads_kernel, "grads",
        [shape((4, 32, 128), BF16), shape((4, 32, 128), BF16), shape((64, 128), F32), shape((64, 128), F32)],
        [
            pltpu.VMEM((10 * PAD, 512), BF16), pltpu.VMEM((10 * PAD, 256), BF16),
            pltpu.VMEM((ROWS, 128), F32), pltpu.VMEM((768, 512), F32),
        ],
        [strips, pre, hid, ins, wide, thin], 3e9, 4e6,
    )
    total = mine + lax.ppermute(rest, ALL, cores)
    got = lax.ppermute(give, "space", swap)
    for stage in stages:
        parts = [lax.ppermute(total, ALL, pairs) for pairs in stage]
        total = (total + parts[2]) + (parts[0] + parts[1])
    other = lax.ppermute(total, ALL, cores)
    input_grad = call(tile_kernel, "tile", shape((4, 8, 8, 128), BF16), [], [own, got], 1e6, 2e5)
    first, second = call(
        unpack_kernel, "unpack", [shape((27, 4, 16), F32), shape((27, 16, 32), F32)], [], [total, other], 1e6, 2e5
    )
    return input_grad[None, None], first, second


def solution(mesh):
    placed = (
        P("dp", "space", None, None, None, None),
        P("dp", "space", None, None, None, None),
        P("dp", "space", None, None, None),
        P(),
        P(),
    )
    return jax.shard_map(
        body,
        mesh=mesh,
        in_specs=placed,
        out_specs=(P("dp", "space", None, None, None, None), P(), P()),
        check_vma=False,
    )
```

```python
import itertools

import jax
import jax.numpy as jnp
from jax import lax
from jax.experimental import pallas as pl
from jax.experimental.pallas import tpu as pltpu
from jax.sharding import PartitionSpec as P

LEAK = 0.3
STRIP = 64
WIDE = 72
PAD = 80
ROWS = 8 * PAD
ALL = ("dp", "space")
F32 = jnp.float32
BF16 = jnp.bfloat16


def iota(shape, dim):
    return lax.broadcasted_iota(jnp.int32, shape, dim)


def one_hot(flags):
    return jnp.where(flags, 1.0, 0.0).astype(BF16)


def dot(a, b):
    return jnp.dot(a, b, preferred_element_type=F32)


def dot_t(a, b):
    return lax.dot_general(a, b, (((1,), (1,)), ((), ())), preferred_element_type=F32)


def call(kernel, name, outs, scratch, args, flops=1e8, size=4e6, space=pltpu.VMEM, limit=10):
    return pl.pallas_call(
        kernel,
        name=name,
        out_shape=outs,
        in_specs=[pl.BlockSpec(memory_space=space)] * len(args),
        out_specs=jax.tree.map(lambda _: pl.BlockSpec(memory_space=pltpu.VMEM), outs),
        scratch_shapes=scratch,
        compiler_params=pltpu.CompilerParams(vmem_limit_bytes=limit << 20),
        cost_estimate=pl.CostEstimate(flops=int(flops), bytes_accessed=int(size), transcendentals=0),
    )(*args)


def plane_rows(ref, z):
    return ref[:, z].astype(F32).reshape(128, 128).astype(BF16)


def row_major():
    src, dst = iota((128, 128), 0), iota((128, 128), 1)
    return one_hot((src // 8 == dst % 16) & (src % 8 == dst // 16))


def cut_kernel(slab_hbm, pre_hbm, out_ref, slab_ref, pre_ref, wide_ref, turned_ref, sems):
    copies = [
        pltpu.make_async_copy(slab_hbm.at[:, :, pl.ds(128 * b, 128)], slab_ref.at[b], sems.at[b]) for b in range(4)
    ]
    copies.append(pltpu.make_async_copy(pre_hbm, pre_ref, sems.at[4]))
    for copy in copies:
        copy.start()
    p, x = iota((WIDE, 512), 0), iota((WIDE, 512), 1)
    gap = jnp.where(p < STRIP + 4, x - p, -9999)
    pick = jnp.concatenate([jnp.where(gap == STRIP * t - 2, 1.0, 0.0) for t in range(8)], axis=0).astype(BF16)
    for b in range(4):
        copies[b].wait()
        wide_ref[b] = slab_ref[b].astype(F32).reshape(512, 128)
        for y in range(16):
            turned_ref[32 * y : 32 * y + 32, 128 * b : 128 * b + 128] = wide_ref[
                b, pl.ds(y, 32, stride=16), :
            ].astype(BF16)
    copies[4].wait()
    row, lane = iota((16, 1024), 0), iota((16, 1024), 1)
    ends = one_hot((lane // 128 == row % 8) & (lane % 128 == jnp.where(row < 8, 127, 0)))
    edges = dot_t(ends, jnp.concatenate([plane_rows(pre_ref, z) for z in range(8)], axis=1))
    edges = dot(edges.astype(BF16), row_major())
    cut = dot_t(pick, turned_ref[...])
    late = iota((8, 128), 0) >= 4
    for t in range(8):
        out_ref[t, :STRIP] = cut[WIDE * t : WIDE * t + STRIP].astype(BF16)
        last = cut[WIDE * t + STRIP : WIDE * t + WIDE]
        edge = edges[:8] if t % 2 == 0 else edges[8:]
        last = jnp.concatenate(
            [
                jnp.where(late, pltpu.roll(edge, 4, 0), last[:, :128]),
                jnp.where(late, edge, last[:, 128:256]),
                last[:, 256:],
            ],
            axis=1,
        )
        out_ref[t, STRIP:] = last.astype(BF16)


def turn_kernel(pre_hbm, in_hbm, keep_ref, send_ref, pre_ref, in_ref, sems):
    copies = [
        pltpu.make_async_copy(pre_hbm, pre_ref, sems.at[0]),
        pltpu.make_async_copy(in_hbm, in_ref, sems.at[1]),
    ]
    for copy in copies:
        copy.start()
    r = lax.rem(lax.axis_index("space"), 2)
    a, x = iota((WIDE, 128), 0), iota((WIDE, 128), 1)
    gap = jnp.where(a < STRIP + 2, x - a, -9999)
    pick = jnp.concatenate(
        [jnp.where(gap == STRIP * r - 1, 1.0, 0.0), jnp.where(gap == STRIP * (1 - r) - 1, 1.0, 0.0)], axis=0
    ).astype(BF16)
    order = row_major()
    for copy in copies:
        copy.wait()
    for z in range(8):
        got = dot(dot_t(pick, plane_rows(pre_ref, z)).astype(BF16), order)
        keep_ref[z] = got[:WIDE].astype(BF16)
        send_ref[z] = got[WIDE:].astype(BF16)
    gap = jnp.where(a < STRIP, x - a, -9999)
    pick = jnp.concatenate(
        [jnp.where(gap == STRIP * r, 1.0, 0.0), jnp.where(gap == STRIP * (1 - r), 1.0, 0.0)], axis=0
    ).astype(BF16)
    src, dst = iota((256, 256), 0), iota((256, 256), 1)
    same = (src // 64 == dst // 8 % 4) & (src // 8 % 8 == dst // 32) & (src % 8 == dst % 8)
    rows = in_ref[...].astype(F32).reshape(256, 128).astype(BF16)
    got = dot(dot_t(pick, rows).astype(BF16), one_hot(same))
    for half in range(2):
        keep_ref[8 + half] = got[:WIDE, 128 * half : 128 * half + 128].astype(BF16)
        send_ref[8 + half] = got[WIDE:, 128 * half : 128 * half + 128].astype(BF16)


def join_kernel(keep_ref, recv_ref, pre_ref, hid_ref, ins_ref, wide_ref, thin_ref):
    r = lax.rem(lax.axis_index("space"), 2)
    left = r == 0
    lane = iota((PAD, 128), 1)
    tail = jnp.zeros((PAD - WIDE, 128), F32)
    own = (iota((PAD, 128), 0) >= 1) & (iota((PAD, 128), 0) <= STRIP)
    for z in range(8):
        mine = jnp.concatenate([keep_ref[z].astype(F32), tail], axis=0)
        other = jnp.concatenate([recv_ref[z].astype(F32), tail], axis=0)
        for part in range(2):
            value = jnp.where(left, mine, other) if part == 0 else jnp.where(left, other, mine)
            pre_ref[z, :, 128 * part : 128 * part + 128] = value.astype(BF16)
            hidden = jnp.where(value > 0, value, LEAK * value)
            wide_ref[PAD * z : PAD * z + PAD, 128 * part : 128 * part + 128] = jnp.where(own, hidden, 0.0)
        mine = jnp.concatenate([keep_ref[8 + z // 4].astype(F32), tail], axis=0)
        other = jnp.concatenate([recv_ref[8 + z // 4].astype(F32), tail], axis=0)
        low, high = jnp.where(left, mine, other), jnp.where(left, other, mine)
        low = pltpu.roll(low, (128 - 32 * (z % 4)) % 128, 1)
        high = pltpu.roll(high, (160 - 32 * (z % 4)) % 128, 1)
        value = jnp.where(lane < 32, low, jnp.where(lane < 64, high, 0.0))
        thin_ref[PAD * z : PAD * z + PAD, :] = value
    for part in range(2):
        turned = wide_ref[:, 128 * part : 128 * part + 128].T
        for kx in range(3):
            shifted = pltpu.roll(turned, 2 - kx, 1) if kx < 2 else turned
            for y in range(8):
                at = 48 * (8 * part + y) + 16 * kx
                hid_ref[at : at + 16, :] = shifted[16 * y : 16 * y + 16].astype(BF16)
    turned = thin_ref[...].T[:64]
    for kx in range(3):
        shifted = pltpu.roll(turned, 2 - kx, 1) if kx < 2 else turned
        ins_ref[64 * kx : 64 * kx + 64, :] = shifted.astype(BF16)


def band_kernel(two_ref, one_ref, wide_ref, thin_ref):
    spread = one_hot(iota((16, 256), 1) % 16 == iota((16, 256), 0))
    two = dot(two_ref[...], spread)
    group = iota((32, 256), 1) // 16
    for kz in range(3):
        for kx in range(3):
            terms = [two[32 * (9 * kz + 3 * ky + kx) :][:32] for ky in range(3)]
            for y in range(16):
                block = jnp.zeros((32, 256), F32)
                for ky in range(3):
                    block = jnp.where(group == y + ky - 1, terms[ky], block)
                wide_ref[512 * kz + 32 * y : 512 * kz + 32 * y + 32, 256 * kx : 256 * kx + 256] = block.astype(BF16)
    lane = iota((4, 128), 1)
    spread = one_hot((lane < 64) & (lane // 8 % 4 == iota((4, 128), 0)))
    one = dot(one_ref[...], spread)
    lane = iota((16, 128), 1)
    group = 8 * (lane // 32) + lane % 8
    for kz in range(3):
        for kx in range(3):
            terms = [one[16 * (9 * kz + 3 * ky + kx) :][:16] for ky in range(3)]
            for y in range(16):
                block = jnp.zeros((16, 128), F32)
                for ky in range(3):
                    block = jnp.where(group == y + ky - 1, terms[ky], block)
                thin_ref[256 * kz + 16 * y : 256 * kz + 16 * y + 16, 128 * kx : 128 * kx + 128] = block.astype(BF16)


def planes(ref, kz):
    return ref[(2 - kz) * PAD : (2 - kz) * PAD + ROWS, :]


def grads_kernel(
    grad_ref, pre_ref, hid_ref, ins_ref, wide_ref, thin_ref,
    own_ref, give_ref, mine_ref, rest_ref, grad_s, act_s, out_s, terms_s,
):
    space = lax.axis_index("space")
    left = lax.rem(space, 2) == 0
    for block in (0, 9):
        grad_s[PAD * block : PAD * block + PAD, :] = jnp.zeros((PAD, 512), BF16)
        act_s[PAD * block : PAD * block + PAD, :] = jnp.zeros((PAD, 256), BF16)
    for z in range(8):
        plane = jnp.concatenate([grad_ref[z].astype(F32), jnp.zeros((PAD - WIDE, 512), F32)], axis=0)
        grad_s[PAD * (z + 1) : PAD * (z + 2), :] = plane.astype(BF16)

    lane = iota((16, 128), 1)
    taps = [None] * 28
    for kz in range(3):
        for half in range(2):
            low = 7 * half
            terms_s[half] = dot(
                hid_ref[48 * low : 48 * low + 432, :],
                grad_s[(2 - kz) * PAD : (2 - kz) * PAD + ROWS, 256 * half : 256 * half + 256],
            )
        for kx in range(3):
            for ky in range(3):
                total = jnp.zeros((16, 128), F32)
                for y in range(16):
                    at = y + ky - 1
                    if 0 <= at < 16:
                        half = y // 8
                        row, col = 48 * (at - 7 * half) + 16 * kx, 128 * (y % 8 // 4)
                        piece = terms_s[half, row : row + 16, col : col + 128]
                        total = total + jnp.where(lane // 32 == y % 4, piece, 0.0)
                total = total + pltpu.roll(total, 64, 1)
                taps[9 * kz + 3 * ky + kx] = total + pltpu.roll(total, 32, 1)

    left_side = jnp.concatenate([planes(grad_s, kz) for kz in range(3)], axis=1)
    sums = dot(left_side, wide_ref[...])
    act = sums[:, 512:] + pltpu.roll(sums[:, 256:512], ROWS - 1, 0) + pltpu.roll(sums[:, :256], ROWS - 2, 0)
    row = iota((PAD, 256), 0)
    at = STRIP * space - 1 + row
    inside = (row < STRIP + 2) & (at >= 0) & (at < 512)
    edge_row = row == jnp.where(left, 0, STRIP + 1)
    side = jnp.clip(space // 2 * 2 + jnp.where(left, -2, 2), 0, 6)
    edges = [grad_ref[side + r, STRIP:, :256].astype(F32) for r in range(2)]
    for z in range(8):
        beside = [edges[r][4 + z % 4 : 5 + z % 4, 128 * (z // 4) : 128 * (z // 4) + 128] for r in range(2)]
        pre = jnp.where(edge_row, jnp.concatenate(beside, axis=1), pre_ref[z].astype(F32))
        value = act[PAD * z : PAD * z + PAD] * jnp.where(pre > 0, 1.0, LEAK)
        act_s[PAD * (z + 1) : PAD * (z + 2), :] = jnp.where(inside, value, 0.0).astype(BF16)

    left_side = jnp.concatenate([planes(act_s, kz) for kz in range(3)], axis=1)
    sums = dot(left_side, thin_ref[...])
    out_s[...] = sums[:, 256:] + pltpu.roll(sums[:, 128:256], ROWS - 1, 0) + pltpu.roll(sums[:, :128], ROWS - 2, 0)
    for z in range(4):
        pair = jnp.concatenate([out_s[PAD * z : PAD * z + STRIP], out_s[PAD * (z + 4) : PAD * (z + 4) + STRIP]], axis=0).T
        own_ref[z] = jnp.where(left, pair[:32], pair[32:64]).astype(BF16)
        give_ref[z] = jnp.where(left, pair[32:64], pair[:32]).astype(BF16)

    row, col = iota((64, 256), 0), iota((64, 256), 1)
    gap = 8 * (row // 32) + row % 8 - col // 16
    packed = jnp.zeros((12, 128), F32)
    for kz in range(3):
        terms = dot(ins_ref[...], planes(act_s, kz)).reshape(3, 64, 256)
        for ky in range(3):
            part = jnp.where((gap == ky - 1)[None], terms, 0.0)
            part = (part[:, :, :128] + part[:, :, 128:]).reshape(3, 2, 4, 8, 128)
            part = jnp.sum(part[:, 0] + part[:, 1], axis=2).reshape(12, 128)
            for by in (64, 32, 16):
                part = part + pltpu.roll(part, by, 1)
            if 3 * kz + ky < 8:
                packed = jnp.where(iota((12, 128), 1) // 16 == 3 * kz + ky, part, packed)
            else:
                last = part
    filler = jnp.zeros((4, 128), F32)
    taps[27] = jnp.concatenate([last, filler], axis=0)
    blocks = []
    for q in range(7):
        block = taps[4 * q]
        for g in range(1, 4):
            block = jnp.where(lane // 32 == g, taps[4 * q + g], block)
        blocks.append(block)
    blocks.append(jnp.concatenate([packed, filler], axis=0))
    first = lax.rem(lax.axis_index("dp"), 2) == 0
    cells = 16 * 8 * 16 * 512
    scale = cells**-0.5
    for q in range(4):
        low, high = blocks[q] * scale, blocks[q + 4] * scale
        mine_ref[16 * q : 16 * q + 16, :] = jnp.where(first, low, high)
        rest_ref[16 * q : 16 * q + 16, :] = jnp.where(first, high, low)


def tile_kernel(own_ref, recv_ref, out_ref):
    left = lax.rem(lax.axis_index("space"), 2) == 0
    low_lanes = iota((32, 128), 1) < STRIP
    for z in range(4):
        own, recv = own_ref[z].astype(F32), recv_ref[z].astype(F32)
        a, b = jnp.where(left, own, recv), jnp.where(left, recv, own)
        near = jnp.where(low_lanes, a, pltpu.roll(b, STRIP, 1))
        far = jnp.where(low_lanes, pltpu.roll(a, STRIP, 1), b)
        out_ref[:, z] = near.reshape(4, 8, 128).astype(BF16)
        out_ref[:, z + 4] = far.reshape(4, 8, 128).astype(BF16)


def unpack_kernel(mine_ref, rest_ref, one_ref, two_ref, flat_ref):
    first = lax.rem(lax.axis_index("dp"), 2) == 0
    mine, rest = mine_ref[...], rest_ref[...]
    low, high = jnp.where(first, mine, rest), jnp.where(first, rest, mine)
    blocks = [low[16 * q : 16 * q + 16] for q in range(4)] + [high[16 * q : 16 * q + 16] for q in range(4)]
    for pair in range(9):
        source, lane = (blocks[7], 16 * pair) if pair < 8 else (blocks[6], 96)
        source = pltpu.roll(source, 128 - lane, 1) if lane else source
        for kx in range(3):
            flat_ref[pl.ds(3 * pair + kx, 4, stride=32), :] = source[4 * kx : 4 * kx + 4]
    for k in range(27):
        two_ref[k] = blocks[k // 4][:, 32 * (k % 4) : 32 * (k % 4) + 32]
    turned = flat_ref[...].T
    for c in range(4):
        one_ref[c] = turned[:16, 32 * c : 32 * c + 27]


def routes():
    def number(zh, x, core, y, zl):
        return ((zh * 4 + x) * 2 + core) * 8 + y * 2 + zl

    every = list(itertools.product(range(2), range(4), range(2), range(4), range(2)))
    cores = [(number(*d), number(d[0], d[1], 1 - d[2], d[3], d[4])) for d in every]
    along_x = [[(number(*d), number(d[0], d[1] ^ j, *d[2:])) for d in every] for j in (1, 3, 2)]
    along_y = [[(number(*d), number(*d[:3], d[3] ^ j, d[4])) for d in every] for j in (1, 3, 2)]
    along_z = []
    for j in (1, 3, 2):
        pairs = []
        for d in every:
            z = (2 * d[0] + d[4]) ^ j
            pairs.append((number(*d), number(z // 2, d[1], d[2], d[3], z % 2)))
        along_z.append(pairs)
    return cores, [along_x, along_y, along_z]


def body(inputs, pre_act, out_grad, conv1_weight, conv2_weight):
    shape = jax.ShapeDtypeStruct
    cores, stages = routes()
    strips = call(
        cut_kernel, "cut", shape((8, WIDE, 512), BF16),
        [
            pltpu.VMEM((4, 32, 16, 128), BF16), pltpu.VMEM((16, 8, 8, 128), BF16), pltpu.VMEM((4, 512, 128), F32),
            pltpu.VMEM((512, 512), BF16), pltpu.SemaphoreType.DMA((5,)),
        ],
        [out_grad[0, 0], pre_act[0, 0]], 3e8, 1.2e6, pl.ANY,
    )
    strips = lax.all_to_all(strips, "space", 0, 0, tiled=True)
    keep, send = call(
        turn_kernel, "turn", [shape((10, WIDE, 128), BF16), shape((10, WIDE, 128), BF16)],
        [pltpu.VMEM((16, 8, 8, 128), BF16), pltpu.VMEM((4, 8, 8, 128), BF16), pltpu.SemaphoreType.DMA((2,))],
        [pre_act[0, 0], inputs[0, 0]], 1e8, 1e6, pl.ANY,
    )
    swap = [(i, i ^ 1) for i in range(8)]
    recv = lax.ppermute(send, "space", swap)
    pre, hid, ins = call(
        join_kernel, "join",
        [shape((8, PAD, 256), BF16), shape((768, ROWS), BF16), shape((192, ROWS), BF16)],
        [pltpu.VMEM((ROWS, 256), F32), pltpu.VMEM((ROWS, 128), F32)], [keep, recv], 1e7, 2e6,
    )
    wide, thin = call(
        band_kernel, "band", [shape((1536, 768), BF16), shape((768, 384), BF16)], [],
        [conv2_weight.transpose(0, 2, 1).reshape(864, 16), conv1_weight.transpose(0, 2, 1).reshape(432, 4)], 1e7, 3e6,
    )
    own, give, mine, rest = call(
        grads_kernel, "grads",
        [shape((4, 32, 128), BF16), shape((4, 32, 128), BF16), shape((64, 128), F32), shape((64, 128), F32)],
        [
            pltpu.VMEM((10 * PAD, 512), BF16), pltpu.VMEM((10 * PAD, 256), BF16),
            pltpu.VMEM((ROWS, 128), F32), pltpu.VMEM((2, 432, 256), F32),
        ],
        [strips, pre, hid, ins, wide, thin], 3e9, 4e6, limit=20,
    )
    total = mine + lax.ppermute(rest, ALL, cores)
    got = lax.ppermute(give, "space", swap)
    for stage in stages:
        parts = [lax.ppermute(total, ALL, pairs) for pairs in stage]
        total = (total + parts[0]) + (parts[1] + parts[2])
    other = lax.ppermute(total, ALL, cores)
    input_grad = call(tile_kernel, "tile", shape((4, 8, 8, 128), BF16), [], [own, got], 1e6, 2e5)
    first, second = call(
        unpack_kernel, "unpack", [shape((4, 16, 27), F32), shape((27, 16, 32), F32)], [pltpu.VMEM((128, 128), F32)],
        [total, other], 1e6, 2e5,
    )
    return input_grad[None, None], first.transpose(2, 0, 1), second


def solution(mesh):
    placed = (
        P("dp", "space", None, None, None, None),
        P("dp", "space", None, None, None, None),
        P("dp", "space", None, None, None),
        P(),
        P(),
    )
    return jax.shard_map(
        body,
        mesh=mesh,
        in_specs=placed,
        out_specs=(P("dp", "space", None, None, None, None), P(), P()),
        check_vma=False,
    )
```

```python
import itertools

import jax
import jax.numpy as jnp
from jax import lax
from jax.experimental import pallas as pl
from jax.experimental.pallas import tpu as pltpu
from jax.sharding import PartitionSpec as P

LEAK = 0.3
STRIP = 64
WIDE = 72
PAD = 80
ROWS = 8 * PAD
FULL = 62
ALL = ("dp", "space")
F32 = jnp.float32
BF16 = jnp.bfloat16


def iota(shape, dim):
    return lax.broadcasted_iota(jnp.int32, shape, dim)


def one_hot(flags):
    return jnp.where(flags, 1.0, 0.0).astype(BF16)


def dot(a, b):
    return jnp.dot(a, b, preferred_element_type=F32)


def dot_t(a, b):
    return lax.dot_general(a, b, (((1,), (1,)), ((), ())), preferred_element_type=F32)


def call(kernel, name, outs, scratch, args, flops, size, limit=10, far_args=()):
    def spec(far):
        return pl.BlockSpec(memory_space=pltpu.HBM if far else pltpu.VMEM)

    return pl.pallas_call(
        kernel,
        name=name,
        out_shape=outs,
        in_specs=[spec(i in far_args) for i in range(len(args))],
        out_specs=[spec(False)] * len(outs),
        scratch_shapes=scratch,
        compiler_params=pltpu.CompilerParams(vmem_limit_bytes=limit << 20),
        cost_estimate=pl.CostEstimate(flops=int(flops), bytes_accessed=int(size), transcendentals=0),
    )(*args)


def plane_rows(ref, z):
    return ref[:, z].astype(F32).reshape(128, 128).astype(BF16)


def row_major():
    src, dst = iota((128, 128), 0), iota((128, 128), 1)
    return one_hot((src // 8 == dst % 16) & (src % 8 == dst // 16))


def turn_kernel(pre_hbm, in_hbm, keep_ref, send_ref, edge_ref, pre_ref, in_ref, sems):
    copies = [
        pltpu.make_async_copy(in_hbm, in_ref, sems.at[0]),
        pltpu.make_async_copy(pre_hbm, pre_ref, sems.at[1]),
    ]
    for copy in copies:
        copy.start()
    r = lax.rem(lax.axis_index("space"), 2)
    a, x = iota((WIDE, 128), 0), iota((WIDE, 128), 1)
    src, dst = iota((256, 256), 0), iota((256, 256), 1)
    same = (src // 64 == dst // 8 % 4) & (src // 8 % 8 == dst // 32) & (src % 8 == dst % 8)
    same = one_hot(same)
    order = row_major()
    gap = jnp.where(a < STRIP, x - a, -9999)
    pick = jnp.concatenate(
        [jnp.where(gap == STRIP * r, 1.0, 0.0), jnp.where(gap == STRIP * (1 - r), 1.0, 0.0)], axis=0
    ).astype(BF16)
    copies[0].wait()
    rows = in_ref[...].astype(F32).reshape(256, 128).astype(BF16)
    got = dot(dot_t(pick, rows).astype(BF16), same)
    for half in range(2):
        keep_ref[8 + half] = got[:WIDE, 128 * half : 128 * half + 128].astype(BF16)
        send_ref[8 + half] = got[WIDE:, 128 * half : 128 * half + 128].astype(BF16)
    gap = jnp.where(a < STRIP + 2, x - a, -9999)
    picks = [jnp.where(gap == STRIP * r - 1, 1.0, 0.0), jnp.where(gap == STRIP * (1 - r) - 1, 1.0, 0.0)]
    end, x1 = iota((16, 128), 0), iota((16, 128), 1)
    edges = jnp.zeros((16, 128), F32)
    copies[1].wait()
    for z in range(8):
        ends = jnp.where((end % 8 == z) & (x1 == jnp.where(end < 8, 127, 0)), 1.0, 0.0)
        pick = jnp.concatenate(picks + [ends], axis=0).astype(BF16)
        got = dot(dot_t(pick, plane_rows(pre_ref, z)).astype(BF16), order)
        keep_ref[z] = got[:WIDE].astype(BF16)
        send_ref[z] = got[WIDE : 2 * WIDE].astype(BF16)
        edges = edges + got[2 * WIDE :]
    edge_ref[...] = edges


def cut_kernel(slab_hbm, edge_ref, out_ref, slab_ref, wide_ref, turned_ref, sems):
    copies = [
        pltpu.make_async_copy(slab_hbm.at[:, :, pl.ds(128 * b, 128)], slab_ref.at[b], sems.at[b]) for b in range(4)
    ]
    for copy in copies:
        copy.start()
    p, x = iota((WIDE, 512), 0), iota((WIDE, 512), 1)
    gap = jnp.where(p < STRIP + 4, x - p, -9999)
    strips = jnp.concatenate([jnp.where(gap == STRIP * t - 2, 1.0, 0.0) for t in range(8)], axis=0).astype(BF16)
    for b in range(4):
        copies[b].wait()
        wide_ref[b] = slab_ref[b].astype(F32).reshape(512, 128)
        for y in range(16):
            turned_ref[32 * y : 32 * y + 32, 128 * b : 128 * b + 128] = wide_ref[
                b, pl.ds(y, 32, stride=16), :
            ].astype(BF16)
    cut = dot_t(strips, turned_ref[...])
    late = iota((8, 128), 0) >= 4
    for t in range(8):
        out_ref[t, :STRIP] = cut[WIDE * t : WIDE * t + STRIP].astype(BF16)
        last = cut[WIDE * t + STRIP : WIDE * t + WIDE]
        edge = edge_ref[:8] if t % 2 == 0 else edge_ref[8:]
        last = jnp.concatenate(
            [
                jnp.where(late, pltpu.roll(edge, 4, 0), last[:, :128]),
                jnp.where(late, edge, last[:, 128:256]),
                last[:, 256:],
            ],
            axis=1,
        )
        out_ref[t, STRIP:] = last.astype(BF16)


def join(keep_ref, recv_ref, pre_ref, hid_ref, ins_ref, wide_ref, thin_ref):
    r = lax.rem(lax.axis_index("space"), 2)
    left = r == 0
    lane = iota((PAD, 128), 1)
    tail = jnp.zeros((PAD - WIDE, 128), F32)
    own = (iota((PAD, 128), 0) >= 1) & (iota((PAD, 128), 0) <= STRIP)
    for z in range(8):
        mine = jnp.concatenate([keep_ref[z].astype(F32), tail], axis=0)
        other = jnp.concatenate([recv_ref[z].astype(F32), tail], axis=0)
        for part in range(2):
            value = jnp.where(left, mine, other) if part == 0 else jnp.where(left, other, mine)
            pre_ref[z, :, 128 * part : 128 * part + 128] = value.astype(BF16)
            hidden = jnp.where(value > 0, value, LEAK * value)
            wide_ref[PAD * z : PAD * z + PAD, 128 * part : 128 * part + 128] = jnp.where(own, hidden, 0.0)
        mine = jnp.concatenate([keep_ref[8 + z // 4].astype(F32), tail], axis=0)
        other = jnp.concatenate([recv_ref[8 + z // 4].astype(F32), tail], axis=0)
        low, high = jnp.where(left, mine, other), jnp.where(left, other, mine)
        low = pltpu.roll(low, (128 - 32 * (z % 4)) % 128, 1)
        high = pltpu.roll(high, (160 - 32 * (z % 4)) % 128, 1)
        value = jnp.where(lane < 32, low, jnp.where(lane < 64, high, 0.0))
        thin_ref[PAD * z : PAD * z + PAD, :] = value
    for part in range(2):
        turned = wide_ref[:, 128 * part : 128 * part + 128].T
        for kx in range(3):
            shifted = pltpu.roll(turned, 2 - kx, 1) if kx < 2 else turned
            for y in range(8):
                at = 48 * (8 * part + y) + 16 * kx
                hid_ref[at : at + 16, :] = shifted[16 * y : 16 * y + 16].astype(BF16)
    turned = thin_ref[...].T[:64]
    for kx in range(3):
        shifted = pltpu.roll(turned, 2 - kx, 1) if kx < 2 else turned
        ins_ref[64 * kx : 64 * kx + 64, :] = shifted.astype(BF16)


def band(two_ref, one_ref, wide_refs, thin_ref):
    spread = one_hot(iota((16, 256), 1) % 16 == iota((16, 256), 0))
    two = dot(two_ref[...], spread)
    group = iota((32, 256), 1) // 16
    for kz in range(3):
        for kx in range(3):
            terms = [two[32 * (9 * kz + 3 * ky + kx) :][:32] for ky in range(3)]
            for y in range(16):
                block = jnp.zeros((32, 256), F32)
                for ky in range(3):
                    block = jnp.where(group == y + ky - 1, terms[ky], block)
                wide_refs[kz][32 * y : 32 * y + 32, 256 * kx : 256 * kx + 256] = block.astype(BF16)
    lane = iota((4, 128), 1)
    spread = one_hot((lane < 64) & (lane // 8 % 4 == iota((4, 128), 0)))
    one = dot(one_ref[...], spread)
    lane = iota((16, 128), 1)
    group = 8 * (lane // 32) + lane % 8
    for kz in range(3):
        for kx in range(3):
            terms = [one[16 * (9 * kz + 3 * ky + kx) :][:16] for ky in range(3)]
            for y in range(16):
                block = jnp.zeros((16, 128), F32)
                for ky in range(3):
                    block = jnp.where(group == y + ky - 1, terms[ky], block)
                thin_ref[256 * kz + 16 * y : 256 * kz + 16 * y + 16, 128 * kx : 128 * kx + 128] = block.astype(BF16)


def ready_kernel(
    keep_ref, recv_ref, two_ref, one_ref,
    pre_ref, hid_ref, ins_ref, wide0_ref, wide1_ref, wide2_ref, thin_ref, hidden_ref, inputs_ref,
):
    band(two_ref, one_ref, (wide0_ref, wide1_ref, wide2_ref), thin_ref)
    join(keep_ref, recv_ref, pre_ref, hid_ref, ins_ref, hidden_ref, inputs_ref)


def planes(ref, kz):
    return ref[(2 - kz) * PAD : (2 - kz) * PAD + ROWS, :]


def grads_kernel(
    grad_hbm, pre_hbm, hid_hbm, ins_hbm, wide0_hbm, wide1_hbm, wide2_hbm, thin_hbm,
    own_ref, give_ref, mine_ref, rest_ref, grad_s, act_s, out_s, terms_s,
    grad_ref, pre_ref, hid_ref, ins_ref, wide0_ref, wide1_ref, wide2_ref, thin_ref, sems,
):
    pairs = [(grad_hbm.at[z], grad_ref.at[z]) for z in range(8)]
    pairs += [(hid_hbm.at[pl.ds(192 * i, 192)], hid_ref.at[pl.ds(192 * i, 192)]) for i in range(4)]
    pairs += [(wide0_hbm, wide0_ref), (wide1_hbm, wide1_ref), (wide2_hbm, wide2_ref)]
    pairs += [(pre_hbm, pre_ref), (thin_hbm, thin_ref), (ins_hbm, ins_ref)]
    copies = [pltpu.make_async_copy(source, target, sems.at[i]) for i, (source, target) in enumerate(pairs)]
    for copy in copies:
        copy.start()
    space = lax.axis_index("space")
    left = lax.rem(space, 2) == 0
    for block in (0, 9):
        grad_s[PAD * block : PAD * block + PAD, :] = jnp.zeros((PAD, 512), BF16)
        act_s[PAD * block : PAD * block + PAD, :] = jnp.zeros((PAD, 256), BF16)
    for z in range(8):
        copies[z].wait()
        plane = jnp.concatenate([grad_ref[z].astype(F32), jnp.zeros((PAD - WIDE, 512), F32)], axis=0)
        grad_s[PAD * (z + 1) : PAD * (z + 2), :] = plane.astype(BF16)

    for copy in copies[8:12]:
        copy.wait()
    lane = iota((16, 128), 1)
    taps = [None] * 28
    for kz in range(3):
        for half in range(2):
            low = 7 * half
            terms_s[half] = dot(
                hid_ref[48 * low : 48 * low + 432, :],
                grad_s[(2 - kz) * PAD : (2 - kz) * PAD + ROWS, 256 * half : 256 * half + 256],
            )
        for kx in range(3):
            for ky in range(3):
                total = jnp.zeros((16, 128), F32)
                for y in range(16):
                    at = y + ky - 1
                    if 0 <= at < 16:
                        half = y // 8
                        row, col = 48 * (at - 7 * half) + 16 * kx, 128 * (y % 8 // 4)
                        piece = terms_s[half, row : row + 16, col : col + 128]
                        total = total + jnp.where(lane // 32 == y % 4, piece, 0.0)
                total = total + pltpu.roll(total, 64, 1)
                taps[9 * kz + 3 * ky + kx] = total + pltpu.roll(total, 32, 1)

    for copy in copies[12:]:
        copy.wait()
    sums = dot(planes(grad_s, 0), wide0_ref[...])
    sums = sums + dot(planes(grad_s, 1), wide1_ref[...])
    sums = sums + dot(planes(grad_s, 2), wide2_ref[...])
    act = sums[:, 512:] + pltpu.roll(sums[:, 256:512], ROWS - 1, 0) + pltpu.roll(sums[:, :256], ROWS - 2, 0)
    row = iota((PAD, 256), 0)
    at = STRIP * space - 1 + row
    inside = (row < STRIP + 2) & (at >= 0) & (at < 512)
    edge_row = row == jnp.where(left, 0, STRIP + 1)
    side = jnp.clip(space // 2 * 2 + jnp.where(left, -2, 2), 0, 6)
    edges = [grad_ref[side + r, STRIP:, :256].astype(F32) for r in range(2)]
    for z in range(8):
        beside = [edges[r][4 + z % 4 : 5 + z % 4, 128 * (z // 4) : 128 * (z // 4) + 128] for r in range(2)]
        pre = jnp.where(edge_row, jnp.concatenate(beside, axis=1), pre_ref[z].astype(F32))
        value = act[PAD * z : PAD * z + PAD] * jnp.where(pre > 0, 1.0, LEAK)
        act_s[PAD * (z + 1) : PAD * (z + 2), :] = jnp.where(inside, value, 0.0).astype(BF16)

    left_side = jnp.concatenate([planes(act_s, kz) for kz in range(3)], axis=1)
    sums = dot(left_side, thin_ref[...])
    out_s[...] = sums[:, 256:] + pltpu.roll(sums[:, 128:256], ROWS - 1, 0) + pltpu.roll(sums[:, :128], ROWS - 2, 0)
    for z in range(4):
        pair = jnp.concatenate([out_s[PAD * z : PAD * z + STRIP], out_s[PAD * (z + 4) : PAD * (z + 4) + STRIP]], axis=0).T
        own_ref[z] = jnp.where(left, pair[:32], pair[32:64]).astype(BF16)
        give_ref[z] = jnp.where(left, pair[32:64], pair[:32]).astype(BF16)

    row, col = iota((64, 256), 0), iota((64, 256), 1)
    gap = 8 * (row // 32) + row % 8 - col // 16
    packed = jnp.zeros((12, 128), F32)
    for kz in range(3):
        terms = dot(ins_ref[...], planes(act_s, kz)).reshape(3, 64, 256)
        for ky in range(3):
            part = jnp.where((gap == ky - 1)[None], terms, 0.0)
            part = (part[:, :, :128] + part[:, :, 128:]).reshape(3, 2, 4, 8, 128)
            part = jnp.sum(part[:, 0] + part[:, 1], axis=2).reshape(12, 128)
            for by in (64, 32, 16):
                part = part + pltpu.roll(part, by, 1)
            if 3 * kz + ky < 8:
                packed = jnp.where(iota((12, 128), 1) // 16 == 3 * kz + ky, part, packed)
            else:
                last = part
    filler = jnp.zeros((4, 128), F32)
    taps[27] = jnp.concatenate([last, filler], axis=0)
    blocks = []
    for q in range(7):
        block = taps[4 * q]
        for g in range(1, 4):
            block = jnp.where(lane // 32 == g, taps[4 * q + g], block)
        blocks.append(block)
    blocks.append(jnp.concatenate([packed, filler], axis=0))
    first = lax.rem(lax.axis_index("dp"), 2) == 0
    cells = 16 * 8 * 16 * 512
    scale = cells**-0.5
    for q in range(4):
        low, high = blocks[q] * scale, blocks[q + 4] * scale
        mine_ref[16 * q : 16 * q + 16, :] = jnp.where(first, low, high)
        rest_ref[16 * q : 16 * q + 16, :] = jnp.where(first, high, low)


def tile_kernel(own_ref, recv_ref, out_ref):
    left = lax.rem(lax.axis_index("space"), 2) == 0
    low_lanes = iota((32, 128), 1) < STRIP
    for z in range(4):
        own, recv = own_ref[z].astype(F32), recv_ref[z].astype(F32)
        a, b = jnp.where(left, own, recv), jnp.where(left, recv, own)
        near = jnp.where(low_lanes, a, pltpu.roll(b, STRIP, 1))
        far = jnp.where(low_lanes, pltpu.roll(a, STRIP, 1), b)
        out_ref[:, z] = near.reshape(4, 8, 128).astype(BF16)
        out_ref[:, z + 4] = far.reshape(4, 8, 128).astype(BF16)


def unpack_kernel(mine_ref, rest_ref, one_ref, two_ref, flat_ref):
    first = lax.rem(lax.axis_index("dp"), 2) == 0
    mine, rest = mine_ref[...], rest_ref[...]
    low, high = jnp.where(first, mine, rest), jnp.where(first, rest, mine)
    blocks = [low[16 * q : 16 * q + 16] for q in range(4)] + [high[16 * q : 16 * q + 16] for q in range(4)]
    for pair in range(9):
        source, lane = (blocks[7], 16 * pair) if pair < 8 else (blocks[6], 96)
        source = pltpu.roll(source, 128 - lane, 1) if lane else source
        for kx in range(3):
            flat_ref[pl.ds(3 * pair + kx, 4, stride=32), :] = source[4 * kx : 4 * kx + 4]
    for k in range(27):
        two_ref[k] = blocks[k // 4][:, 32 * (k % 4) : 32 * (k % 4) + 32]
    turned = flat_ref[...].T
    for c in range(4):
        one_ref[c] = turned[:16, 32 * c : 32 * c + 27]


def routes():
    def number(zh, x, core, y, zl):
        return ((zh * 4 + x) * 2 + core) * 8 + y * 2 + zl

    every = list(itertools.product(range(2), range(4), range(2), range(4), range(2)))
    cores = [(number(*d), number(d[0], d[1], 1 - d[2], d[3], d[4])) for d in every]
    along_x = [[(number(*d), number(d[0], d[1] ^ j, *d[2:])) for d in every] for j in (1, 3, 2)]
    along_y = [[(number(*d), number(*d[:3], d[3] ^ j, d[4])) for d in every] for j in (1, 3, 2)]
    along_z = []
    for j in (1, 3, 2):
        pairs = []
        for d in every:
            z = (2 * d[0] + d[4]) ^ j
            pairs.append((number(*d), number(z // 2, d[1], d[2], d[3], z % 2)))
        along_z.append(pairs)
    return cores, [along_x, along_y, along_z]


def body(inputs, pre_act, out_grad, conv1_weight, conv2_weight):
    shape = jax.ShapeDtypeStruct
    cores, stages = routes()
    keep, send, edges = call(
        turn_kernel, "turn", [shape((10, WIDE, 128), BF16), shape((10, WIDE, 128), BF16), shape((16, 128), F32)],
        [pltpu.VMEM((16, 8, 8, 128), BF16), pltpu.VMEM((4, 8, 8, 128), BF16), pltpu.SemaphoreType.DMA((2,))],
        [pre_act[0, 0], inputs[0, 0]], 1e8, 1e6, limit=FULL, far_args=(0, 1),
    )
    swap = [(i, i ^ 1) for i in range(8)]
    recv = lax.ppermute(send, "space", swap)
    (strips,) = call(
        cut_kernel, "cut", [shape((8, WIDE, 512), BF16)],
        [
            pltpu.VMEM((4, 32, 16, 128), BF16), pltpu.VMEM((4, 512, 128), F32),
            pltpu.VMEM((512, 512), BF16), pltpu.SemaphoreType.DMA((4,)),
        ],
        [out_grad[0, 0], edges], 4e8, 2e6, limit=FULL, far_args=(0,),
    )
    strips = lax.all_to_all(strips, "space", 0, 0, tiled=True)
    pre, hid, ins, wide0, wide1, wide2, thin = call(
        ready_kernel, "ready",
        [
            shape((8, PAD, 256), BF16), shape((768, ROWS), BF16), shape((192, ROWS), BF16),
            shape((512, 768), BF16), shape((512, 768), BF16), shape((512, 768), BF16), shape((768, 384), BF16),
        ],
        [pltpu.VMEM((ROWS, 256), F32), pltpu.VMEM((ROWS, 128), F32)],
        [
            keep, recv, conv2_weight.transpose(0, 2, 1).reshape(864, 16),
            conv1_weight.transpose(0, 2, 1).reshape(432, 4),
        ],
        1e12, 5e6, limit=FULL,
    )
    own, give, mine, rest = call(
        grads_kernel, "grads",
        [shape((4, 32, 128), BF16), shape((4, 32, 128), BF16), shape((64, 128), F32), shape((64, 128), F32)],
        [
            pltpu.VMEM((10 * PAD, 512), BF16), pltpu.VMEM((10 * PAD, 256), BF16),
            pltpu.VMEM((ROWS, 128), F32), pltpu.VMEM((2, 432, 256), F32),
            pltpu.VMEM((8, WIDE, 512), BF16), pltpu.VMEM((8, PAD, 256), BF16), pltpu.VMEM((768, ROWS), BF16),
            pltpu.VMEM((192, ROWS), BF16), pltpu.VMEM((512, 768), BF16), pltpu.VMEM((512, 768), BF16),
            pltpu.VMEM((512, 768), BF16), pltpu.VMEM((768, 384), BF16), pltpu.SemaphoreType.DMA((18,)),
        ],
        [strips, pre, hid, ins, wide0, wide1, wide2, thin], 3e9, 4e6, limit=FULL, far_args=range(8),
    )
    total = mine + lax.ppermute(rest, ALL, cores)
    got = lax.ppermute(give, "space", swap)
    for stage in stages:
        parts = [lax.ppermute(total, ALL, pairs) for pairs in stage]
        total = (total + parts[0]) + (parts[1] + parts[2])
    other = lax.ppermute(total, ALL, cores)
    (input_grad,) = call(tile_kernel, "tile", [shape((4, 8, 8, 128), BF16)], [], [own, got], 1e6, 2e5)
    first, second = call(
        unpack_kernel, "unpack", [shape((4, 16, 27), F32), shape((27, 16, 32), F32)], [pltpu.VMEM((128, 128), F32)],
        [total, other], 1e6, 2e5,
    )
    return input_grad[None, None], first.transpose(2, 0, 1), second


def solution(mesh):
    placed = (
        P("dp", "space", None, None, None, None),
        P("dp", "space", None, None, None, None),
        P("dp", "space", None, None, None),
        P(),
        P(),
    )
    return jax.shard_map(
        body,
        mesh=mesh,
        in_specs=placed,
        out_specs=(P("dp", "space", None, None, None, None), P(), P()),
        check_vma=False,
    )
```

```python
import itertools

import jax
import jax.numpy as jnp
from jax import lax
from jax.experimental import pallas as pl
from jax.experimental.pallas import tpu as pltpu
from jax.sharding import PartitionSpec as P

LEAK = 0.3
STRIP = 64
WIDE = 72
PAD = 80
ROWS = 8 * PAD
FULL = 62
ALL = ("dp", "space")
F32 = jnp.float32
BF16 = jnp.bfloat16


def iota(shape, dim):
    return lax.broadcasted_iota(jnp.int32, shape, dim)


def one_hot(flags):
    return jnp.where(flags, 1.0, 0.0).astype(BF16)


def dot(a, b):
    return jnp.dot(a, b, preferred_element_type=F32)


def dot_t(a, b):
    return lax.dot_general(a, b, (((1,), (1,)), ((), ())), preferred_element_type=F32)


def call(kernel, name, outs, scratch, args, flops, size, limit=10, far_args=(), far_outs=()):
    def spec(far):
        return pl.BlockSpec(memory_space=pltpu.HBM if far else pltpu.VMEM)

    return pl.pallas_call(
        kernel,
        name=name,
        out_shape=outs,
        in_specs=[spec(i in far_args) for i in range(len(args))],
        out_specs=[spec(i in far_outs) for i in range(len(outs))],
        scratch_shapes=scratch,
        compiler_params=pltpu.CompilerParams(vmem_limit_bytes=limit << 20),
        cost_estimate=pl.CostEstimate(flops=int(flops), bytes_accessed=int(size), transcendentals=0),
    )(*args)


def row_major():
    src, dst = iota((128, 128), 0), iota((128, 128), 1)
    return one_hot((src // 8 == dst % 16) & (src % 8 == dst // 16))


def cut_kernel(
    slab_hbm, pre_hbm, in_hbm, keep_hbm, send_hbm, out_hbm,
    slab_ref, pre_ref, in_ref, keep_ref, send_ref, out_ref, wide_ref, turned_ref, sems, done,
):
    copies = [pltpu.make_async_copy(in_hbm, in_ref, sems.at[0])]
    copies += [
        pltpu.make_async_copy(pre_hbm.at[:, pl.ds(4 * i, 4)], pre_ref.at[i], sems.at[1 + i]) for i in range(2)
    ]
    copies += [
        pltpu.make_async_copy(slab_hbm.at[:, :, pl.ds(128 * b, 128)], slab_ref.at[b], sems.at[3 + b]) for b in range(4)
    ]
    for copy in copies:
        copy.start()
    r = lax.rem(lax.axis_index("space"), 2)
    a, x = iota((WIDE, 128), 0), iota((WIDE, 128), 1)
    src, dst = iota((256, 256), 0), iota((256, 256), 1)
    same = one_hot((src // 64 == dst // 8 % 4) & (src // 8 % 8 == dst // 32) & (src % 8 == dst % 8))
    order = row_major()
    gap = jnp.where(a < STRIP, x - a, -9999)
    pick = jnp.concatenate(
        [jnp.where(gap == STRIP * r, 1.0, 0.0), jnp.where(gap == STRIP * (1 - r), 1.0, 0.0)], axis=0
    ).astype(BF16)
    copies[0].wait()
    rows = in_ref[...].astype(F32).reshape(256, 128).astype(BF16)
    got = dot(dot_t(pick, rows).astype(BF16), same)
    for half in range(2):
        keep_ref[8 + half] = got[:WIDE, 128 * half : 128 * half + 128].astype(BF16)
        send_ref[8 + half] = got[WIDE:, 128 * half : 128 * half + 128].astype(BF16)
    gap = jnp.where(a < STRIP + 2, x - a, -9999)
    picks = [jnp.where(gap == STRIP * r - 1, 1.0, 0.0), jnp.where(gap == STRIP * (1 - r) - 1, 1.0, 0.0)]
    end, x1 = iota((16, 128), 0), iota((16, 128), 1)
    edges = jnp.zeros((16, 128), F32)
    for z in range(8):
        if z % 4 == 0:
            copies[1 + z // 4].wait()
        ends = jnp.where((end % 8 == z) & (x1 == jnp.where(end < 8, 127, 0)), 1.0, 0.0)
        pick = jnp.concatenate(picks + [ends], axis=0).astype(BF16)
        rows = pre_ref[z // 4, :, z % 4].astype(F32).reshape(128, 128).astype(BF16)
        got = dot(dot_t(pick, rows).astype(BF16), order)
        keep_ref[z] = got[:WIDE].astype(BF16)
        send_ref[z] = got[WIDE : 2 * WIDE].astype(BF16)
        edges = edges + got[2 * WIDE :]
    results = [
        pltpu.make_async_copy(send_ref, send_hbm, done.at[8]), pltpu.make_async_copy(keep_ref, keep_hbm, done.at[9])
    ]
    for copy in results:
        copy.start()

    for b in range(4):
        copies[3 + b].wait()
        wide_ref[b] = slab_ref[b].astype(F32).reshape(512, 128)
        for y in range(16):
            turned_ref[32 * y : 32 * y + 32, 128 * b : 128 * b + 128] = wide_ref[
                b, pl.ds(y, 32, stride=16), :
            ].astype(BF16)
    p, x = iota((WIDE, 512), 0), iota((WIDE, 512), 1)
    gap = jnp.where(p < STRIP + 4, x - p, -9999)
    late = iota((8, 128), 0) >= 4
    for pair in range(2):
        strips = [jnp.where(gap == STRIP * t - 2, 1.0, 0.0) for t in range(4 * pair, 4 * pair + 4)]
        cut = dot_t(jnp.concatenate(strips, axis=0).astype(BF16), turned_ref[...])
        for i in range(4):
            t = 4 * pair + i
            out_ref[t, :STRIP] = cut[WIDE * i : WIDE * i + STRIP].astype(BF16)
            last = cut[WIDE * i + STRIP : WIDE * i + WIDE]
            edge = edges[:8] if t % 2 == 0 else edges[8:]
            last = jnp.concatenate(
                [
                    jnp.where(late, pltpu.roll(edge, 4, 0), last[:, :128]),
                    jnp.where(late, edge, last[:, 128:256]),
                    last[:, 256:],
                ],
                axis=1,
            )
            out_ref[t, STRIP:] = last.astype(BF16)
            results.append(pltpu.make_async_copy(out_ref.at[t], out_hbm.at[t], done.at[t]))
            results[-1].start()
    for copy in results:
        copy.wait()


def join(keep_ref, recv_ref, pre_ref, hid_ref, ins_ref, wide_ref, thin_ref):
    r = lax.rem(lax.axis_index("space"), 2)
    left = r == 0
    lane = iota((PAD, 128), 1)
    tail = jnp.zeros((PAD - WIDE, 128), F32)
    own = (iota((PAD, 128), 0) >= 1) & (iota((PAD, 128), 0) <= STRIP)
    for z in range(8):
        mine = jnp.concatenate([keep_ref[z].astype(F32), tail], axis=0)
        other = jnp.concatenate([recv_ref[z].astype(F32), tail], axis=0)
        for part in range(2):
            value = jnp.where(left, mine, other) if part == 0 else jnp.where(left, other, mine)
            pre_ref[z, :, 128 * part : 128 * part + 128] = value.astype(BF16)
            hidden = jnp.where(value > 0, value, LEAK * value)
            wide_ref[PAD * z : PAD * z + PAD, 128 * part : 128 * part + 128] = jnp.where(own, hidden, 0.0)
        mine = jnp.concatenate([keep_ref[8 + z // 4].astype(F32), tail], axis=0)
        other = jnp.concatenate([recv_ref[8 + z // 4].astype(F32), tail], axis=0)
        low, high = jnp.where(left, mine, other), jnp.where(left, other, mine)
        low = pltpu.roll(low, (128 - 32 * (z % 4)) % 128, 1)
        high = pltpu.roll(high, (160 - 32 * (z % 4)) % 128, 1)
        value = jnp.where(lane < 32, low, jnp.where(lane < 64, high, 0.0))
        thin_ref[PAD * z : PAD * z + PAD, :] = value
    for part in range(2):
        turned = wide_ref[:, 128 * part : 128 * part + 128].T
        for kx in range(3):
            shifted = pltpu.roll(turned, 2 - kx, 1) if kx < 2 else turned
            for y in range(8):
                at = 48 * (8 * part + y) + 16 * kx
                hid_ref[at : at + 16, :] = shifted[16 * y : 16 * y + 16].astype(BF16)
    turned = thin_ref[...].T[:64]
    for kx in range(3):
        shifted = pltpu.roll(turned, 2 - kx, 1) if kx < 2 else turned
        ins_ref[64 * kx : 64 * kx + 64, :] = shifted.astype(BF16)


def band(two_ref, one_ref, wide_refs, thin_ref):
    spread = one_hot(iota((16, 256), 1) % 16 == iota((16, 256), 0))
    two = dot(two_ref[...], spread)
    group = iota((32, 256), 1) // 16
    for kz in range(3):
        for kx in range(3):
            terms = [two[32 * (9 * kz + 3 * ky + kx) :][:32] for ky in range(3)]
            for y in range(16):
                block = jnp.zeros((32, 256), F32)
                for ky in range(3):
                    block = jnp.where(group == y + ky - 1, terms[ky], block)
                wide_refs[kz][32 * y : 32 * y + 32, 256 * kx : 256 * kx + 256] = block.astype(BF16)
    lane = iota((4, 128), 1)
    spread = one_hot((lane < 64) & (lane // 8 % 4 == iota((4, 128), 0)))
    one = dot(one_ref[...], spread)
    lane = iota((16, 128), 1)
    group = 8 * (lane // 32) + lane % 8
    for kz in range(3):
        for kx in range(3):
            terms = [one[16 * (9 * kz + 3 * ky + kx) :][:16] for ky in range(3)]
            for y in range(16):
                block = jnp.zeros((16, 128), F32)
                for ky in range(3):
                    block = jnp.where(group == y + ky - 1, terms[ky], block)
                thin_ref[256 * kz + 16 * y : 256 * kz + 16 * y + 16, 128 * kx : 128 * kx + 128] = block.astype(BF16)


def ready_kernel(
    keep_ref, recv_ref, two_ref, one_ref,
    pre_ref, hid_ref, ins_ref, wide0_ref, wide1_ref, wide2_ref, thin_ref, hidden_ref, inputs_ref,
):
    band(two_ref, one_ref, (wide0_ref, wide1_ref, wide2_ref), thin_ref)
    join(keep_ref, recv_ref, pre_ref, hid_ref, ins_ref, hidden_ref, inputs_ref)


def planes(ref, kz):
    return ref[(2 - kz) * PAD : (2 - kz) * PAD + ROWS, :]


def grads_kernel(
    grad_hbm, pre_hbm, hid_hbm, ins_hbm, wide0_hbm, wide1_hbm, wide2_hbm, thin_hbm,
    own_ref, give_ref, mine_ref, rest_ref, grad_s, act_s, out_s, terms_s,
    grad_ref, pre_ref, hid_ref, ins_ref, wide0_ref, wide1_ref, wide2_ref, thin_ref, sems,
):
    pairs = [(grad_hbm.at[z], grad_ref.at[z]) for z in range(8)]
    pairs += [(hid_hbm.at[pl.ds(192 * i, 192)], hid_ref.at[pl.ds(192 * i, 192)]) for i in range(4)]
    pairs += [(wide0_hbm, wide0_ref), (wide1_hbm, wide1_ref), (wide2_hbm, wide2_ref)]
    pairs += [(pre_hbm, pre_ref), (thin_hbm, thin_ref), (ins_hbm, ins_ref)]
    copies = [pltpu.make_async_copy(source, target, sems.at[i]) for i, (source, target) in enumerate(pairs)]
    for copy in copies[:12]:
        copy.start()
    space = lax.axis_index("space")
    left = lax.rem(space, 2) == 0
    for block in (0, 9):
        grad_s[PAD * block : PAD * block + PAD, :] = jnp.zeros((PAD, 512), BF16)
        act_s[PAD * block : PAD * block + PAD, :] = jnp.zeros((PAD, 256), BF16)
    for z in range(8):
        copies[z].wait()
        plane = jnp.concatenate([grad_ref[z].astype(F32), jnp.zeros((PAD - WIDE, 512), F32)], axis=0)
        grad_s[PAD * (z + 1) : PAD * (z + 2), :] = plane.astype(BF16)

    for copy in copies[8:12]:
        copy.wait()
    for copy in copies[12:]:
        copy.start()
    lane = iota((16, 128), 1)
    taps = [None] * 28
    for kz in range(3):
        for half in range(2):
            low = 7 * half
            terms_s[half] = dot(
                hid_ref[48 * low : 48 * low + 432, :],
                grad_s[(2 - kz) * PAD : (2 - kz) * PAD + ROWS, 256 * half : 256 * half + 256],
            )
        for kx in range(3):
            for ky in range(3):
                total = jnp.zeros((16, 128), F32)
                for y in range(16):
                    at = y + ky - 1
                    if 0 <= at < 16:
                        half = y // 8
                        row, col = 48 * (at - 7 * half) + 16 * kx, 128 * (y % 8 // 4)
                        piece = terms_s[half, row : row + 16, col : col + 128]
                        total = total + jnp.where(lane // 32 == y % 4, piece, 0.0)
                total = total + pltpu.roll(total, 64, 1)
                taps[9 * kz + 3 * ky + kx] = total + pltpu.roll(total, 32, 1)

    for copy in copies[12:]:
        copy.wait()
    sums = dot(planes(grad_s, 0), wide0_ref[...])
    sums = sums + dot(planes(grad_s, 1), wide1_ref[...])
    sums = sums + dot(planes(grad_s, 2), wide2_ref[...])
    act = sums[:, 512:] + pltpu.roll(sums[:, 256:512], ROWS - 1, 0) + pltpu.roll(sums[:, :256], ROWS - 2, 0)
    row = iota((PAD, 256), 0)
    at = STRIP * space - 1 + row
    inside = (row < STRIP + 2) & (at >= 0) & (at < 512)
    edge_row = row == jnp.where(left, 0, STRIP + 1)
    side = jnp.clip(space // 2 * 2 + jnp.where(left, -2, 2), 0, 6)
    edges = [grad_ref[side + r, STRIP:, :256].astype(F32) for r in range(2)]
    for z in range(8):
        beside = [edges[r][4 + z % 4 : 5 + z % 4, 128 * (z // 4) : 128 * (z // 4) + 128] for r in range(2)]
        pre = jnp.where(edge_row, jnp.concatenate(beside, axis=1), pre_ref[z].astype(F32))
        value = act[PAD * z : PAD * z + PAD] * jnp.where(pre > 0, 1.0, LEAK)
        act_s[PAD * (z + 1) : PAD * (z + 2), :] = jnp.where(inside, value, 0.0).astype(BF16)

    left_side = jnp.concatenate([planes(act_s, kz) for kz in range(3)], axis=1)
    sums = dot(left_side, thin_ref[...])
    out_s[...] = sums[:, 256:] + pltpu.roll(sums[:, 128:256], ROWS - 1, 0) + pltpu.roll(sums[:, :128], ROWS - 2, 0)
    for z in range(4):
        pair = jnp.concatenate([out_s[PAD * z : PAD * z + STRIP], out_s[PAD * (z + 4) : PAD * (z + 4) + STRIP]], axis=0).T
        own_ref[z] = jnp.where(left, pair[:32], pair[32:64]).astype(BF16)
        give_ref[z] = jnp.where(left, pair[32:64], pair[:32]).astype(BF16)

    row, col = iota((64, 256), 0), iota((64, 256), 1)
    gap = 8 * (row // 32) + row % 8 - col // 16
    packed = jnp.zeros((12, 128), F32)
    for kz in range(3):
        terms = dot(ins_ref[...], planes(act_s, kz)).reshape(3, 64, 256)
        for ky in range(3):
            part = jnp.where((gap == ky - 1)[None], terms, 0.0)
            part = (part[:, :, :128] + part[:, :, 128:]).reshape(3, 2, 4, 8, 128)
            part = jnp.sum(part[:, 0] + part[:, 1], axis=2).reshape(12, 128)
            for by in (64, 32, 16):
                part = part + pltpu.roll(part, by, 1)
            if 3 * kz + ky < 8:
                packed = jnp.where(iota((12, 128), 1) // 16 == 3 * kz + ky, part, packed)
            else:
                last = part
    filler = jnp.zeros((4, 128), F32)
    taps[27] = jnp.concatenate([last, filler], axis=0)
    blocks = []
    for q in range(7):
        block = taps[4 * q]
        for g in range(1, 4):
            block = jnp.where(lane // 32 == g, taps[4 * q + g], block)
        blocks.append(block)
    blocks.append(jnp.concatenate([packed, filler], axis=0))
    first = lax.rem(lax.axis_index("dp"), 2) == 0
    cells = 16 * 8 * 16 * 512
    scale = cells**-0.5
    for q in range(4):
        low, high = blocks[q] * scale, blocks[q + 4] * scale
        mine_ref[16 * q : 16 * q + 16, :] = jnp.where(first, low, high)
        rest_ref[16 * q : 16 * q + 16, :] = jnp.where(first, high, low)


def tile_kernel(own_ref, recv_ref, out_ref):
    left = lax.rem(lax.axis_index("space"), 2) == 0
    low_lanes = iota((32, 128), 1) < STRIP
    for z in range(4):
        own, recv = own_ref[z].astype(F32), recv_ref[z].astype(F32)
        a, b = jnp.where(left, own, recv), jnp.where(left, recv, own)
        near = jnp.where(low_lanes, a, pltpu.roll(b, STRIP, 1))
        far = jnp.where(low_lanes, pltpu.roll(a, STRIP, 1), b)
        out_ref[:, z] = near.reshape(4, 8, 128).astype(BF16)
        out_ref[:, z + 4] = far.reshape(4, 8, 128).astype(BF16)


def unpack_kernel(mine_ref, rest_ref, one_ref, two_ref, flat_ref):
    first = lax.rem(lax.axis_index("dp"), 2) == 0
    mine, rest = mine_ref[...], rest_ref[...]
    low, high = jnp.where(first, mine, rest), jnp.where(first, rest, mine)
    blocks = [low[16 * q : 16 * q + 16] for q in range(4)] + [high[16 * q : 16 * q + 16] for q in range(4)]
    for pair in range(9):
        source, lane = (blocks[7], 16 * pair) if pair < 8 else (blocks[6], 96)
        source = pltpu.roll(source, 128 - lane, 1) if lane else source
        for kx in range(3):
            flat_ref[pl.ds(3 * pair + kx, 4, stride=32), :] = source[4 * kx : 4 * kx + 4]
    for k in range(27):
        two_ref[k] = blocks[k // 4][:, 32 * (k % 4) : 32 * (k % 4) + 32]
    turned = flat_ref[...].T
    for c in range(4):
        one_ref[c] = turned[:16, 32 * c : 32 * c + 27]


def routes():
    def number(zh, x, core, y, zl):
        return ((zh * 4 + x) * 2 + core) * 8 + y * 2 + zl

    every = list(itertools.product(range(2), range(4), range(2), range(4), range(2)))
    cores = [(number(*d), number(d[0], d[1], 1 - d[2], d[3], d[4])) for d in every]
    along_x = [[(number(*d), number(d[0], d[1] ^ j, *d[2:])) for d in every] for j in (1, 3, 2)]
    along_y = [[(number(*d), number(*d[:3], d[3] ^ j, d[4])) for d in every] for j in (1, 3, 2)]
    along_z = []
    for j in (1, 3, 2):
        pairs = []
        for d in every:
            z = (2 * d[0] + d[4]) ^ j
            pairs.append((number(*d), number(z // 2, d[1], d[2], d[3], z % 2)))
        along_z.append(pairs)
    return cores, [along_x, along_y, along_z]


def body(inputs, pre_act, out_grad, conv1_weight, conv2_weight):
    shape = jax.ShapeDtypeStruct
    cores, stages = routes()
    keep, send, strips = call(
        cut_kernel, "cut",
        [shape((10, WIDE, 128), BF16), shape((10, WIDE, 128), BF16), shape((8, WIDE, 512), BF16)],
        [
            pltpu.VMEM((4, 32, 16, 128), BF16), pltpu.VMEM((2, 16, 4, 8, 128), BF16), pltpu.VMEM((4, 8, 8, 128), BF16),
            pltpu.VMEM((10, WIDE, 128), BF16), pltpu.VMEM((10, WIDE, 128), BF16), pltpu.VMEM((8, WIDE, 512), BF16),
            pltpu.VMEM((4, 512, 128), F32), pltpu.VMEM((512, 512), BF16),
            pltpu.SemaphoreType.DMA((7,)), pltpu.SemaphoreType.DMA((10,)),
        ],
        [out_grad[0, 0], pre_act[0, 0], inputs[0, 0]], 4e8, 2e6, limit=FULL, far_args=(0, 1, 2), far_outs=(0, 1, 2),
    )
    swap = [(i, i ^ 1) for i in range(8)]
    recv = lax.ppermute(send, "space", swap)
    strips = lax.all_to_all(strips, "space", 0, 0, tiled=True)
    pre, hid, ins, wide0, wide1, wide2, thin = call(
        ready_kernel, "ready",
        [
            shape((8, PAD, 256), BF16), shape((768, ROWS), BF16), shape((192, ROWS), BF16),
            shape((512, 768), BF16), shape((512, 768), BF16), shape((512, 768), BF16), shape((768, 384), BF16),
        ],
        [pltpu.VMEM((ROWS, 256), F32), pltpu.VMEM((ROWS, 128), F32)],
        [
            keep, recv, conv2_weight.transpose(0, 2, 1).reshape(864, 16),
            conv1_weight.transpose(0, 2, 1).reshape(432, 4),
        ],
        1e12, 5e6, limit=FULL,
    )
    own, give, mine, rest = call(
        grads_kernel, "grads",
        [shape((4, 32, 128), BF16), shape((4, 32, 128), BF16), shape((64, 128), F32), shape((64, 128), F32)],
        [
            pltpu.VMEM((10 * PAD, 512), BF16), pltpu.VMEM((10 * PAD, 256), BF16),
            pltpu.VMEM((ROWS, 128), F32), pltpu.VMEM((2, 432, 256), F32),
            pltpu.VMEM((8, WIDE, 512), BF16), pltpu.VMEM((8, PAD, 256), BF16), pltpu.VMEM((768, ROWS), BF16),
            pltpu.VMEM((192, ROWS), BF16), pltpu.VMEM((512, 768), BF16), pltpu.VMEM((512, 768), BF16),
            pltpu.VMEM((512, 768), BF16), pltpu.VMEM((768, 384), BF16), pltpu.SemaphoreType.DMA((18,)),
        ],
        [strips, pre, hid, ins, wide0, wide1, wide2, thin], 3e9, 4e6, limit=FULL, far_args=range(8),
    )
    total = mine + lax.ppermute(rest, ALL, cores)
    got = lax.ppermute(give, "space", swap)
    for stage in stages:
        parts = [lax.ppermute(total, ALL, pairs) for pairs in stage]
        total = (total + parts[0]) + (parts[1] + parts[2])
    other = lax.ppermute(total, ALL, cores)
    (input_grad,) = call(tile_kernel, "tile", [shape((4, 8, 8, 128), BF16)], [], [own, got], 1e6, 2e5)
    first, second = call(
        unpack_kernel, "unpack", [shape((4, 16, 27), F32), shape((27, 16, 32), F32)], [pltpu.VMEM((128, 128), F32)],
        [total, other], 1e6, 2e5,
    )
    return input_grad[None, None], first.transpose(2, 0, 1), second


def solution(mesh):
    placed = (
        P("dp", "space", None, None, None, None),
        P("dp", "space", None, None, None, None),
        P("dp", "space", None, None, None),
        P(),
        P(),
    )
    return jax.shard_map(
        body,
        mesh=mesh,
        in_specs=placed,
        out_specs=(P("dp", "space", None, None, None, None), P(), P()),
        check_vma=False,
    )
```

```python
import itertools

import jax
import jax.numpy as jnp
from jax import lax
from jax.experimental import pallas as pl
from jax.experimental.pallas import tpu as pltpu
from jax.sharding import PartitionSpec as P

LEAK = 0.3
STRIP = 64
WIDE = 72
PAD = 80
ROWS = 8 * PAD
FULL = 62
SOME = 20
ALL = ("dp", "space")
F32 = jnp.float32
BF16 = jnp.bfloat16


def iota(shape, dim):
    return lax.broadcasted_iota(jnp.int32, shape, dim)


def one_hot(flags):
    return jnp.where(flags, 1.0, 0.0).astype(BF16)


def dot(a, b):
    return jnp.dot(a, b, preferred_element_type=F32)


def dot_t(a, b):
    return lax.dot_general(a, b, (((1,), (1,)), ((), ())), preferred_element_type=F32)


def call(kernel, name, outs, scratch, args, flops, size, limit=10, far_args=(), far_outs=()):
    def spec(far):
        return pl.BlockSpec(memory_space=pltpu.HBM if far else pltpu.VMEM)

    return pl.pallas_call(
        kernel,
        name=name,
        out_shape=outs,
        in_specs=[spec(i in far_args) for i in range(len(args))],
        out_specs=[spec(i in far_outs) for i in range(len(outs))],
        scratch_shapes=scratch,
        compiler_params=pltpu.CompilerParams(vmem_limit_bytes=limit << 20),
        cost_estimate=pl.CostEstimate(flops=int(flops), bytes_accessed=int(size), transcendentals=0),
    )(*args)


def row_major():
    src, dst = iota((128, 128), 0), iota((128, 128), 1)
    return one_hot((src // 8 == dst % 16) & (src % 8 == dst // 16))


def cut_kernel(
    slab_hbm, pre_hbm, in_hbm, keep_hbm, send_hbm, out_hbm,
    slab_ref, pre_ref, in_ref, keep_ref, send_ref, out_ref, wide_ref, turned_ref, sems, done,
):
    copies = [pltpu.make_async_copy(in_hbm, in_ref, sems.at[0])]
    copies += [
        pltpu.make_async_copy(pre_hbm.at[:, pl.ds(4 * i, 4)], pre_ref.at[i], sems.at[1 + i]) for i in range(2)
    ]
    copies += [
        pltpu.make_async_copy(slab_hbm.at[:, :, pl.ds(128 * b, 128)], slab_ref.at[b], sems.at[3 + b]) for b in range(4)
    ]
    for copy in copies:
        copy.start()
    r = lax.rem(lax.axis_index("space"), 2)
    a, x = iota((WIDE, 128), 0), iota((WIDE, 128), 1)
    src, dst = iota((256, 256), 0), iota((256, 256), 1)
    same = one_hot((src // 64 == dst // 8 % 4) & (src // 8 % 8 == dst // 32) & (src % 8 == dst % 8))
    order = row_major()
    gap = jnp.where(a < STRIP, x - a, -9999)
    pick = jnp.concatenate(
        [jnp.where(gap == STRIP * r, 1.0, 0.0), jnp.where(gap == STRIP * (1 - r), 1.0, 0.0)], axis=0
    ).astype(BF16)
    copies[0].wait()
    rows = in_ref[...].astype(F32).reshape(256, 128).astype(BF16)
    got = dot(dot_t(pick, rows).astype(BF16), same)
    for half in range(2):
        keep_ref[8 + half] = got[:WIDE, 128 * half : 128 * half + 128].astype(BF16)
        send_ref[8 + half] = got[WIDE:, 128 * half : 128 * half + 128].astype(BF16)
    gap = jnp.where(a < STRIP + 2, x - a, -9999)
    picks = [jnp.where(gap == STRIP * r - 1, 1.0, 0.0), jnp.where(gap == STRIP * (1 - r) - 1, 1.0, 0.0)]
    end, x1 = iota((16, 128), 0), iota((16, 128), 1)
    edges = jnp.zeros((16, 128), F32)
    for z in range(8):
        if z % 4 == 0:
            copies[1 + z // 4].wait()
        ends = jnp.where((end % 8 == z) & (x1 == jnp.where(end < 8, 127, 0)), 1.0, 0.0)
        pick = jnp.concatenate(picks + [ends], axis=0).astype(BF16)
        rows = pre_ref[z // 4, :, z % 4].astype(F32).reshape(128, 128).astype(BF16)
        got = dot(dot_t(pick, rows).astype(BF16), order)
        keep_ref[z] = got[:WIDE].astype(BF16)
        send_ref[z] = got[WIDE : 2 * WIDE].astype(BF16)
        edges = edges + got[2 * WIDE :]
    results = [
        pltpu.make_async_copy(send_ref, send_hbm, done.at[8]), pltpu.make_async_copy(keep_ref, keep_hbm, done.at[9])
    ]
    for copy in results:
        copy.start()

    for b in range(4):
        copies[3 + b].wait()
        wide_ref[b] = slab_ref[b].astype(F32).reshape(512, 128)
        for y in range(16):
            slot = (y + 1) % 16
            turned_ref[32 * slot : 32 * slot + 32, 128 * b : 128 * b + 128] = wide_ref[
                b, pl.ds(y, 32, stride=16), :
            ].astype(BF16)
    p, x = iota((WIDE, 512), 0), iota((WIDE, 512), 1)
    gap = jnp.where(p < STRIP + 4, x - p, -9999)
    late = iota((8, 128), 0) >= 4
    for pair in range(2):
        strips = [jnp.where(gap == STRIP * t - 2, 1.0, 0.0) for t in range(4 * pair, 4 * pair + 4)]
        cut = dot_t(jnp.concatenate(strips, axis=0).astype(BF16), turned_ref[...])
        for i in range(4):
            t = 4 * pair + i
            out_ref[t, :STRIP] = cut[WIDE * i : WIDE * i + STRIP].astype(BF16)
            last = cut[WIDE * i + STRIP : WIDE * i + WIDE]
            edge = edges[:8] if t % 2 == 0 else edges[8:]
            last = jnp.concatenate(
                [
                    jnp.where(late, pltpu.roll(edge, 4, 0), last[:, :128]),
                    jnp.where(late, edge, last[:, 128:256]),
                    last[:, 256:],
                ],
                axis=1,
            )
            out_ref[t, STRIP:] = last.astype(BF16)
            results.append(pltpu.make_async_copy(out_ref.at[t], out_hbm.at[t], done.at[t]))
            results[-1].start()
    for copy in results:
        copy.wait()


def join(keep_ref, recv_ref, pre_ref, hid_ref, ins_ref, wide_ref, thin_ref):
    r = lax.rem(lax.axis_index("space"), 2)
    left = r == 0
    lane = iota((PAD, 128), 1)
    tail = jnp.zeros((PAD - WIDE, 128), F32)
    own = (iota((PAD, 128), 0) >= 1) & (iota((PAD, 128), 0) <= STRIP)
    for z in range(8):
        mine = jnp.concatenate([keep_ref[z].astype(F32), tail], axis=0)
        other = jnp.concatenate([recv_ref[z].astype(F32), tail], axis=0)
        for part in range(2):
            value = jnp.where(left, mine, other) if part == 0 else jnp.where(left, other, mine)
            pre_ref[z, :, 128 * part : 128 * part + 128] = value.astype(BF16)
            hidden = jnp.where(value > 0, value, LEAK * value)
            wide_ref[PAD * z : PAD * z + PAD, 128 * part : 128 * part + 128] = jnp.where(own, hidden, 0.0)
        mine = jnp.concatenate([keep_ref[8 + z // 4].astype(F32), tail], axis=0)
        other = jnp.concatenate([recv_ref[8 + z // 4].astype(F32), tail], axis=0)
        low, high = jnp.where(left, mine, other), jnp.where(left, other, mine)
        low = pltpu.roll(low, (128 - 32 * (z % 4)) % 128, 1)
        high = pltpu.roll(high, (160 - 32 * (z % 4)) % 128, 1)
        value = jnp.where(lane < 32, low, jnp.where(lane < 64, high, 0.0))
        thin_ref[PAD * z : PAD * z + PAD, :] = value
    for part in range(2):
        turned = wide_ref[:, 128 * part : 128 * part + 128].T
        for kx in range(3):
            shifted = pltpu.roll(turned, 2 - kx, 1) if kx < 2 else turned
            for y in range(8 * part, 8 * part + 8):
                rows = shifted[16 * (y % 8) : 16 * (y % 8) + 16].astype(BF16)
                for slot in {(y + 2) % 16, y + 2}:
                    hid_ref[48 * slot + 16 * kx : 48 * slot + 16 * kx + 16, :] = rows
    turned = thin_ref[...].T[:64]
    for kx in range(3):
        shifted = pltpu.roll(turned, 2 - kx, 1) if kx < 2 else turned
        ins_ref[64 * kx : 64 * kx + 64, :] = shifted.astype(BF16)


def band(two_ref, one_ref, wide_ref, thin_ref):
    def lay(terms, rows, kz, ky):
        parts = [terms[rows * (9 * kz + 3 * ky + kx) :][:rows] for kx in range(3)]
        return jnp.where(iota((rows, 128), 1) < 64, parts[0], parts[1]), parts[2]

    two = dot(two_ref[...], one_hot(iota((16, 128), 1) % 16 == iota((16, 128), 0)))
    group = iota((32, 128), 1) // 16 % 4
    for kz in range(3):
        terms = [lay(two, 32, kz, ky) for ky in range(3)]
        for slot in range(8):
            for half in range(2):
                block = jnp.zeros((32, 128), F32)
                for ky in range(3):
                    block = jnp.where(group == ky + slot - 2, terms[ky][half], block)
                at = 256 * kz + 32 * slot
                wide_ref[at : at + 32, 128 * half : 128 * half + 128] = block.astype(BF16)
    one = dot(one_ref[...], one_hot(iota((4, 128), 1) // 8 % 4 == iota((4, 128), 0)))
    lane = iota((16, 128), 1)
    group = 8 * (lane // 32 % 2) + lane % 8
    for kz in range(3):
        terms = [lay(one, 16, kz, ky) for ky in range(3)]
        for y in range(16):
            for half in range(2):
                block = jnp.zeros((16, 128), F32)
                for ky in range(3):
                    block = jnp.where(group == y + ky - 1, terms[ky][half], block)
                at = 256 * kz + 16 * y
                thin_ref[at : at + 16, 128 * half : 128 * half + 128] = block.astype(BF16)


def ready_kernel(
    keep_ref, recv_ref, two_ref, one_ref,
    pre_ref, hid_ref, ins_ref, wide_ref, thin_ref, hidden_ref, inputs_ref,
):
    band(two_ref, one_ref, wide_ref, thin_ref)
    join(keep_ref, recv_ref, pre_ref, hid_ref, ins_ref, hidden_ref, inputs_ref)


def planes(ref, kz, low, size):
    return ref[(2 - kz) * PAD : (2 - kz) * PAD + ROWS, low : low + size]


def across(sums):
    pair = sums[:, :128]
    pair = jnp.where(iota((ROWS, 128), 1) < 64, pltpu.roll(pair, ROWS - 2, 0), pltpu.roll(pair, ROWS - 1, 0))
    return pair + pltpu.roll(pair, 64, 1) + sums[:, 128:]


def grads_kernel(
    grad_ref, pre_ref, hid_ref, ins_ref, wide_ref, thin_ref,
    own_ref, give_ref, mine_ref, rest_ref, grad_s, act_s, out_s, terms_s,
):
    space = lax.axis_index("space")
    left = lax.rem(space, 2) == 0
    for block in (0, 9):
        grad_s[PAD * block : PAD * block + PAD, :] = jnp.zeros((PAD, 512), BF16)
        act_s[PAD * block : PAD * block + PAD, :] = jnp.zeros((PAD, 256), BF16)
    for z in range(8):
        plane = jnp.concatenate([grad_ref[z].astype(F32), jnp.zeros((PAD - WIDE, 512), F32)], axis=0)
        grad_s[PAD * (z + 1) : PAD * (z + 2), :] = plane.astype(BF16)

    lane = iota((16, 128), 1)
    taps = [None] * 28
    for kz in range(3):
        for half in range(2):
            terms_s[half] = dot(hid_ref[384 * half : 384 * half + 480, :], planes(grad_s, kz, 256 * half, 256))
        for kx in range(3):
            for ky in range(3):
                total = jnp.zeros((16, 128), F32)
                for y in range(16):
                    at = y + ky - 1
                    if 0 <= at < 16:
                        slot = (y + 1) % 16
                        half = slot // 8
                        row = 48 * ((at + 2) % 16 if half == 0 else at - 6) + 16 * kx
                        col = 128 * (slot % 8 // 4)
                        piece = terms_s[half, row : row + 16, col : col + 128]
                        total = total + jnp.where(lane // 32 == slot % 4, piece, 0.0)
                total = total + pltpu.roll(total, 64, 1)
                taps[9 * kz + 3 * ky + kx] = total + pltpu.roll(total, 32, 1)

    wide = [wide_ref[256 * kz : 256 * kz + 256, :] for kz in range(3)]
    none = jnp.zeros((32, 256), BF16)
    top = jnp.concatenate([part for w in wide for part in (none, w[32:])], axis=0)
    bottom = jnp.concatenate([part for w in wide for part in (w[:160], none, w[192:])], axis=0)
    parts = []
    for group in range(4):
        if group < 3:
            sides = [planes(grad_s, kz, 128 * group, 256) for kz in range(3)]
        else:
            sides = [planes(grad_s, kz, low, 128) for kz in range(3) for low in (384, 0)]
        weights = top if group == 0 else bottom if group == 3 else wide_ref[...]
        parts.append(across(dot(jnp.concatenate(sides, axis=1), weights)))
    low = iota((ROWS, 128), 1) < 64
    act = jnp.concatenate([jnp.where(low, parts[0], parts[1]), jnp.where(low, parts[2], parts[3])], axis=1)
    row = iota((PAD, 256), 0)
    at = STRIP * space - 1 + row
    inside = (row < STRIP + 2) & (at >= 0) & (at < 512)
    edge_row = row == jnp.where(left, 0, STRIP + 1)
    side = jnp.clip(space // 2 * 2 + jnp.where(left, -2, 2), 0, 6)
    edges = [grad_ref[side + r, STRIP:, :256].astype(F32) for r in range(2)]
    for z in range(8):
        beside = [edges[r][4 + z % 4 : 5 + z % 4, 128 * (z // 4) : 128 * (z // 4) + 128] for r in range(2)]
        pre = jnp.where(edge_row, jnp.concatenate(beside, axis=1), pre_ref[z].astype(F32))
        value = act[PAD * z : PAD * z + PAD] * jnp.where(pre > 0, 1.0, LEAK)
        act_s[PAD * (z + 1) : PAD * (z + 2), :] = jnp.where(inside, value, 0.0).astype(BF16)

    sides = jnp.concatenate([planes(act_s, kz, 0, 256) for kz in range(3)], axis=1)
    out_s[...] = across(dot(sides, thin_ref[...]))
    for z in range(4):
        pair = jnp.concatenate([out_s[PAD * z : PAD * z + STRIP], out_s[PAD * (z + 4) : PAD * (z + 4) + STRIP]], axis=0).T
        own_ref[z] = jnp.where(left, pair[:32], pair[32:64]).astype(BF16)
        give_ref[z] = jnp.where(left, pair[32:64], pair[:32]).astype(BF16)

    row, col = iota((64, 256), 0), iota((64, 256), 1)
    gap = 8 * (row // 32) + row % 8 - col // 16
    packed = jnp.zeros((12, 128), F32)
    for kz in range(3):
        terms = dot(ins_ref[...], planes(act_s, kz, 0, 256)).reshape(3, 64, 256)
        for ky in range(3):
            part = jnp.where((gap == ky - 1)[None], terms, 0.0)
            part = (part[:, :, :128] + part[:, :, 128:]).reshape(3, 2, 4, 8, 128)
            part = jnp.sum(part[:, 0] + part[:, 1], axis=2).reshape(12, 128)
            for by in (64, 32, 16):
                part = part + pltpu.roll(part, by, 1)
            if 3 * kz + ky < 8:
                packed = jnp.where(iota((12, 128), 1) // 16 == 3 * kz + ky, part, packed)
            else:
                last = part
    filler = jnp.zeros((4, 128), F32)
    taps[27] = jnp.concatenate([last, filler], axis=0)
    blocks = []
    for q in range(7):
        block = taps[4 * q]
        for g in range(1, 4):
            block = jnp.where(lane // 32 == g, taps[4 * q + g], block)
        blocks.append(block)
    blocks.append(jnp.concatenate([packed, filler], axis=0))
    first = lax.rem(lax.axis_index("dp"), 2) == 0
    cells = 16 * 8 * 16 * 512
    scale = cells**-0.5
    for q in range(4):
        low, high = blocks[q] * scale, blocks[q + 4] * scale
        mine_ref[16 * q : 16 * q + 16, :] = jnp.where(first, low, high)
        rest_ref[16 * q : 16 * q + 16, :] = jnp.where(first, high, low)


def tile_kernel(own_ref, recv_ref, out_ref):
    left = lax.rem(lax.axis_index("space"), 2) == 0
    low_lanes = iota((32, 128), 1) < STRIP
    for z in range(4):
        own, recv = own_ref[z].astype(F32), recv_ref[z].astype(F32)
        a, b = jnp.where(left, own, recv), jnp.where(left, recv, own)
        near = jnp.where(low_lanes, a, pltpu.roll(b, STRIP, 1))
        far = jnp.where(low_lanes, pltpu.roll(a, STRIP, 1), b)
        out_ref[:, z] = near.reshape(4, 8, 128).astype(BF16)
        out_ref[:, z + 4] = far.reshape(4, 8, 128).astype(BF16)


def unpack_kernel(mine_ref, rest_ref, one_ref, two_ref, flat_ref):
    first = lax.rem(lax.axis_index("dp"), 2) == 0
    mine, rest = mine_ref[...], rest_ref[...]
    low, high = jnp.where(first, mine, rest), jnp.where(first, rest, mine)
    blocks = [low[16 * q : 16 * q + 16] for q in range(4)] + [high[16 * q : 16 * q + 16] for q in range(4)]
    for pair in range(9):
        source, lane = (blocks[7], 16 * pair) if pair < 8 else (blocks[6], 96)
        source = pltpu.roll(source, 128 - lane, 1) if lane else source
        for kx in range(3):
            flat_ref[pl.ds(3 * pair + kx, 4, stride=32), :] = source[4 * kx : 4 * kx + 4]
    for k in range(27):
        two_ref[k] = blocks[k // 4][:, 32 * (k % 4) : 32 * (k % 4) + 32]
    turned = flat_ref[...].T
    for c in range(4):
        one_ref[c] = turned[:16, 32 * c : 32 * c + 27]


def routes():
    def number(zh, x, core, y, zl):
        return ((zh * 4 + x) * 2 + core) * 8 + y * 2 + zl

    every = list(itertools.product(range(2), range(4), range(2), range(4), range(2)))
    cores = [(number(*d), number(d[0], d[1], 1 - d[2], d[3], d[4])) for d in every]
    along_x = [[(number(*d), number(d[0], d[1] ^ j, *d[2:])) for d in every] for j in (1, 3, 2)]
    along_y = [[(number(*d), number(*d[:3], d[3] ^ j, d[4])) for d in every] for j in (1, 3, 2)]
    along_z = []
    for j in (1, 3, 2):
        pairs = []
        for d in every:
            z = (2 * d[0] + d[4]) ^ j
            pairs.append((number(*d), number(z // 2, d[1], d[2], d[3], z % 2)))
        along_z.append(pairs)
    return cores, [along_x, along_y, along_z]


def body(inputs, pre_act, out_grad, conv1_weight, conv2_weight):
    shape = jax.ShapeDtypeStruct
    cores, stages = routes()
    keep, send, strips = call(
        cut_kernel, "cut",
        [shape((10, WIDE, 128), BF16), shape((10, WIDE, 128), BF16), shape((8, WIDE, 512), BF16)],
        [
            pltpu.VMEM((4, 32, 16, 128), BF16), pltpu.VMEM((2, 16, 4, 8, 128), BF16), pltpu.VMEM((4, 8, 8, 128), BF16),
            pltpu.VMEM((10, WIDE, 128), BF16), pltpu.VMEM((10, WIDE, 128), BF16), pltpu.VMEM((8, WIDE, 512), BF16),
            pltpu.VMEM((4, 512, 128), F32), pltpu.VMEM((512, 512), BF16),
            pltpu.SemaphoreType.DMA((7,)), pltpu.SemaphoreType.DMA((10,)),
        ],
        [out_grad[0, 0], pre_act[0, 0], inputs[0, 0]], 4e8, 2e6, limit=FULL, far_args=(0, 1, 2), far_outs=(0, 1, 2),
    )
    swap = [(i, i ^ 1) for i in range(8)]
    recv = lax.ppermute(send, "space", swap)
    strips = lax.all_to_all(strips, "space", 0, 0, tiled=True)
    pre, hid, ins, wide, thin = call(
        ready_kernel, "ready",
        [
            shape((8, PAD, 256), BF16), shape((864, ROWS), BF16), shape((192, ROWS), BF16),
            shape((768, 256), BF16), shape((768, 256), BF16),
        ],
        [pltpu.VMEM((ROWS, 256), F32), pltpu.VMEM((ROWS, 128), F32)],
        [
            keep, recv, conv2_weight.transpose(0, 2, 1).reshape(864, 16),
            conv1_weight.transpose(0, 2, 1).reshape(432, 4),
        ],
        1e12, 5e6, limit=SOME,
    )
    own, give, mine, rest = call(
        grads_kernel, "grads",
        [shape((4, 32, 128), BF16), shape((4, 32, 128), BF16), shape((64, 128), F32), shape((64, 128), F32)],
        [
            pltpu.VMEM((10 * PAD, 512), BF16), pltpu.VMEM((10 * PAD, 256), BF16),
            pltpu.VMEM((ROWS, 128), F32), pltpu.VMEM((2, 480, 256), F32),
        ],
        [strips, pre, hid, ins, wide, thin], 3e9, 4e6, limit=SOME,
    )
    total = mine + lax.ppermute(rest, ALL, cores)
    got = lax.ppermute(give, "space", swap)
    for stage in stages:
        parts = [lax.ppermute(total, ALL, pairs) for pairs in stage]
        total = (total + parts[0]) + (parts[1] + parts[2])
    other = lax.ppermute(total, ALL, cores)
    (input_grad,) = call(tile_kernel, "tile", [shape((4, 8, 8, 128), BF16)], [], [own, got], 1e6, 2e5)
    first, second = call(
        unpack_kernel, "unpack", [shape((4, 16, 27), F32), shape((27, 16, 32), F32)], [pltpu.VMEM((128, 128), F32)],
        [total, other], 1e6, 2e5,
    )
    return input_grad[None, None], first.transpose(2, 0, 1), second


def solution(mesh):
    placed = (
        P("dp", "space", None, None, None, None),
        P("dp", "space", None, None, None, None),
        P("dp", "space", None, None, None),
        P(),
        P(),
    )
    return jax.shard_map(
        body,
        mesh=mesh,
        in_specs=placed,
        out_specs=(P("dp", "space", None, None, None, None), P(), P()),
        check_vma=False,
    )
```

```python
import itertools

import jax
import jax.numpy as jnp
from jax import lax
from jax.experimental import pallas as pl
from jax.experimental.pallas import tpu as pltpu
from jax.sharding import PartitionSpec as P

LEAK = 0.3
STRIP = 64
WIDE = 72
PAD = 80
ROWS = 8 * PAD
FULL = 62
SOME = 20
ALL = ("dp", "space")
F32 = jnp.float32
BF16 = jnp.bfloat16


def iota(shape, dim):
    return lax.broadcasted_iota(jnp.int32, shape, dim)


def one_hot(flags):
    return jnp.where(flags, 1.0, 0.0).astype(BF16)


def dot(a, b):
    return jnp.dot(a, b, preferred_element_type=F32)


def dot_t(a, b):
    return lax.dot_general(a, b, (((1,), (1,)), ((), ())), preferred_element_type=F32)


def call(kernel, name, outs, scratch, args, flops, size, limit=10, far_args=(), far_outs=()):
    def spec(far):
        return pl.BlockSpec(memory_space=pltpu.HBM if far else pltpu.VMEM)

    return pl.pallas_call(
        kernel,
        name=name,
        out_shape=outs,
        in_specs=[spec(i in far_args) for i in range(len(args))],
        out_specs=[spec(i in far_outs) for i in range(len(outs))],
        scratch_shapes=scratch,
        compiler_params=pltpu.CompilerParams(vmem_limit_bytes=limit << 20),
        cost_estimate=pl.CostEstimate(flops=int(flops), bytes_accessed=int(size), transcendentals=0),
    )(*args)


def row_major():
    src, dst = iota((128, 128), 0), iota((128, 128), 1)
    return one_hot((src // 8 == dst % 16) & (src % 8 == dst // 16))


def cut_kernel(
    slab_hbm, pre_hbm, in_hbm, keep_hbm, send_hbm, out_hbm,
    slab_ref, pre_ref, in_ref, keep_ref, send_ref, out_ref, wide_ref, turned_ref, sems, done,
):
    copies = [pltpu.make_async_copy(in_hbm, in_ref, sems.at[0])]
    copies += [
        pltpu.make_async_copy(pre_hbm.at[:, z], pre_ref.at[z], sems.at[5 + z]) for z in range(8)
    ]
    copies += [
        pltpu.make_async_copy(slab_hbm.at[:, :, pl.ds(128 * b, 128)], slab_ref.at[b], sems.at[1 + b]) for b in range(4)
    ]
    for copy in copies:
        copy.start()
    r = lax.rem(lax.axis_index("space"), 2)
    a, x = iota((WIDE, 128), 0), iota((WIDE, 128), 1)
    src, dst = iota((256, 256), 0), iota((256, 256), 1)
    same = one_hot((src // 64 == dst % 4) & (src // 8 % 8 == dst // 32) & (src % 8 == dst // 4 % 8))
    order = row_major()
    gap = jnp.where(a < STRIP, x - a, -9999)
    pick = jnp.concatenate(
        [jnp.where(gap == STRIP * r, 1.0, 0.0), jnp.where(gap == STRIP * (1 - r), 1.0, 0.0)], axis=0
    ).astype(BF16)
    copies[0].wait()
    rows = in_ref[...].astype(F32).reshape(256, 128).astype(BF16)
    got = dot(dot_t(pick, rows).astype(BF16), same)
    for half in range(2):
        keep_ref[8 + half] = got[:WIDE, 128 * half : 128 * half + 128].astype(BF16)
        send_ref[8 + half] = got[WIDE:, 128 * half : 128 * half + 128].astype(BF16)
    gap = jnp.where(a < STRIP + 2, x - a, -9999)
    end = iota((16, 128), 0)
    pick = jnp.concatenate(
        [
            jnp.where(gap == STRIP * r - 1, 1.0, 0.0),
            jnp.where(gap == STRIP * (1 - r) - 1, 1.0, 0.0),
            jnp.where(iota((16, 128), 1) == jnp.where(end == 0, 127, jnp.where(end == 8, 0, -1)), 1.0, 0.0),
        ],
        axis=0,
    ).astype(BF16)
    for copy in copies[1:9]:
        copy.wait()
    got = dot_t(pick, pre_ref[...].astype(F32).reshape(1024, 128).astype(BF16)).astype(BF16)
    got = dot(jnp.concatenate([got[:, 128 * z : 128 * z + 128] for z in range(8)], axis=0), order)
    edges = [jnp.zeros((8, 128), F32)] * 2
    for z in range(8):
        at = 160 * z
        keep_ref[z] = got[at : at + WIDE].astype(BF16)
        send_ref[z] = got[at + WIDE : at + 2 * WIDE].astype(BF16)
        for i in range(2):
            edges[i] = jnp.where(iota((8, 128), 0) == z, got[at + 144 + 8 * i : at + 145 + 8 * i], edges[i])
    results = [
        pltpu.make_async_copy(send_ref, send_hbm, done.at[8]), pltpu.make_async_copy(keep_ref, keep_hbm, done.at[9])
    ]
    for copy in results:
        copy.start()

    for b in range(4):
        copies[9 + b].wait()
        wide_ref[b] = slab_ref[b].astype(F32).reshape(512, 128)
        for y in range(16):
            slot = (y + 1) % 16
            turned_ref[32 * slot : 32 * slot + 32, 128 * b : 128 * b + 128] = wide_ref[
                b, pl.ds(y, 32, stride=16), :
            ].astype(BF16)
    p, x = iota((WIDE, 512), 0), iota((WIDE, 512), 1)
    gap = jnp.where(p < STRIP + 4, x - p, -9999)
    late = iota((8, 128), 0) >= 4
    for pair in range(2):
        strips = [jnp.where(gap == STRIP * t - 2, 1.0, 0.0) for t in range(4 * pair, 4 * pair + 4)]
        cut = dot_t(jnp.concatenate(strips, axis=0).astype(BF16), turned_ref[...])
        for i in range(4):
            t = 4 * pair + i
            out_ref[t, :STRIP] = cut[WIDE * i : WIDE * i + STRIP].astype(BF16)
            last = cut[WIDE * i + STRIP : WIDE * i + WIDE]
            edge = edges[t % 2]
            last = jnp.concatenate(
                [
                    jnp.where(late, pltpu.roll(edge, 4, 0), last[:, :128]),
                    jnp.where(late, edge, last[:, 128:256]),
                    last[:, 256:],
                ],
                axis=1,
            )
            out_ref[t, STRIP:] = last.astype(BF16)
            results.append(pltpu.make_async_copy(out_ref.at[t], out_hbm.at[t], done.at[t]))
            results[-1].start()
    for copy in results:
        copy.wait()


def join(keep_ref, recv_ref, pre_ref, hid_ref, ins_ref, wide_ref, thin_ref, rows_ref):
    r = lax.rem(lax.axis_index("space"), 2)
    left = r == 0
    lane = iota((PAD, 128), 1)
    tail = jnp.zeros((PAD - WIDE, 128), F32)
    own = (iota((PAD, 128), 0) >= 1) & (iota((PAD, 128), 0) <= STRIP)
    for z in range(8):
        mine = jnp.concatenate([keep_ref[z].astype(F32), tail], axis=0)
        other = jnp.concatenate([recv_ref[z].astype(F32), tail], axis=0)
        for part in range(2):
            value = jnp.where(left, mine, other) if part == 0 else jnp.where(left, other, mine)
            pre_ref[z, :, 128 * part : 128 * part + 128] = value.astype(BF16)
            hidden = jnp.where(value > 0, value, LEAK * value)
            wide_ref[PAD * z : PAD * z + PAD, 128 * part : 128 * part + 128] = jnp.where(own, hidden, 0.0)
        mine = jnp.concatenate([keep_ref[8 + z // 4].astype(F32), tail], axis=0)
        other = jnp.concatenate([recv_ref[8 + z // 4].astype(F32), tail], axis=0)
        low, high = jnp.where(left, mine, other), jnp.where(left, other, mine)
        low = pltpu.roll(low, (128 - 32 * (z % 4)) % 128, 1)
        high = pltpu.roll(high, (160 - 32 * (z % 4)) % 128, 1)
        value = jnp.where(lane < 32, low, jnp.where(lane < 64, high, 0.0))
        thin_ref[PAD * z : PAD * z + PAD, :] = value
    for part in range(2):
        turned = wide_ref[:, 128 * part : 128 * part + 128].T
        for kx in range(3):
            shifted = pltpu.roll(turned, 2 - kx, 1) if kx < 2 else turned
            for y in range(8 * part, 8 * part + 8):
                rows = shifted[16 * (y % 8) : 16 * (y % 8) + 16].astype(BF16)
                for slot in {(y + 2) % 16, y + 2}:
                    hid_ref[48 * slot + 16 * kx : 48 * slot + 16 * kx + 16, :] = rows
    turned = thin_ref[...].T[:64]
    rows_ref[...] = jnp.zeros((256, ROWS), F32)
    for kx in range(3):
        shifted = pltpu.roll(turned, 2 - kx, 1) if kx < 2 else turned
        for y in range(16):
            rows_ref[16 * y + 4 * kx : 16 * y + 4 * kx + 4, :] = shifted[4 * y : 4 * y + 4]
    ins_ref[...] = rows_ref[...].astype(BF16)


def band(two_ref, one_ref, wide_ref, thin_ref):
    def lay(terms, rows, kz, ky):
        parts = [terms[rows * (9 * kz + 3 * ky + kx) :][:rows] for kx in range(3)]
        return jnp.where(iota((rows, 128), 1) < 64, parts[0], parts[1]), parts[2]

    two = dot(two_ref[...], one_hot(iota((16, 128), 1) % 16 == iota((16, 128), 0)))
    group = iota((32, 128), 1) // 16 % 4
    for kz in range(3):
        terms = [lay(two, 32, kz, ky) for ky in range(3)]
        for slot in range(8):
            for half in range(2):
                block = jnp.zeros((32, 128), F32)
                for ky in range(3):
                    block = jnp.where(group == ky + slot - 2, terms[ky][half], block)
                at = 256 * kz + 32 * slot
                wide_ref[at : at + 32, 128 * half : 128 * half + 128] = block.astype(BF16)
    one = dot(one_ref[...], one_hot(iota((4, 128), 1) // 8 % 4 == iota((4, 128), 0)))
    lane = iota((16, 128), 1)
    group = 8 * (lane // 32 % 2) + lane % 8
    for kz in range(3):
        terms = [lay(one, 16, kz, ky) for ky in range(3)]
        for y in range(16):
            for half in range(2):
                block = jnp.zeros((16, 128), F32)
                for ky in range(3):
                    block = jnp.where(group == y + ky - 1, terms[ky][half], block)
                at = 256 * kz + 16 * y
                thin_ref[at : at + 16, 128 * half : 128 * half + 128] = block.astype(BF16)


def ready_kernel(
    keep_ref, recv_ref, two_ref, one_ref,
    pre_ref, hid_ref, ins_ref, wide_ref, thin_ref, hidden_ref, inputs_ref, rows_ref,
):
    band(two_ref, one_ref, wide_ref, thin_ref)
    join(keep_ref, recv_ref, pre_ref, hid_ref, ins_ref, hidden_ref, inputs_ref, rows_ref)


def planes(ref, kz, low, size):
    return ref[(2 - kz) * PAD : (2 - kz) * PAD + ROWS, low : low + size]


def across(sums):
    pair = sums[:, :128]
    pair = jnp.where(iota((ROWS, 128), 1) < 64, pltpu.roll(pair, ROWS - 2, 0), pltpu.roll(pair, ROWS - 1, 0))
    return pair + pltpu.roll(pair, 64, 1) + sums[:, 128:]


def grads_kernel(
    grad_hbm, pre_ref, hid_ref, ins_ref, wide_ref, thin_ref,
    own_ref, give_ref, mine_ref, rest_ref, grad_s, act_s, out_s, terms_s, first_s, sums_s, grad_ref, sems,
):
    copies = [pltpu.make_async_copy(grad_hbm.at[z], grad_ref.at[z], sems.at[z]) for z in range(8)]
    for copy in copies:
        copy.start()
    space = lax.axis_index("space")
    left = lax.rem(space, 2) == 0
    for block in (0, 9):
        grad_s[PAD * block : PAD * block + PAD, :] = jnp.zeros((PAD, 512), BF16)
        act_s[PAD * block : PAD * block + PAD, :] = jnp.zeros((PAD, 256), BF16)
    for z in range(8):
        copies[z].wait()
        plane = jnp.concatenate([grad_ref[z].astype(F32), jnp.zeros((PAD - WIDE, 512), F32)], axis=0)
        grad_s[PAD * (z + 1) : PAD * (z + 2), :] = plane.astype(BF16)

    for kz in range(3):
        for half in range(2):
            terms_s[kz, half] = dot(hid_ref[384 * half : 384 * half + 480, :], planes(grad_s, kz, 256 * half, 256))

    wide = [wide_ref[256 * kz : 256 * kz + 256, :] for kz in range(3)]
    none = jnp.zeros((32, 256), BF16)
    top = jnp.concatenate([part for w in wide for part in (none, w[32:])], axis=0)
    bottom = jnp.concatenate([part for w in wide for part in (w[:160], none, w[192:])], axis=0)
    parts = []
    for group in range(4):
        if group < 3:
            sides = [planes(grad_s, kz, 128 * group, 256) for kz in range(3)]
        else:
            sides = [planes(grad_s, kz, low, 128) for kz in range(3) for low in (384, 0)]
        weights = top if group == 0 else bottom if group == 3 else wide_ref[...]
        parts.append(across(dot(jnp.concatenate(sides, axis=1), weights)))
    low = iota((ROWS, 128), 1) < 64
    act = jnp.concatenate([jnp.where(low, parts[0], parts[1]), jnp.where(low, parts[2], parts[3])], axis=1)
    row = iota((PAD, 256), 0)
    at = STRIP * space - 1 + row
    inside = (row < STRIP + 2) & (at >= 0) & (at < 512)
    edge_row = row == jnp.where(left, 0, STRIP + 1)
    side = jnp.clip(space // 2 * 2 + jnp.where(left, -2, 2), 0, 6)
    edges = [grad_ref[side + r, STRIP:, :256].astype(F32) for r in range(2)]
    for z in range(8):
        beside = [edges[r][4 + z % 4 : 5 + z % 4, 128 * (z // 4) : 128 * (z // 4) + 128] for r in range(2)]
        pre = jnp.where(edge_row, jnp.concatenate(beside, axis=1), pre_ref[z].astype(F32))
        value = act[PAD * z : PAD * z + PAD] * jnp.where(pre > 0, 1.0, LEAK)
        act_s[PAD * (z + 1) : PAD * (z + 2), :] = jnp.where(inside, value, 0.0).astype(BF16)

    sides = jnp.concatenate([planes(act_s, kz, 0, 256) for kz in range(3)], axis=1)
    out_s[...] = across(dot(sides, thin_ref[...]))
    for kz in range(3):
        first_s[kz] = dot(ins_ref[...], planes(act_s, kz, 0, 256))

    cells = 16 * 8 * 16 * 512
    scale = cells**-0.5
    lane = iota((16, 128), 1)
    for kz in range(3):
        for ky in range(3):
            for kx in range(3):
                total = jnp.zeros((16, 128), F32)
                for y in range(16):
                    at = y + ky - 1
                    if 0 <= at < 16:
                        slot = (y + 1) % 16
                        half = slot // 8
                        row = 48 * ((at + 2) % 16 if half == 0 else at - 6) + 16 * kx
                        col = 128 * (slot % 8 // 4)
                        piece = terms_s[kz, half, row : row + 16, col : col + 128]
                        total = total + jnp.where(lane // 32 == slot % 4, piece, 0.0)
                total = total + pltpu.roll(total, 64, 1)
                total = (total + pltpu.roll(total, 32, 1)) * scale
                tap = 9 * kz + 3 * ky + kx
                at = 16 * (tap // 4)
                if tap % 4 == 0:
                    sums_s[at : at + 16, :] = total
                else:
                    sums_s[at : at + 16, :] = jnp.where(lane // 32 == tap % 4, total, sums_s[at : at + 16, :])

    row, col = iota((64, 128), 0), iota((64, 128), 1)
    eye = one_hot(jnp.where(left, row, (row + 32) % 64) == col)
    for z in range(4):
        pair = jnp.concatenate([out_s[PAD * z : PAD * z + STRIP], out_s[PAD * (z + 4) : PAD * (z + 4) + STRIP]], axis=0)
        pair = dot_t(eye, pair.astype(BF16))
        own_ref[z] = pair[:32].astype(BF16)
        give_ref[z] = pair[32:].astype(BF16)

    packed = jnp.zeros((16, 128), F32)
    for kz in range(3):
        for ky in range(3):
            total = jnp.zeros((16, 128), F32)
            for y in range(16):
                at = y + ky - 1
                if 0 <= at < 16:
                    piece = first_s[kz, 16 * at : 16 * at + 16, 128 * (y // 8) : 128 * (y // 8) + 128]
                    total = total + jnp.where(lane // 16 == y % 8, piece, 0.0)
            for by in (64, 32, 16):
                total = total + pltpu.roll(total, by, 1)
            total = total * scale
            if 3 * kz + ky < 8:
                packed = jnp.where(lane // 16 == 3 * kz + ky, total, packed)
            else:
                sums_s[96:112, :] = jnp.where(lane // 32 == 3, total, sums_s[96:112, :])
    sums_s[112:128, :] = packed
    first = lax.rem(lax.axis_index("dp"), 2) == 0
    mine_ref[...] = jnp.where(first, sums_s[:64, :], sums_s[64:, :])
    rest_ref[...] = jnp.where(first, sums_s[64:, :], sums_s[:64, :])


def tile_kernel(own_ref, recv_ref, out_ref):
    left = lax.rem(lax.axis_index("space"), 2) == 0
    low_lanes = iota((32, 128), 1) < STRIP
    for z in range(4):
        own, recv = own_ref[z].astype(F32), recv_ref[z].astype(F32)
        a, b = jnp.where(left, own, recv), jnp.where(left, recv, own)
        near = jnp.where(low_lanes, a, pltpu.roll(b, STRIP, 1))
        far = jnp.where(low_lanes, pltpu.roll(a, STRIP, 1), b)
        out_ref[:, z] = near.reshape(4, 8, 128).astype(BF16)
        out_ref[:, z + 4] = far.reshape(4, 8, 128).astype(BF16)


def unpack_kernel(mine_ref, rest_ref, one_ref, two_ref, flat_ref):
    first = lax.rem(lax.axis_index("dp"), 2) == 0
    mine, rest = mine_ref[...], rest_ref[...]
    low, high = jnp.where(first, mine, rest), jnp.where(first, rest, mine)
    blocks = [low[16 * q : 16 * q + 16] for q in range(4)] + [high[16 * q : 16 * q + 16] for q in range(4)]
    for pair in range(9):
        source, lane = (blocks[7], 16 * pair) if pair < 8 else (blocks[6], 96)
        source = pltpu.roll(source, 128 - lane, 1) if lane else source
        for kx in range(3):
            flat_ref[pl.ds(3 * pair + kx, 4, stride=32), :] = source[4 * kx : 4 * kx + 4]
    for k in range(27):
        two_ref[k] = blocks[k // 4][:, 32 * (k % 4) : 32 * (k % 4) + 32]
    turned = flat_ref[...].T
    for c in range(4):
        one_ref[c] = turned[:16, 32 * c : 32 * c + 27]


def routes():
    def number(zh, x, core, y, zl):
        return ((zh * 4 + x) * 2 + core) * 8 + y * 2 + zl

    every = list(itertools.product(range(2), range(4), range(2), range(4), range(2)))
    cores = [(number(*d), number(d[0], d[1], 1 - d[2], d[3], d[4])) for d in every]
    along_x = [[(number(*d), number(d[0], d[1] ^ j, *d[2:])) for d in every] for j in (1, 3, 2)]
    along_y = [[(number(*d), number(*d[:3], d[3] ^ j, d[4])) for d in every] for j in (1, 3, 2)]
    along_z = []
    for j in (1, 3, 2):
        pairs = []
        for d in every:
            z = (2 * d[0] + d[4]) ^ j
            pairs.append((number(*d), number(z // 2, d[1], d[2], d[3], z % 2)))
        along_z.append(pairs)
    return cores, [along_x, along_y, along_z]


def body(inputs, pre_act, out_grad, conv1_weight, conv2_weight):
    shape = jax.ShapeDtypeStruct
    cores, stages = routes()
    keep, send, strips = call(
        cut_kernel, "cut",
        [shape((10, WIDE, 128), BF16), shape((10, WIDE, 128), BF16), shape((8, WIDE, 512), BF16)],
        [
            pltpu.VMEM((4, 32, 16, 128), BF16), pltpu.VMEM((8, 16, 8, 128), BF16), pltpu.VMEM((4, 8, 8, 128), BF16),
            pltpu.VMEM((10, WIDE, 128), BF16), pltpu.VMEM((10, WIDE, 128), BF16), pltpu.VMEM((8, WIDE, 512), BF16),
            pltpu.VMEM((4, 512, 128), F32), pltpu.VMEM((512, 512), BF16),
            pltpu.SemaphoreType.DMA((13,)), pltpu.SemaphoreType.DMA((10,)),
        ],
        [out_grad[0, 0], pre_act[0, 0], inputs[0, 0]], 4e8, 2e6, limit=FULL, far_args=(0, 1, 2), far_outs=(0, 1, 2),
    )
    swap = [(i, i ^ 1) for i in range(8)]
    recv = lax.ppermute(send, "space", swap)
    strips = lax.all_to_all(strips, "space", 0, 0, tiled=True)
    pre, hid, ins, wide, thin = call(
        ready_kernel, "ready",
        [
            shape((8, PAD, 256), BF16), shape((864, ROWS), BF16), shape((256, ROWS), BF16),
            shape((768, 256), BF16), shape((768, 256), BF16),
        ],
        [pltpu.VMEM((ROWS, 256), F32), pltpu.VMEM((ROWS, 128), F32), pltpu.VMEM((256, ROWS), F32)],
        [
            keep, recv, conv2_weight.transpose(0, 2, 1).reshape(864, 16),
            conv1_weight.transpose(0, 2, 1).reshape(432, 4),
        ],
        1e12, 5e6, limit=SOME,
    )
    own, give, mine, rest = call(
        grads_kernel, "grads",
        [shape((4, 32, 128), BF16), shape((4, 32, 128), BF16), shape((64, 128), F32), shape((64, 128), F32)],
        [
            pltpu.VMEM((10 * PAD, 512), BF16), pltpu.VMEM((10 * PAD, 256), BF16),
            pltpu.VMEM((ROWS, 128), F32), pltpu.VMEM((3, 2, 480, 256), F32), pltpu.VMEM((3, 256, 256), F32), pltpu.VMEM((128, 128), F32),
            pltpu.VMEM((8, WIDE, 512), BF16), pltpu.SemaphoreType.DMA((8,)),
        ],
        [strips, pre, hid, ins, wide, thin], 3e9, 4e6, limit=SOME, far_args=(0,),
    )
    total = mine + lax.ppermute(rest, ALL, cores)
    got = lax.ppermute(give, "space", swap)
    for stage in stages:
        parts = [lax.ppermute(total, ALL, pairs) for pairs in stage]
        total = (total + parts[0]) + (parts[1] + parts[2])
    other = lax.ppermute(total, ALL, cores)
    (input_grad,) = call(tile_kernel, "tile", [shape((4, 8, 8, 128), BF16)], [], [own, got], 1e6, 2e5)
    first, second = call(
        unpack_kernel, "unpack", [shape((4, 16, 27), F32), shape((27, 16, 32), F32)], [pltpu.VMEM((128, 128), F32)],
        [total, other], 1e6, 2e5,
    )
    return input_grad[None, None], first.transpose(2, 0, 1), second


def solution(mesh):
    placed = (
        P("dp", "space", None, None, None, None),
        P("dp", "space", None, None, None, None),
        P("dp", "space", None, None, None),
        P(),
        P(),
    )
    return jax.shard_map(
        body,
        mesh=mesh,
        in_specs=placed,
        out_specs=(P("dp", "space", None, None, None, None), P(), P()),
        check_vma=False,
    )
```

```python
import itertools

import jax
import jax.numpy as jnp
from jax import lax
from jax.experimental import pallas as pl
from jax.experimental.pallas import tpu as pltpu
from jax.sharding import PartitionSpec as P

LEAK = 0.3
STRIP = 64
WIDE = 72
PAD = 80
ROWS = 8 * PAD
FULL = 62
SOME = 20
ALL = ("dp", "space")
F32 = jnp.float32
BF16 = jnp.bfloat16


def iota(shape, dim):
    return lax.broadcasted_iota(jnp.int32, shape, dim)


def one_hot(flags):
    return jnp.where(flags, 1.0, 0.0).astype(BF16)


def dot(a, b):
    return jnp.dot(a, b, preferred_element_type=F32)


def dot_t(a, b):
    return lax.dot_general(a, b, (((1,), (1,)), ((), ())), preferred_element_type=F32)


def call(kernel, name, outs, scratch, args, flops, size, limit=10, far_args=(), far_outs=()):
    def spec(far):
        return pl.BlockSpec(memory_space=pltpu.HBM if far else pltpu.VMEM)

    return pl.pallas_call(
        kernel,
        name=name,
        out_shape=outs,
        in_specs=[spec(i in far_args) for i in range(len(args))],
        out_specs=[spec(i in far_outs) for i in range(len(outs))],
        scratch_shapes=scratch,
        compiler_params=pltpu.CompilerParams(vmem_limit_bytes=limit << 20),
        cost_estimate=pl.CostEstimate(flops=int(flops), bytes_accessed=int(size), transcendentals=0),
    )(*args)


def row_major():
    src, dst = iota((128, 128), 0), iota((128, 128), 1)
    return one_hot((src // 8 == dst % 16) & (src % 8 == dst // 16))


def cut_kernel(
    slab_hbm, pre_hbm, in_hbm, keep_hbm, send_hbm, out_hbm,
    slab_ref, pre_ref, in_ref, keep_ref, send_ref, out_ref, wide_ref, turned_ref, sems, done,
):
    copies = [pltpu.make_async_copy(in_hbm, in_ref, sems.at[0])]
    copies += [
        pltpu.make_async_copy(pre_hbm.at[:, z], pre_ref.at[z], sems.at[5 + z]) for z in range(8)
    ]
    copies += [
        pltpu.make_async_copy(slab_hbm.at[:, :, pl.ds(128 * b, 128)], slab_ref.at[b], sems.at[1 + b]) for b in range(4)
    ]
    for copy in copies:
        copy.start()
    r = lax.rem(lax.axis_index("space"), 2)
    a, x = iota((WIDE, 128), 0), iota((WIDE, 128), 1)
    src, dst = iota((256, 256), 0), iota((256, 256), 1)
    same = one_hot((src // 64 == dst % 4) & (src // 8 % 8 == dst // 32) & (src % 8 == dst // 4 % 8))
    order = row_major()
    gap = jnp.where(a < STRIP, x - a, -9999)
    pick = jnp.concatenate(
        [jnp.where(gap == STRIP * r, 1.0, 0.0), jnp.where(gap == STRIP * (1 - r), 1.0, 0.0)], axis=0
    ).astype(BF16)
    copies[0].wait()
    rows = in_ref[...].astype(F32).reshape(256, 128).astype(BF16)
    got = dot(dot_t(pick, rows).astype(BF16), same)
    for half in range(2):
        keep_ref[8 + half] = got[:WIDE, 128 * half : 128 * half + 128].astype(BF16)
        send_ref[8 + half] = got[WIDE:, 128 * half : 128 * half + 128].astype(BF16)
    gap = jnp.where(a < STRIP + 2, x - a, -9999)
    end = iota((16, 128), 0)
    pick = jnp.concatenate(
        [
            jnp.where(gap == STRIP * r - 1, 1.0, 0.0),
            jnp.where(gap == STRIP * (1 - r) - 1, 1.0, 0.0),
            jnp.where(iota((16, 128), 1) == jnp.where(end == 0, 127, jnp.where(end == 8, 0, -1)), 1.0, 0.0),
        ],
        axis=0,
    ).astype(BF16)
    for copy in copies[1:9]:
        copy.wait()
    got = dot_t(pick, pre_ref[...].astype(F32).reshape(1024, 128).astype(BF16)).astype(BF16)
    got = dot(jnp.concatenate([got[:, 128 * z : 128 * z + 128] for z in range(8)], axis=0), order)
    edges = [jnp.zeros((8, 128), F32)] * 2
    for z in range(8):
        at = 160 * z
        keep_ref[z] = got[at : at + WIDE].astype(BF16)
        send_ref[z] = got[at + WIDE : at + 2 * WIDE].astype(BF16)
        for i in range(2):
            edges[i] = jnp.where(iota((8, 128), 0) == z, got[at + 144 + 8 * i : at + 145 + 8 * i], edges[i])
    results = [
        pltpu.make_async_copy(send_ref, send_hbm, done.at[8]), pltpu.make_async_copy(keep_ref, keep_hbm, done.at[9])
    ]
    for copy in results:
        copy.start()

    for b in range(4):
        copies[9 + b].wait()
        wide_ref[b] = slab_ref[b].astype(F32).reshape(512, 128)
        for y in range(16):
            slot = (y + 1) % 16
            turned_ref[32 * slot : 32 * slot + 32, 128 * b : 128 * b + 128] = wide_ref[
                b, pl.ds(y, 32, stride=16), :
            ].astype(BF16)
    p, x = iota((WIDE, 512), 0), iota((WIDE, 512), 1)
    gap = jnp.where(p < STRIP + 4, x - p, -9999)
    late = iota((8, 128), 0) >= 4
    for pair in range(2):
        strips = [jnp.where(gap == STRIP * t - 2, 1.0, 0.0) for t in range(4 * pair, 4 * pair + 4)]
        cut = dot_t(jnp.concatenate(strips, axis=0).astype(BF16), turned_ref[...])
        for i in range(4):
            t = 4 * pair + i
            out_ref[t, :STRIP] = cut[WIDE * i : WIDE * i + STRIP].astype(BF16)
            last = cut[WIDE * i + STRIP : WIDE * i + WIDE]
            edge = edges[t % 2]
            last = jnp.concatenate(
                [
                    jnp.where(late, pltpu.roll(edge, 4, 0), last[:, :128]),
                    jnp.where(late, edge, last[:, 128:256]),
                    last[:, 256:],
                ],
                axis=1,
            )
            out_ref[t, STRIP:] = last.astype(BF16)
            results.append(pltpu.make_async_copy(out_ref.at[t], out_hbm.at[t], done.at[t]))
            results[-1].start()
    for copy in results:
        copy.wait()


def join(keep_ref, recv_ref, pre_ref, hid_ref, ins_ref, wide_ref, thin_ref, rows_ref):
    r = lax.rem(lax.axis_index("space"), 2)
    left = r == 0
    lane = iota((PAD, 128), 1)
    tail = jnp.zeros((PAD - WIDE, 128), F32)
    own = (iota((PAD, 128), 0) >= 1) & (iota((PAD, 128), 0) <= STRIP)
    for z in range(8):
        mine = jnp.concatenate([keep_ref[z].astype(F32), tail], axis=0)
        other = jnp.concatenate([recv_ref[z].astype(F32), tail], axis=0)
        for part in range(2):
            value = jnp.where(left, mine, other) if part == 0 else jnp.where(left, other, mine)
            pre_ref[z, :, 128 * part : 128 * part + 128] = value.astype(BF16)
            hidden = jnp.where(value > 0, value, LEAK * value)
            wide_ref[PAD * z : PAD * z + PAD, 128 * part : 128 * part + 128] = jnp.where(own, hidden, 0.0)
        mine = jnp.concatenate([keep_ref[8 + z // 4].astype(F32), tail], axis=0)
        other = jnp.concatenate([recv_ref[8 + z // 4].astype(F32), tail], axis=0)
        low, high = jnp.where(left, mine, other), jnp.where(left, other, mine)
        low = pltpu.roll(low, (128 - 32 * (z % 4)) % 128, 1)
        high = pltpu.roll(high, (160 - 32 * (z % 4)) % 128, 1)
        value = jnp.where(lane < 32, low, jnp.where(lane < 64, high, 0.0))
        thin_ref[PAD * z : PAD * z + PAD, :] = value
    for part in range(2):
        turned = wide_ref[:, 128 * part : 128 * part + 128].T
        for kx in range(3):
            shifted = pltpu.roll(turned, 2 - kx, 1) if kx < 2 else turned
            for y in range(8 * part, 8 * part + 8):
                rows = shifted[16 * (y % 8) : 16 * (y % 8) + 16].astype(BF16)
                for slot in {(y + 2) % 16, y + 2}:
                    hid_ref[48 * slot + 16 * kx : 48 * slot + 16 * kx + 16, :] = rows
    turned = thin_ref[...].T[:64]
    rows_ref[...] = jnp.zeros((256, ROWS), F32)
    for kx in range(3):
        shifted = pltpu.roll(turned, 2 - kx, 1) if kx < 2 else turned
        for y in range(16):
            rows_ref[16 * y + 4 * kx : 16 * y + 4 * kx + 4, :] = shifted[4 * y : 4 * y + 4]
    ins_ref[...] = rows_ref[...].astype(BF16)


def lay(terms, rows, kz, ky):
    parts = [terms[rows * (9 * kz + 3 * ky + kx) :][:rows] for kx in range(3)]
    return jnp.where(iota((rows, 128), 1) < 64, parts[0], parts[1]), parts[2]


def band_two(two_ref, wide_ref):
    two = dot(two_ref[...], one_hot(iota((16, 128), 1) % 16 == iota((16, 128), 0)))
    group = iota((32, 128), 1) // 16 % 4
    for kz in range(3):
        terms = [lay(two, 32, kz, ky) for ky in range(3)]
        for slot in range(8):
            for half in range(2):
                block = jnp.zeros((32, 128), F32)
                for ky in range(3):
                    block = jnp.where(group == ky + slot - 2, terms[ky][half], block)
                at = 256 * kz + 32 * slot
                wide_ref[at : at + 32, 128 * half : 128 * half + 128] = block.astype(BF16)


def band_one(one_ref, thin_ref):
    one = dot(one_ref[...], one_hot(iota((4, 128), 1) // 8 % 4 == iota((4, 128), 0)))
    lane = iota((16, 128), 1)
    group = 8 * (lane // 32 % 2) + lane % 8
    for kz in range(3):
        terms = [lay(one, 16, kz, ky) for ky in range(3)]
        for y in range(16):
            for half in range(2):
                block = jnp.zeros((16, 128), F32)
                for ky in range(3):
                    block = jnp.where(group == y + ky - 1, terms[ky][half], block)
                at = 256 * kz + 16 * y
                thin_ref[at : at + 16, 128 * half : 128 * half + 128] = block.astype(BF16)


def ready_kernel(
    keep_ref, recv_ref, two_ref, pre_ref, hid_ref, ins_ref, wide_ref, hidden_ref, inputs_ref, rows_ref
):
    band_two(two_ref, wide_ref)
    join(keep_ref, recv_ref, pre_ref, hid_ref, ins_ref, hidden_ref, inputs_ref, rows_ref)


def planes(ref, kz, low, size):
    return ref[(2 - kz) * PAD : (2 - kz) * PAD + ROWS, low : low + size]


def across(sums):
    pair = sums[:, :128]
    pair = jnp.where(iota((ROWS, 128), 1) < 64, pltpu.roll(pair, ROWS - 2, 0), pltpu.roll(pair, ROWS - 1, 0))
    return pair + pltpu.roll(pair, 64, 1) + sums[:, 128:]


def grads_kernel(
    grad_ref, pre_ref, hid_ref, ins_ref, wide_ref,
    act_s, mine_ref, rest_ref, grad_s, terms_s, first_s, sums_s,
):
    space = lax.axis_index("space")
    left = lax.rem(space, 2) == 0
    for block in (0, 9):
        grad_s[PAD * block : PAD * block + PAD, :] = jnp.zeros((PAD, 512), BF16)
        act_s[PAD * block : PAD * block + PAD, :] = jnp.zeros((PAD, 256), BF16)
    for z in range(8):
        plane = jnp.concatenate([grad_ref[z].astype(F32), jnp.zeros((PAD - WIDE, 512), F32)], axis=0)
        grad_s[PAD * (z + 1) : PAD * (z + 2), :] = plane.astype(BF16)

    for kz in range(3):
        for half in range(2):
            terms_s[kz, half] = dot(hid_ref[384 * half : 384 * half + 480, :], planes(grad_s, kz, 256 * half, 256))

    wide = [wide_ref[256 * kz : 256 * kz + 256, :] for kz in range(3)]
    none = jnp.zeros((32, 256), BF16)
    top = jnp.concatenate([part for w in wide for part in (none, w[32:])], axis=0)
    bottom = jnp.concatenate([part for w in wide for part in (w[:160], none, w[192:])], axis=0)
    parts = []
    for group in range(4):
        if group < 3:
            sides = [planes(grad_s, kz, 128 * group, 256) for kz in range(3)]
        else:
            sides = [planes(grad_s, kz, low, 128) for kz in range(3) for low in (384, 0)]
        weights = top if group == 0 else bottom if group == 3 else wide_ref[...]
        parts.append(across(dot(jnp.concatenate(sides, axis=1), weights)))
    low = iota((ROWS, 128), 1) < 64
    act = jnp.concatenate([jnp.where(low, parts[0], parts[1]), jnp.where(low, parts[2], parts[3])], axis=1)
    row = iota((PAD, 256), 0)
    at = STRIP * space - 1 + row
    inside = (row < STRIP + 2) & (at >= 0) & (at < 512)
    edge_row = row == jnp.where(left, 0, STRIP + 1)
    side = jnp.clip(space // 2 * 2 + jnp.where(left, -2, 2), 0, 6)
    edges = [grad_ref[side + r, STRIP:, :256].astype(F32) for r in range(2)]
    for z in range(8):
        beside = [edges[r][4 + z % 4 : 5 + z % 4, 128 * (z // 4) : 128 * (z // 4) + 128] for r in range(2)]
        pre = jnp.where(edge_row, jnp.concatenate(beside, axis=1), pre_ref[z].astype(F32))
        value = act[PAD * z : PAD * z + PAD] * jnp.where(pre > 0, 1.0, LEAK)
        act_s[PAD * (z + 1) : PAD * (z + 2), :] = jnp.where(inside, value, 0.0).astype(BF16)

    for kz in range(3):
        first_s[kz] = dot(ins_ref[...], planes(act_s, kz, 0, 256))

    cells = 16 * 8 * 16 * 512
    scale = cells**-0.5
    lane = iota((16, 128), 1)
    for kz in range(3):
        for ky in range(3):
            for kx in range(3):
                total = jnp.zeros((16, 128), F32)
                for y in range(16):
                    at = y + ky - 1
                    if 0 <= at < 16:
                        slot = (y + 1) % 16
                        half = slot // 8
                        row = 48 * ((at + 2) % 16 if half == 0 else at - 6) + 16 * kx
                        col = 128 * (slot % 8 // 4)
                        piece = terms_s[kz, half, row : row + 16, col : col + 128]
                        total = total + jnp.where(lane // 32 == slot % 4, piece, 0.0)
                total = total + pltpu.roll(total, 64, 1)
                total = (total + pltpu.roll(total, 32, 1)) * scale
                tap = 9 * kz + 3 * ky + kx
                at = 16 * (tap // 4)
                if tap % 4 == 0:
                    sums_s[at : at + 16, :] = total
                else:
                    sums_s[at : at + 16, :] = jnp.where(lane // 32 == tap % 4, total, sums_s[at : at + 16, :])

    packed = jnp.zeros((16, 128), F32)
    for kz in range(3):
        for ky in range(3):
            total = jnp.zeros((16, 128), F32)
            for y in range(16):
                at = y + ky - 1
                if 0 <= at < 16:
                    piece = first_s[kz, 16 * at : 16 * at + 16, 128 * (y // 8) : 128 * (y // 8) + 128]
                    total = total + jnp.where(lane // 16 == y % 8, piece, 0.0)
            for by in (64, 32, 16):
                total = total + pltpu.roll(total, by, 1)
            total = total * scale
            if 3 * kz + ky < 8:
                packed = jnp.where(lane // 16 == 3 * kz + ky, total, packed)
            else:
                sums_s[96:112, :] = jnp.where(lane // 32 == 3, total, sums_s[96:112, :])
    sums_s[112:128, :] = packed
    first = lax.rem(lax.axis_index("dp"), 2) == 0
    mine_ref[...] = jnp.where(first, sums_s[:64, :], sums_s[64:, :])
    rest_ref[...] = jnp.where(first, sums_s[64:, :], sums_s[:64, :])


def back_kernel(act_s, one_ref, own_ref, give_ref, out_s, thin_ref):
    band_one(one_ref, thin_ref)
    left = lax.rem(lax.axis_index("space"), 2) == 0
    sides = jnp.concatenate([planes(act_s, kz, 0, 256) for kz in range(3)], axis=1)
    out_s[...] = across(dot(sides, thin_ref[...]))
    row, col = iota((64, 128), 0), iota((64, 128), 1)
    eye = one_hot(jnp.where(left, row, (row + 32) % 64) == col)
    for z in range(4):
        pair = jnp.concatenate([out_s[PAD * z : PAD * z + STRIP], out_s[PAD * (z + 4) : PAD * (z + 4) + STRIP]], axis=0)
        pair = dot_t(eye, pair.astype(BF16))
        own_ref[z] = pair[:32].astype(BF16)
        give_ref[z] = pair[32:].astype(BF16)


def tile_kernel(own_ref, recv_ref, out_ref):
    left = lax.rem(lax.axis_index("space"), 2) == 0
    low_lanes = iota((32, 128), 1) < STRIP
    for z in range(4):
        own, recv = own_ref[z].astype(F32), recv_ref[z].astype(F32)
        a, b = jnp.where(left, own, recv), jnp.where(left, recv, own)
        near = jnp.where(low_lanes, a, pltpu.roll(b, STRIP, 1))
        far = jnp.where(low_lanes, pltpu.roll(a, STRIP, 1), b)
        out_ref[:, z] = near.reshape(4, 8, 128).astype(BF16)
        out_ref[:, z + 4] = far.reshape(4, 8, 128).astype(BF16)


def unpack_kernel(mine_ref, rest_ref, one_ref, two_ref, flat_ref):
    first = lax.rem(lax.axis_index("dp"), 2) == 0
    mine, rest = mine_ref[...], rest_ref[...]
    low, high = jnp.where(first, mine, rest), jnp.where(first, rest, mine)
    blocks = [low[16 * q : 16 * q + 16] for q in range(4)] + [high[16 * q : 16 * q + 16] for q in range(4)]
    for pair in range(9):
        source, lane = (blocks[7], 16 * pair) if pair < 8 else (blocks[6], 96)
        source = pltpu.roll(source, 128 - lane, 1) if lane else source
        for kx in range(3):
            flat_ref[pl.ds(3 * pair + kx, 4, stride=32), :] = source[4 * kx : 4 * kx + 4]
    for k in range(27):
        two_ref[k] = blocks[k // 4][:, 32 * (k % 4) : 32 * (k % 4) + 32]
    turned = flat_ref[...].T
    for c in range(4):
        one_ref[c] = turned[:16, 32 * c : 32 * c + 27]


def routes():
    def number(zh, x, core, y, zl):
        return ((zh * 4 + x) * 2 + core) * 8 + y * 2 + zl

    every = list(itertools.product(range(2), range(4), range(2), range(4), range(2)))
    cores = [(number(*d), number(d[0], d[1], 1 - d[2], d[3], d[4])) for d in every]
    along_x = [[(number(*d), number(d[0], d[1] ^ j, *d[2:])) for d in every] for j in (1, 3, 2)]
    along_y = [[(number(*d), number(*d[:3], d[3] ^ j, d[4])) for d in every] for j in (1, 3, 2)]
    along_z = []
    for j in (1, 3, 2):
        pairs = []
        for d in every:
            z = (2 * d[0] + d[4]) ^ j
            pairs.append((number(*d), number(z // 2, d[1], d[2], d[3], z % 2)))
        along_z.append(pairs)
    return cores, [along_x, along_y, along_z]


def body(inputs, pre_act, out_grad, conv1_weight, conv2_weight):
    shape = jax.ShapeDtypeStruct
    cores, stages = routes()
    keep, send, strips = call(
        cut_kernel, "cut",
        [shape((10, WIDE, 128), BF16), shape((10, WIDE, 128), BF16), shape((8, WIDE, 512), BF16)],
        [
            pltpu.VMEM((4, 32, 16, 128), BF16), pltpu.VMEM((8, 16, 8, 128), BF16), pltpu.VMEM((4, 8, 8, 128), BF16),
            pltpu.VMEM((10, WIDE, 128), BF16), pltpu.VMEM((10, WIDE, 128), BF16), pltpu.VMEM((8, WIDE, 512), BF16),
            pltpu.VMEM((4, 512, 128), F32), pltpu.VMEM((512, 512), BF16),
            pltpu.SemaphoreType.DMA((13,)), pltpu.SemaphoreType.DMA((10,)),
        ],
        [out_grad[0, 0], pre_act[0, 0], inputs[0, 0]], 4e8, 2e6, limit=FULL, far_args=(0, 1, 2), far_outs=(0, 1, 2),
    )
    swap = [(i, i ^ 1) for i in range(8)]
    recv = lax.ppermute(send, "space", swap)
    strips = lax.all_to_all(strips, "space", 0, 0, tiled=True)
    pre, hid, ins, wide = call(
        ready_kernel, "ready",
        [
            shape((8, PAD, 256), BF16), shape((864, ROWS), BF16), shape((256, ROWS), BF16),
            shape((768, 256), BF16),
        ],
        [pltpu.VMEM((ROWS, 256), F32), pltpu.VMEM((ROWS, 128), F32), pltpu.VMEM((256, ROWS), F32)],
        [keep, recv, conv2_weight.transpose(0, 2, 1).reshape(864, 16)],
        2e10, 5e6, limit=SOME,
    )
    act, mine, rest = call(
        grads_kernel, "grads",
        [shape((10 * PAD, 256), BF16), shape((64, 128), F32), shape((64, 128), F32)],
        [
            pltpu.VMEM((10 * PAD, 512), BF16), pltpu.VMEM((3, 2, 480, 256), F32), pltpu.VMEM((3, 256, 256), F32),
            pltpu.VMEM((128, 128), F32),
        ],
        [strips, pre, hid, ins, wide], 3e9, 4e6, limit=SOME,
    )
    own, give = call(
        back_kernel, "back", [shape((4, 32, 128), BF16), shape((4, 32, 128), BF16)], [pltpu.VMEM((ROWS, 128), F32), pltpu.VMEM((768, 256), BF16)],
        [act, conv1_weight.transpose(0, 2, 1).reshape(432, 4)], 5e8, 1e6,
    )
    total = mine + lax.ppermute(rest, ALL, cores)
    got = lax.ppermute(give, "space", swap)
    for stage in stages:
        parts = [lax.ppermute(total, ALL, pairs) for pairs in stage]
        total = (total + parts[0]) + (parts[1] + parts[2])
    other = lax.ppermute(total, ALL, cores)
    (input_grad,) = call(tile_kernel, "tile", [shape((4, 8, 8, 128), BF16)], [], [own, got], 1e6, 2e5)
    first, second = call(
        unpack_kernel, "unpack", [shape((4, 16, 27), F32), shape((27, 16, 32), F32)], [pltpu.VMEM((128, 128), F32)],
        [total, other], 1e6, 2e5,
    )
    return input_grad[None, None], first.transpose(2, 0, 1), second


def solution(mesh):
    placed = (
        P("dp", "space", None, None, None, None),
        P("dp", "space", None, None, None, None),
        P("dp", "space", None, None, None),
        P(),
        P(),
    )
    return jax.shard_map(
        body,
        mesh=mesh,
        in_specs=placed,
        out_specs=(P("dp", "space", None, None, None, None), P(), P()),
        check_vma=False,
    )
```

```python
import itertools

import jax
import jax.numpy as jnp
from jax import lax
from jax.experimental import pallas as pl
from jax.experimental.pallas import tpu as pltpu
from jax.sharding import PartitionSpec as P

LEAK = 0.3
STRIP = 64
WIDE = 72
PAD = 80
ROWS = 8 * PAD
FULL = 62
SOME = 20
ALL = ("dp", "space")
F32 = jnp.float32
BF16 = jnp.bfloat16


def iota(shape, dim):
    return lax.broadcasted_iota(jnp.int32, shape, dim)


def one_hot(flags):
    return jnp.where(flags, 1.0, 0.0).astype(BF16)


def dot(a, b):
    return jnp.dot(a, b, preferred_element_type=F32)


def dot_t(a, b):
    return lax.dot_general(a, b, (((1,), (1,)), ((), ())), preferred_element_type=F32)


def call(kernel, name, outs, scratch, args, flops, size, limit=10, far_args=(), far_outs=()):
    def spec(far):
        return pl.BlockSpec(memory_space=pltpu.HBM if far else pltpu.VMEM)

    return pl.pallas_call(
        kernel,
        name=name,
        out_shape=outs,
        in_specs=[spec(i in far_args) for i in range(len(args))],
        out_specs=[spec(i in far_outs) for i in range(len(outs))],
        scratch_shapes=scratch,
        compiler_params=pltpu.CompilerParams(vmem_limit_bytes=limit << 20),
        cost_estimate=pl.CostEstimate(flops=int(flops), bytes_accessed=int(size), transcendentals=0),
    )(*args)


def row_major():
    src, dst = iota((128, 128), 0), iota((128, 128), 1)
    return one_hot((src // 8 == dst % 16) & (src % 8 == dst // 16))


def cut_kernel(
    slab_hbm, pre_hbm, in_hbm, keep_hbm, send_hbm, out_hbm,
    slab_ref, pre_ref, in_ref, keep_ref, send_ref, out_ref, wide_ref, turned_ref, sems, done,
):
    copies = [pltpu.make_async_copy(in_hbm, in_ref, sems.at[0])]
    copies += [
        pltpu.make_async_copy(pre_hbm.at[:, z], pre_ref.at[z], sems.at[5 + z]) for z in range(8)
    ]
    copies += [
        pltpu.make_async_copy(slab_hbm.at[:, :, pl.ds(128 * b, 128)], slab_ref.at[b], sems.at[1 + b]) for b in range(4)
    ]
    for copy in copies:
        copy.start()
    r = lax.rem(lax.axis_index("space"), 2)
    a, x = iota((WIDE, 128), 0), iota((WIDE, 128), 1)
    src, dst = iota((256, 256), 0), iota((256, 256), 1)
    same = one_hot((src // 64 == dst % 4) & (src // 8 % 8 == dst // 32) & (src % 8 == dst // 4 % 8))
    order = row_major()
    gap = jnp.where(a < STRIP, x - a, -9999)
    pick = jnp.concatenate(
        [jnp.where(gap == STRIP * r, 1.0, 0.0), jnp.where(gap == STRIP * (1 - r), 1.0, 0.0)], axis=0
    ).astype(BF16)
    copies[0].wait()
    rows = in_ref[...].astype(F32).reshape(256, 128).astype(BF16)
    got = dot(dot_t(pick, rows).astype(BF16), same)
    for half in range(2):
        keep_ref[8 + half] = got[:WIDE, 128 * half : 128 * half + 128].astype(BF16)
        send_ref[8 + half] = got[WIDE:, 128 * half : 128 * half + 128].astype(BF16)
    gap = jnp.where(a < STRIP + 2, x - a, -9999)
    end = iota((16, 128), 0)
    pick = jnp.concatenate(
        [
            jnp.where(gap == STRIP * r - 1, 1.0, 0.0),
            jnp.where(gap == STRIP * (1 - r) - 1, 1.0, 0.0),
            jnp.where(iota((16, 128), 1) == jnp.where(end == 0, 127, jnp.where(end == 8, 0, -1)), 1.0, 0.0),
        ],
        axis=0,
    ).astype(BF16)
    for copy in copies[1:9]:
        copy.wait()
    got = dot_t(pick, pre_ref[...].astype(F32).reshape(1024, 128).astype(BF16)).astype(BF16)
    got = dot(jnp.concatenate([got[:, 128 * z : 128 * z + 128] for z in range(8)], axis=0), order)
    edges = [jnp.zeros((8, 128), F32)] * 2
    for z in range(8):
        at = 160 * z
        keep_ref[z] = got[at : at + WIDE].astype(BF16)
        send_ref[z] = got[at + WIDE : at + 2 * WIDE].astype(BF16)
        for i in range(2):
            edges[i] = jnp.where(iota((8, 128), 0) == z, got[at + 144 + 8 * i : at + 145 + 8 * i], edges[i])
    results = [
        pltpu.make_async_copy(send_ref, send_hbm, done.at[8]), pltpu.make_async_copy(keep_ref, keep_hbm, done.at[9])
    ]
    for copy in results:
        copy.start()

    for b in range(4):
        copies[9 + b].wait()
        wide_ref[b] = slab_ref[b].astype(F32).reshape(512, 128)
        for y in range(16):
            slot = (y + 1) % 16
            turned_ref[32 * slot : 32 * slot + 32, 128 * b : 128 * b + 128] = wide_ref[
                b, pl.ds(y, 32, stride=16), :
            ].astype(BF16)
    p, x = iota((WIDE, 512), 0), iota((WIDE, 512), 1)
    gap = jnp.where(p < STRIP + 4, x - p, -9999)
    late = iota((8, 128), 0) >= 4
    for pair in range(2):
        strips = [jnp.where(gap == STRIP * t - 2, 1.0, 0.0) for t in range(4 * pair, 4 * pair + 4)]
        cut = dot_t(jnp.concatenate(strips, axis=0).astype(BF16), turned_ref[...])
        for i in range(4):
            t = 4 * pair + i
            out_ref[t, :STRIP] = cut[WIDE * i : WIDE * i + STRIP].astype(BF16)
            last = cut[WIDE * i + STRIP : WIDE * i + WIDE]
            edge = edges[t % 2]
            last = jnp.concatenate(
                [
                    jnp.where(late, pltpu.roll(edge, 4, 0), last[:, :128]),
                    jnp.where(late, edge, last[:, 128:256]),
                    last[:, 256:],
                ],
                axis=1,
            )
            out_ref[t, STRIP:] = last.astype(BF16)
            results.append(pltpu.make_async_copy(out_ref.at[t], out_hbm.at[t], done.at[t]))
            results[-1].start()
    for copy in results:
        copy.wait()


def join(keep_ref, recv_ref, pre_ref, hid_ref, ins_ref, wide_ref, thin_ref, rows_ref):
    r = lax.rem(lax.axis_index("space"), 2)
    left = r == 0
    lane = iota((PAD, 128), 1)
    tail = jnp.zeros((PAD - WIDE, 128), F32)
    own = (iota((PAD, 128), 0) >= 1) & (iota((PAD, 128), 0) <= STRIP)
    for z in range(8):
        mine = jnp.concatenate([keep_ref[z].astype(F32), tail], axis=0)
        other = jnp.concatenate([recv_ref[z].astype(F32), tail], axis=0)
        for part in range(2):
            value = jnp.where(left, mine, other) if part == 0 else jnp.where(left, other, mine)
            pre_ref[z, :, 128 * part : 128 * part + 128] = value.astype(BF16)
            hidden = jnp.where(value > 0, value, LEAK * value)
            wide_ref[PAD * z : PAD * z + PAD, 128 * part : 128 * part + 128] = jnp.where(own, hidden, 0.0)
        mine = jnp.concatenate([keep_ref[8 + z // 4].astype(F32), tail], axis=0)
        other = jnp.concatenate([recv_ref[8 + z // 4].astype(F32), tail], axis=0)
        low, high = jnp.where(left, mine, other), jnp.where(left, other, mine)
        low = pltpu.roll(low, (128 - 32 * (z % 4)) % 128, 1)
        high = pltpu.roll(high, (160 - 32 * (z % 4)) % 128, 1)
        value = jnp.where(lane < 32, low, jnp.where(lane < 64, high, 0.0))
        thin_ref[PAD * z : PAD * z + PAD, :] = value
    for part in range(2):
        turned = wide_ref[:, 128 * part : 128 * part + 128].T
        for kx in range(3):
            shifted = pltpu.roll(turned, 2 - kx, 1) if kx < 2 else turned
            for y in range(8 * part, 8 * part + 8):
                rows = shifted[16 * (y % 8) : 16 * (y % 8) + 16].astype(BF16)
                for slot in {(y + 2) % 16, y + 2}:
                    hid_ref[48 * slot + 16 * kx : 48 * slot + 16 * kx + 16, :] = rows
    turned = thin_ref[...].T[:64]
    rows_ref[...] = jnp.zeros((256, ROWS), F32)
    for kx in range(3):
        shifted = pltpu.roll(turned, 2 - kx, 1) if kx < 2 else turned
        for y in range(16):
            rows_ref[16 * y + 4 * kx : 16 * y + 4 * kx + 4, :] = shifted[4 * y : 4 * y + 4]
    ins_ref[...] = rows_ref[...].astype(BF16)


def lay(terms, rows, kz, ky):
    parts = [terms[rows * (9 * kz + 3 * ky + kx) :][:rows] for kx in range(3)]
    return jnp.where(iota((rows, 128), 1) < 64, parts[0], parts[1]), parts[2]


def band_two(two_ref, wide_ref):
    two = dot(two_ref[...], one_hot(iota((16, 128), 1) % 16 == iota((16, 128), 0)))
    group = iota((32, 128), 1) // 16 % 4
    for kz in range(3):
        terms = [lay(two, 32, kz, ky) for ky in range(3)]
        for slot in range(8):
            for half in range(2):
                block = jnp.zeros((32, 128), F32)
                for ky in range(3):
                    block = jnp.where(group == ky + slot - 2, terms[ky][half], block)
                at = 256 * kz + 32 * slot
                wide_ref[at : at + 32, 128 * half : 128 * half + 128] = block.astype(BF16)


def band_one(one_ref, thin_ref):
    one = dot(one_ref[...], one_hot(iota((4, 128), 1) // 8 % 4 == iota((4, 128), 0)))
    lane = iota((16, 128), 1)
    group = 8 * (lane // 32 % 2) + lane % 8
    for kz in range(3):
        terms = [lay(one, 16, kz, ky) for ky in range(3)]
        for y in range(16):
            for half in range(2):
                block = jnp.zeros((16, 128), F32)
                for ky in range(3):
                    block = jnp.where(group == y + ky - 1, terms[ky][half], block)
                at = 256 * kz + 16 * y
                thin_ref[at : at + 16, 128 * half : 128 * half + 128] = block.astype(BF16)


def ready_kernel(
    keep_ref, recv_ref, two_ref, pre_ref, hid_ref, ins_ref, wide_ref, hidden_ref, inputs_ref, rows_ref
):
    band_two(two_ref, wide_ref)
    join(keep_ref, recv_ref, pre_ref, hid_ref, ins_ref, hidden_ref, inputs_ref, rows_ref)


def planes(ref, kz, low, size):
    return ref[(2 - kz) * PAD : (2 - kz) * PAD + ROWS, low : low + size]


def across(sums):
    pair = sums[:, :128]
    pair = jnp.where(iota((ROWS, 128), 1) < 64, pltpu.roll(pair, ROWS - 2, 0), pltpu.roll(pair, ROWS - 1, 0))
    return pair + pltpu.roll(pair, 64, 1) + sums[:, 128:]


def grads_kernel(
    grad_ref, pre_ref, hid_ref, ins_ref, wide_ref,
    act_s, sums_s, grad_s, terms_s, first_s,
):
    space = lax.axis_index("space")
    left = lax.rem(space, 2) == 0
    for block in (0, 9):
        grad_s[PAD * block : PAD * block + PAD, :] = jnp.zeros((PAD, 512), BF16)
        act_s[PAD * block : PAD * block + PAD, :] = jnp.zeros((PAD, 256), BF16)
    for z in range(8):
        at = PAD * (z + 1)
        grad_s[at : at + STRIP, :] = grad_ref[z, :STRIP]
        last = jnp.concatenate([grad_ref[z, STRIP:].astype(F32), jnp.zeros((PAD - WIDE, 512), F32)], axis=0)
        grad_s[at + STRIP : at + PAD, :] = last.astype(BF16)

    for kz in range(3):
        for half in range(2):
            terms_s[kz, half] = dot(hid_ref[384 * half : 384 * half + 480, :], planes(grad_s, kz, 256 * half, 256))

    wide = [wide_ref[256 * kz : 256 * kz + 256, :] for kz in range(3)]
    none = jnp.zeros((32, 256), BF16)
    top = jnp.concatenate([part for w in wide for part in (none, w[32:])], axis=0)
    bottom = jnp.concatenate([part for w in wide for part in (w[:160], none, w[192:])], axis=0)
    parts = []
    for group in range(4):
        if group < 3:
            sides = [planes(grad_s, kz, 128 * group, 256) for kz in range(3)]
        else:
            sides = [planes(grad_s, kz, low, 128) for kz in range(3) for low in (384, 0)]
        weights = top if group == 0 else bottom if group == 3 else wide_ref[...]
        parts.append(across(dot(jnp.concatenate(sides, axis=1), weights)))
    low = iota((ROWS, 128), 1) < 64
    act = jnp.concatenate([jnp.where(low, parts[0], parts[1]), jnp.where(low, parts[2], parts[3])], axis=1)
    row = iota((PAD, 256), 0)
    at = STRIP * space - 1 + row
    inside = (row < STRIP + 2) & (at >= 0) & (at < 512)
    edge_row = row == jnp.where(left, 0, STRIP + 1)
    side = jnp.clip(space // 2 * 2 + jnp.where(left, -2, 2), 0, 6)
    edges = [grad_ref[side + r, STRIP:, :256].astype(F32) for r in range(2)]
    for z in range(8):
        beside = [edges[r][4 + z % 4 : 5 + z % 4, 128 * (z // 4) : 128 * (z // 4) + 128] for r in range(2)]
        pre = jnp.where(edge_row, jnp.concatenate(beside, axis=1), pre_ref[z].astype(F32))
        value = act[PAD * z : PAD * z + PAD] * jnp.where(pre > 0, 1.0, LEAK)
        act_s[PAD * (z + 1) : PAD * (z + 2), :] = jnp.where(inside, value, 0.0).astype(BF16)

    for kz in range(3):
        first_s[kz] = dot(ins_ref[...], planes(act_s, kz, 0, 256))

    cells = 16 * 8 * 16 * 512
    scale = cells**-0.5
    lane = iota((16, 128), 1)
    for kz in range(3):
        for ky in range(3):
            for kx in range(3):
                total = jnp.zeros((16, 128), F32)
                for y in range(16):
                    at = y + ky - 1
                    if 0 <= at < 16:
                        slot = (y + 1) % 16
                        half = slot // 8
                        row = 48 * ((at + 2) % 16 if half == 0 else at - 6) + 16 * kx
                        col = 128 * (slot % 8 // 4)
                        piece = terms_s[kz, half, row : row + 16, col : col + 128]
                        total = total + jnp.where(lane // 32 == slot % 4, piece, 0.0)
                total = total + pltpu.roll(total, 64, 1)
                total = (total + pltpu.roll(total, 32, 1)) * scale
                tap = 9 * kz + 3 * ky + kx
                at = 16 * (tap // 4)
                if tap % 4 == 0:
                    sums_s[at : at + 16, :] = total
                else:
                    sums_s[at : at + 16, :] = jnp.where(lane // 32 == tap % 4, total, sums_s[at : at + 16, :])

    packed = jnp.zeros((16, 128), F32)
    for kz in range(3):
        for ky in range(3):
            total = jnp.zeros((16, 128), F32)
            for y in range(16):
                at = y + ky - 1
                if 0 <= at < 16:
                    piece = first_s[kz, 16 * at : 16 * at + 16, 128 * (y // 8) : 128 * (y // 8) + 128]
                    total = total + jnp.where(lane // 16 == y % 8, piece, 0.0)
            for by in (64, 32, 16):
                total = total + pltpu.roll(total, by, 1)
            total = total * scale
            if 3 * kz + ky < 8:
                packed = jnp.where(lane // 16 == 3 * kz + ky, total, packed)
            else:
                sums_s[96:112, :] = jnp.where(lane // 32 == 3, total, sums_s[96:112, :])
    sums_s[112:128, :] = packed


def back_kernel(act_s, one_ref, own_ref, give_ref, out_s, thin_ref):
    band_one(one_ref, thin_ref)
    left = lax.rem(lax.axis_index("space"), 2) == 0
    sides = jnp.concatenate([planes(act_s, kz, 0, 256) for kz in range(3)], axis=1)
    out_s[...] = across(dot(sides, thin_ref[...]))
    row, col = iota((64, 128), 0), iota((64, 128), 1)
    eye = one_hot(jnp.where(left, row, (row + 32) % 64) == col)
    for z in range(4):
        pair = jnp.concatenate([out_s[PAD * z : PAD * z + STRIP], out_s[PAD * (z + 4) : PAD * (z + 4) + STRIP]], axis=0)
        pair = dot_t(eye, pair.astype(BF16))
        own_ref[z] = pair[:32].astype(BF16)
        give_ref[z] = pair[32:].astype(BF16)


def tile_kernel(own_ref, recv_ref, out_ref):
    left = lax.rem(lax.axis_index("space"), 2) == 0
    low_lanes = iota((32, 128), 1) < STRIP
    for z in range(4):
        own, recv = own_ref[z].astype(F32), recv_ref[z].astype(F32)
        a, b = jnp.where(left, own, recv), jnp.where(left, recv, own)
        near = jnp.where(low_lanes, a, pltpu.roll(b, STRIP, 1))
        far = jnp.where(low_lanes, pltpu.roll(a, STRIP, 1), b)
        out_ref[:, z] = near.reshape(4, 8, 128).astype(BF16)
        out_ref[:, z + 4] = far.reshape(4, 8, 128).astype(BF16)


def unpack_kernel(total_ref, one_ref, two_ref, flat_ref):
    blocks = [total_ref[16 * q : 16 * q + 16] for q in range(8)]
    for pair in range(9):
        source, lane = (blocks[7], 16 * pair) if pair < 8 else (blocks[6], 96)
        source = pltpu.roll(source, 128 - lane, 1) if lane else source
        for kx in range(3):
            flat_ref[pl.ds(3 * pair + kx, 4, stride=32), :] = source[4 * kx : 4 * kx + 4]
    for k in range(27):
        two_ref[k] = blocks[k // 4][:, 32 * (k % 4) : 32 * (k % 4) + 32]
    turned = flat_ref[...].T
    for c in range(4):
        one_ref[c] = turned[:16, 32 * c : 32 * c + 27]


def routes():
    def number(zh, x, core, y, zl):
        return ((zh * 4 + x) * 2 + core) * 8 + y * 2 + zl

    every = list(itertools.product(range(2), range(4), range(2), range(4), range(2)))
    cores = [(number(*d), number(d[0], d[1], 1 - d[2], d[3], d[4])) for d in every]
    along_x = [[(number(*d), number(d[0], d[1] ^ j, *d[2:])) for d in every] for j in (1, 3, 2)]
    along_y = [[(number(*d), number(*d[:3], d[3] ^ j, d[4])) for d in every] for j in (1, 3, 2)]
    along_z = []
    for j in (1, 3, 2):
        pairs = []
        for d in every:
            z = (2 * d[0] + d[4]) ^ j
            pairs.append((number(*d), number(z // 2, d[1], d[2], d[3], z % 2)))
        along_z.append(pairs)
    return cores, [along_x, along_y, along_z]


def body(inputs, pre_act, out_grad, conv1_weight, conv2_weight):
    shape = jax.ShapeDtypeStruct
    cores, stages = routes()
    keep, send, strips = call(
        cut_kernel, "cut",
        [shape((10, WIDE, 128), BF16), shape((10, WIDE, 128), BF16), shape((8, WIDE, 512), BF16)],
        [
            pltpu.VMEM((4, 32, 16, 128), BF16), pltpu.VMEM((8, 16, 8, 128), BF16), pltpu.VMEM((4, 8, 8, 128), BF16),
            pltpu.VMEM((10, WIDE, 128), BF16), pltpu.VMEM((10, WIDE, 128), BF16), pltpu.VMEM((8, WIDE, 512), BF16),
            pltpu.VMEM((4, 512, 128), F32), pltpu.VMEM((512, 512), BF16),
            pltpu.SemaphoreType.DMA((13,)), pltpu.SemaphoreType.DMA((10,)),
        ],
        [out_grad[0, 0], pre_act[0, 0], inputs[0, 0]], 4e8, 2e6, limit=FULL, far_args=(0, 1, 2), far_outs=(0, 1, 2),
    )
    swap = [(i, i ^ 1) for i in range(8)]
    recv = lax.ppermute(send, "space", swap)
    strips = lax.all_to_all(strips, "space", 0, 0, tiled=True)
    pre, hid, ins, wide = call(
        ready_kernel, "ready",
        [
            shape((8, PAD, 256), BF16), shape((864, ROWS), BF16), shape((256, ROWS), BF16),
            shape((768, 256), BF16),
        ],
        [pltpu.VMEM((ROWS, 256), F32), pltpu.VMEM((ROWS, 128), F32), pltpu.VMEM((256, ROWS), F32)],
        [keep, recv, conv2_weight.transpose(0, 2, 1).reshape(864, 16)],
        2e10, 5e6, limit=SOME,
    )
    act, sums = call(
        grads_kernel, "grads",
        [shape((10 * PAD, 256), BF16), shape((128, 128), F32)],
        [
            pltpu.VMEM((10 * PAD, 512), BF16), pltpu.VMEM((3, 2, 480, 256), F32), pltpu.VMEM((3, 256, 256), F32),
        ],
        [strips, pre, hid, ins, wide], 3e9, 4e6, limit=SOME,
    )
    own, give = call(
        back_kernel, "back", [shape((4, 32, 128), BF16), shape((4, 32, 128), BF16)], [pltpu.VMEM((ROWS, 128), F32), pltpu.VMEM((768, 256), BF16)],
        [act, conv1_weight.transpose(0, 2, 1).reshape(432, 4)], 5e8, 1e6,
    )
    total = sums + lax.ppermute(sums, ALL, cores)
    got = None
    for stage in stages:
        parts = [lax.ppermute(total, ALL, pairs) for pairs in stage]
        total = (total + parts[0]) + (parts[1] + parts[2])
        if got is None:
            total, give = lax.optimization_barrier((total, give))
            got = lax.ppermute(give, "space", swap)
        elif stage is stages[1]:
            total, got = lax.optimization_barrier((total, got))
    (input_grad,) = call(tile_kernel, "tile", [shape((4, 8, 8, 128), BF16)], [], [own, got], 1e6, 2e5)
    first, second = call(
        unpack_kernel, "unpack", [shape((4, 16, 27), F32), shape((27, 16, 32), F32)], [pltpu.VMEM((128, 128), F32)],
        [total], 1e6, 2e5,
    )
    return input_grad[None, None], first.transpose(2, 0, 1), second


def solution(mesh):
    placed = (
        P("dp", "space", None, None, None, None),
        P("dp", "space", None, None, None, None),
        P("dp", "space", None, None, None),
        P(),
        P(),
    )
    return jax.shard_map(
        body,
        mesh=mesh,
        in_specs=placed,
        out_specs=(P("dp", "space", None, None, None, None), P(), P()),
        check_vma=False,
    )
```

```python
import itertools

import jax
import jax.numpy as jnp
from jax import lax
from jax.experimental import pallas as pl
from jax.experimental.pallas import tpu as pltpu
from jax.sharding import PartitionSpec as P

LEAK = 0.3
STRIP = 64
WIDE = 72
PAD = 80
ROWS = 8 * PAD
FULL = 62
SOME = 20
ALL = ("dp", "space")
F32 = jnp.float32
BF16 = jnp.bfloat16


def iota(shape, dim):
    return lax.broadcasted_iota(jnp.int32, shape, dim)


def one_hot(flags):
    return jnp.where(flags, 1.0, 0.0).astype(BF16)


def dot(a, b):
    return jnp.dot(a, b, preferred_element_type=F32)


def dot_t(a, b):
    return lax.dot_general(a, b, (((1,), (1,)), ((), ())), preferred_element_type=F32)


def call(kernel, name, outs, scratch, args, flops, size, limit=10, far_args=(), far_outs=()):
    def spec(far):
        return pl.BlockSpec(memory_space=pltpu.HBM if far else pltpu.VMEM)

    return pl.pallas_call(
        kernel,
        name=name,
        out_shape=outs,
        in_specs=[spec(i in far_args) for i in range(len(args))],
        out_specs=[spec(i in far_outs) for i in range(len(outs))],
        scratch_shapes=scratch,
        compiler_params=pltpu.CompilerParams(vmem_limit_bytes=limit << 20),
        cost_estimate=pl.CostEstimate(flops=int(flops), bytes_accessed=int(size), transcendentals=0),
    )(*args)


def row_major():
    src, dst = iota((128, 128), 0), iota((128, 128), 1)
    return one_hot((src // 8 == dst % 16) & (src % 8 == dst // 16))


def cut_kernel(
    slab_hbm, pre_hbm, in_hbm, keep_hbm, send_hbm, out_hbm,
    slab_ref, pre_ref, in_ref, keep_ref, send_ref, out_ref, wide_ref, turned_ref, sems, done,
):
    copies = [pltpu.make_async_copy(in_hbm, in_ref, sems.at[0])]
    copies += [
        pltpu.make_async_copy(pre_hbm.at[:, z], pre_ref.at[z], sems.at[5 + z]) for z in range(8)
    ]
    copies += [
        pltpu.make_async_copy(slab_hbm.at[:, :, pl.ds(128 * b, 128)], slab_ref.at[b], sems.at[1 + b]) for b in range(4)
    ]
    for copy in copies:
        copy.start()
    r = lax.rem(lax.axis_index("space"), 2)
    a, x = iota((WIDE, 128), 0), iota((WIDE, 128), 1)
    src, dst = iota((256, 256), 0), iota((256, 256), 1)
    same = one_hot((src // 64 == dst % 4) & (src // 8 % 8 == dst // 32) & (src % 8 == dst // 4 % 8))
    order = row_major()
    gap = jnp.where(a < STRIP, x - a, -9999)
    pick = jnp.concatenate(
        [jnp.where(gap == STRIP * r, 1.0, 0.0), jnp.where(gap == STRIP * (1 - r), 1.0, 0.0)], axis=0
    ).astype(BF16)
    copies[0].wait()
    rows = in_ref[...].astype(F32).reshape(256, 128).astype(BF16)
    got = dot(dot_t(pick, rows).astype(BF16), same)
    for half in range(2):
        keep_ref[8 + half] = got[:WIDE, 128 * half : 128 * half + 128].astype(BF16)
        send_ref[8 + half] = got[WIDE:, 128 * half : 128 * half + 128].astype(BF16)
    gap = jnp.where(a < STRIP + 2, x - a, -9999)
    end = iota((16, 128), 0)
    pick = jnp.concatenate(
        [
            jnp.where(gap == STRIP * r - 1, 1.0, 0.0),
            jnp.where(gap == STRIP * (1 - r) - 1, 1.0, 0.0),
            jnp.where(iota((16, 128), 1) == jnp.where(end == 0, 127, jnp.where(end == 8, 0, -1)), 1.0, 0.0),
        ],
        axis=0,
    ).astype(BF16)
    for copy in copies[1:9]:
        copy.wait()
    got = dot_t(pick, pre_ref[...].astype(F32).reshape(1024, 128).astype(BF16)).astype(BF16)
    got = dot(jnp.concatenate([got[:, 128 * z : 128 * z + 128] for z in range(8)], axis=0), order)
    edges = [jnp.zeros((8, 128), F32)] * 2
    for z in range(8):
        at = 160 * z
        keep_ref[z] = got[at : at + WIDE].astype(BF16)
        send_ref[z] = got[at + WIDE : at + 2 * WIDE].astype(BF16)
        for i in range(2):
            edges[i] = jnp.where(iota((8, 128), 0) == z, got[at + 144 + 8 * i : at + 145 + 8 * i], edges[i])
    results = [
        pltpu.make_async_copy(send_ref, send_hbm, done.at[8]), pltpu.make_async_copy(keep_ref, keep_hbm, done.at[9])
    ]
    for copy in results:
        copy.start()

    for b in range(4):
        copies[9 + b].wait()
        wide_ref[b] = slab_ref[b].astype(F32).reshape(512, 128)
        for y in range(16):
            slot = (y + 1) % 16
            turned_ref[32 * slot : 32 * slot + 32, 128 * b : 128 * b + 128] = wide_ref[
                b, pl.ds(y, 32, stride=16), :
            ].astype(BF16)
    p, x = iota((WIDE, 512), 0), iota((WIDE, 512), 1)
    gap = jnp.where(p < STRIP + 4, x - p, -9999)
    late = iota((8, 128), 0) >= 4
    for pair in range(2):
        strips = [jnp.where(gap == STRIP * t - 2, 1.0, 0.0) for t in range(4 * pair, 4 * pair + 4)]
        cut = dot_t(jnp.concatenate(strips, axis=0).astype(BF16), turned_ref[...])
        for i in range(4):
            t = 4 * pair + i
            out_ref[t, :STRIP] = cut[WIDE * i : WIDE * i + STRIP].astype(BF16)
            last = cut[WIDE * i + STRIP : WIDE * i + WIDE]
            edge = edges[t % 2]
            last = jnp.concatenate(
                [
                    jnp.where(late, pltpu.roll(edge, 4, 0), last[:, :128]),
                    jnp.where(late, edge, last[:, 128:256]),
                    last[:, 256:],
                ],
                axis=1,
            )
            out_ref[t, STRIP:] = last.astype(BF16)
            results.append(pltpu.make_async_copy(out_ref.at[t], out_hbm.at[t], done.at[t]))
            results[-1].start()
    for copy in results:
        copy.wait()


def join(keep_ref, recv_ref, pre_ref, hid_ref, ins_ref, wide_ref, thin_ref, rows_ref):
    r = lax.rem(lax.axis_index("space"), 2)
    left = r == 0
    lane = iota((PAD, 128), 1)
    tail = jnp.zeros((PAD - WIDE, 128), F32)
    own = (iota((PAD, 128), 0) >= 1) & (iota((PAD, 128), 0) <= STRIP)
    for z in range(8):
        mine = jnp.concatenate([keep_ref[z].astype(F32), tail], axis=0)
        other = jnp.concatenate([recv_ref[z].astype(F32), tail], axis=0)
        for part in range(2):
            value = jnp.where(left, mine, other) if part == 0 else jnp.where(left, other, mine)
            pre_ref[z, :, 128 * part : 128 * part + 128] = value.astype(BF16)
            hidden = jnp.where(value > 0, value, LEAK * value)
            wide_ref[PAD * z : PAD * z + PAD, 128 * part : 128 * part + 128] = jnp.where(own, hidden, 0.0)
        mine = jnp.concatenate([keep_ref[8 + z // 4].astype(F32), tail], axis=0)
        other = jnp.concatenate([recv_ref[8 + z // 4].astype(F32), tail], axis=0)
        low, high = jnp.where(left, mine, other), jnp.where(left, other, mine)
        low = pltpu.roll(low, (128 - 32 * (z % 4)) % 128, 1)
        high = pltpu.roll(high, (160 - 32 * (z % 4)) % 128, 1)
        value = jnp.where(lane < 32, low, jnp.where(lane < 64, high, 0.0))
        thin_ref[PAD * z : PAD * z + PAD, :] = value
    for part in range(2):
        turned = wide_ref[:, 128 * part : 128 * part + 128].T
        for kx in range(3):
            shifted = pltpu.roll(turned, 2 - kx, 1) if kx < 2 else turned
            for y in range(8 * part, 8 * part + 8):
                rows = shifted[16 * (y % 8) : 16 * (y % 8) + 16].astype(BF16)
                for slot in {(y + 2) % 16, y + 2}:
                    hid_ref[48 * slot + 16 * kx : 48 * slot + 16 * kx + 16, :] = rows
    turned = thin_ref[...].T[:64]
    rows_ref[...] = jnp.zeros((256, ROWS), F32)
    for kx in range(3):
        shifted = pltpu.roll(turned, 2 - kx, 1) if kx < 2 else turned
        for y in range(16):
            rows_ref[16 * y + 4 * kx : 16 * y + 4 * kx + 4, :] = shifted[4 * y : 4 * y + 4]
    ins_ref[...] = rows_ref[...].astype(BF16)


def lay(terms, rows, kz, ky):
    parts = [terms[rows * (9 * kz + 3 * ky + kx) :][:rows] for kx in range(3)]
    return jnp.where(iota((rows, 128), 1) < 64, parts[0], parts[1]), parts[2]


def band_two(two_ref, wide_ref):
    two = dot(two_ref[...], one_hot(iota((16, 128), 1) % 16 == iota((16, 128), 0)))
    group = iota((32, 128), 1) // 16 % 4
    for kz in range(3):
        terms = [lay(two, 32, kz, ky) for ky in range(3)]
        for slot in range(8):
            for half in range(2):
                block = jnp.zeros((32, 128), F32)
                for ky in range(3):
                    block = jnp.where(group == ky + slot - 2, terms[ky][half], block)
                at = 256 * kz + 32 * slot
                wide_ref[at : at + 32, 128 * half : 128 * half + 128] = block.astype(BF16)


def band_one(one_ref, thin_ref):
    one = dot(one_ref[...], one_hot(iota((4, 128), 1) // 8 % 4 == iota((4, 128), 0)))
    lane = iota((16, 128), 1)
    group = 8 * (lane // 32 % 2) + lane % 8
    for kz in range(3):
        terms = [lay(one, 16, kz, ky) for ky in range(3)]
        for y in range(16):
            for half in range(2):
                block = jnp.zeros((16, 128), F32)
                for ky in range(3):
                    block = jnp.where(group == y + ky - 1, terms[ky][half], block)
                at = 256 * kz + 16 * y
                thin_ref[at : at + 16, 128 * half : 128 * half + 128] = block.astype(BF16)


def ready_kernel(
    keep_ref, recv_ref, two_ref, pre_ref, hid_ref, ins_ref, wide_ref, hidden_ref, inputs_ref, rows_ref
):
    band_two(two_ref, wide_ref)
    join(keep_ref, recv_ref, pre_ref, hid_ref, ins_ref, hidden_ref, inputs_ref, rows_ref)


def planes(ref, kz, low, size):
    return ref[(2 - kz) * PAD : (2 - kz) * PAD + ROWS, low : low + size]


def across(sums):
    pair = sums[:, :128]
    pair = jnp.where(iota((ROWS, 128), 1) < 64, pltpu.roll(pair, ROWS - 2, 0), pltpu.roll(pair, ROWS - 1, 0))
    return pair + pltpu.roll(pair, 64, 1) + sums[:, 128:]


def grads_kernel(
    grad_ref, pre_ref, hid_ref, ins_ref, wide_ref,
    act_s, mine_ref, rest_ref, grad_s, terms_s, first_s, sums_s, raw_s,
):
    space = lax.axis_index("space")
    left = lax.rem(space, 2) == 0
    for block in (0, 9):
        grad_s[PAD * block : PAD * block + PAD, :] = jnp.zeros((PAD, 512), BF16)
        act_s[PAD * block : PAD * block + PAD, :] = jnp.zeros((PAD, 256), BF16)
    for z in range(8):
        at = PAD * (z + 1)
        grad_s[at : at + STRIP, :] = grad_ref[z, :STRIP]
        last = jnp.concatenate([grad_ref[z, STRIP:].astype(F32), jnp.zeros((PAD - WIDE, 512), F32)], axis=0)
        grad_s[at + STRIP : at + PAD, :] = last.astype(BF16)

    wide = [wide_ref[256 * kz : 256 * kz + 256, :] for kz in range(3)]
    none = jnp.zeros((32, 256), BF16)
    top = jnp.concatenate([part for w in wide for part in (none, w[32:])], axis=0)
    bottom = jnp.concatenate([part for w in wide for part in (w[:160], none, w[192:])], axis=0)
    for group in range(4):
        if group < 3:
            sides = [planes(grad_s, kz, 128 * group, 256) for kz in range(3)]
        else:
            sides = [planes(grad_s, kz, low, 128) for kz in range(3) for low in (384, 0)]
        weights = top if group == 0 else bottom if group == 3 else wide_ref[...]
        raw_s[group] = dot(jnp.concatenate(sides, axis=1), weights)
    for kz in range(3):
        for half in range(2):
            terms_s[kz, half] = dot(hid_ref[384 * half : 384 * half + 480, :], planes(grad_s, kz, 256 * half, 256))
    parts = [across(raw_s[group]) for group in range(4)]
    low = iota((ROWS, 128), 1) < 64
    act = jnp.concatenate([jnp.where(low, parts[0], parts[1]), jnp.where(low, parts[2], parts[3])], axis=1)
    row = iota((PAD, 256), 0)
    at = STRIP * space - 1 + row
    inside = (row < STRIP + 2) & (at >= 0) & (at < 512)
    edge_row = row == jnp.where(left, 0, STRIP + 1)
    side = jnp.clip(space // 2 * 2 + jnp.where(left, -2, 2), 0, 6)
    edges = [grad_ref[side + r, STRIP:, :256].astype(F32) for r in range(2)]
    for z in range(8):
        beside = [edges[r][4 + z % 4 : 5 + z % 4, 128 * (z // 4) : 128 * (z // 4) + 128] for r in range(2)]
        pre = jnp.where(edge_row, jnp.concatenate(beside, axis=1), pre_ref[z].astype(F32))
        value = act[PAD * z : PAD * z + PAD] * jnp.where(pre > 0, 1.0, LEAK)
        act_s[PAD * (z + 1) : PAD * (z + 2), :] = jnp.where(inside, value, 0.0).astype(BF16)

    for kz in range(3):
        first_s[kz] = dot(ins_ref[...], planes(act_s, kz, 0, 256))

    cells = 16 * 8 * 16 * 512
    scale = cells**-0.5
    lane = iota((16, 128), 1)
    for kz in range(3):
        for ky in range(3):
            for kx in range(3):
                total = jnp.zeros((16, 128), F32)
                for y in range(16):
                    at = y + ky - 1
                    if 0 <= at < 16:
                        slot = (y + 1) % 16
                        half = slot // 8
                        row = 48 * ((at + 2) % 16 if half == 0 else at - 6) + 16 * kx
                        col = 128 * (slot % 8 // 4)
                        piece = terms_s[kz, half, row : row + 16, col : col + 128]
                        total = total + jnp.where(lane // 32 == slot % 4, piece, 0.0)
                total = total + pltpu.roll(total, 64, 1)
                total = (total + pltpu.roll(total, 32, 1)) * scale
                tap = 9 * kz + 3 * ky + kx
                at = 16 * (tap // 4)
                if tap % 4 == 0:
                    sums_s[at : at + 16, :] = total
                else:
                    sums_s[at : at + 16, :] = jnp.where(lane // 32 == tap % 4, total, sums_s[at : at + 16, :])

    packed = jnp.zeros((16, 128), F32)
    for kz in range(3):
        for ky in range(3):
            total = jnp.zeros((16, 128), F32)
            for y in range(16):
                at = y + ky - 1
                if 0 <= at < 16:
                    piece = first_s[kz, 16 * at : 16 * at + 16, 128 * (y // 8) : 128 * (y // 8) + 128]
                    total = total + jnp.where(lane // 16 == y % 8, piece, 0.0)
            for by in (64, 32, 16):
                total = total + pltpu.roll(total, by, 1)
            total = total * scale
            if 3 * kz + ky < 8:
                packed = jnp.where(lane // 16 == 3 * kz + ky, total, packed)
            else:
                sums_s[96:112, :] = jnp.where(lane // 32 == 3, total, sums_s[96:112, :])
    sums_s[112:128, :] = packed
    first = lax.rem(lax.axis_index("dp"), 2) == 0
    mine_ref[...] = jnp.where(first, sums_s[:64, :], sums_s[64:, :])
    rest_ref[...] = jnp.where(first, sums_s[64:, :], sums_s[:64, :])


def back_kernel(act_s, one_ref, own_ref, give_ref, out_s, thin_ref):
    band_one(one_ref, thin_ref)
    left = lax.rem(lax.axis_index("space"), 2) == 0
    sides = jnp.concatenate([planes(act_s, kz, 0, 256) for kz in range(3)], axis=1)
    out_s[...] = across(dot(sides, thin_ref[...]))
    row, col = iota((64, 128), 0), iota((64, 128), 1)
    eye = one_hot(jnp.where(left, row, (row + 32) % 64) == col)
    for z in range(4):
        pair = jnp.concatenate([out_s[PAD * z : PAD * z + STRIP], out_s[PAD * (z + 4) : PAD * (z + 4) + STRIP]], axis=0)
        pair = dot_t(eye, pair.astype(BF16))
        own_ref[z] = pair[:32].astype(BF16)
        give_ref[z] = pair[32:].astype(BF16)


def tile_kernel(own_ref, recv_ref, out_ref):
    left = lax.rem(lax.axis_index("space"), 2) == 0
    low_lanes = iota((32, 128), 1) < STRIP
    for z in range(4):
        own, recv = own_ref[z].astype(F32), recv_ref[z].astype(F32)
        a, b = jnp.where(left, own, recv), jnp.where(left, recv, own)
        near = jnp.where(low_lanes, a, pltpu.roll(b, STRIP, 1))
        far = jnp.where(low_lanes, pltpu.roll(a, STRIP, 1), b)
        out_ref[:, z] = near.reshape(4, 8, 128).astype(BF16)
        out_ref[:, z + 4] = far.reshape(4, 8, 128).astype(BF16)


def unpack_kernel(mine_ref, rest_ref, one_ref, two_ref, flat_ref):
    first = lax.rem(lax.axis_index("dp"), 2) == 0
    mine, rest = mine_ref[...], rest_ref[...]
    low, high = jnp.where(first, mine, rest), jnp.where(first, rest, mine)
    blocks = [low[16 * q : 16 * q + 16] for q in range(4)] + [high[16 * q : 16 * q + 16] for q in range(4)]
    for pair in range(9):
        source, lane = (blocks[7], 16 * pair) if pair < 8 else (blocks[6], 96)
        source = pltpu.roll(source, 128 - lane, 1) if lane else source
        for kx in range(3):
            flat_ref[pl.ds(3 * pair + kx, 4, stride=32), :] = source[4 * kx : 4 * kx + 4]
    for k in range(27):
        two_ref[k] = blocks[k // 4][:, 32 * (k % 4) : 32 * (k % 4) + 32]
    turned = flat_ref[...].T
    for c in range(4):
        one_ref[c] = turned[:16, 32 * c : 32 * c + 27]


def routes():
    def number(zh, x, core, y, zl):
        return ((zh * 4 + x) * 2 + core) * 8 + y * 2 + zl

    every = list(itertools.product(range(2), range(4), range(2), range(4), range(2)))
    cores = [(number(*d), number(d[0], d[1], 1 - d[2], d[3], d[4])) for d in every]
    along_x = [[(number(*d), number(d[0], d[1] ^ j, *d[2:])) for d in every] for j in (1, 3, 2)]
    along_y = [[(number(*d), number(*d[:3], d[3] ^ j, d[4])) for d in every] for j in (1, 3, 2)]
    along_z = []
    for j in (1, 3, 2):
        pairs = []
        for d in every:
            z = (2 * d[0] + d[4]) ^ j
            pairs.append((number(*d), number(z // 2, d[1], d[2], d[3], z % 2)))
        along_z.append(pairs)
    return cores, [along_x, along_y, along_z]


def body(inputs, pre_act, out_grad, conv1_weight, conv2_weight):
    shape = jax.ShapeDtypeStruct
    cores, stages = routes()
    keep, send, strips = call(
        cut_kernel, "cut",
        [shape((10, WIDE, 128), BF16), shape((10, WIDE, 128), BF16), shape((8, WIDE, 512), BF16)],
        [
            pltpu.VMEM((4, 32, 16, 128), BF16), pltpu.VMEM((8, 16, 8, 128), BF16), pltpu.VMEM((4, 8, 8, 128), BF16),
            pltpu.VMEM((10, WIDE, 128), BF16), pltpu.VMEM((10, WIDE, 128), BF16), pltpu.VMEM((8, WIDE, 512), BF16),
            pltpu.VMEM((4, 512, 128), F32), pltpu.VMEM((512, 512), BF16),
            pltpu.SemaphoreType.DMA((13,)), pltpu.SemaphoreType.DMA((10,)),
        ],
        [out_grad[0, 0], pre_act[0, 0], inputs[0, 0]], 4e8, 2e6, limit=FULL, far_args=(0, 1, 2), far_outs=(0, 1, 2),
    )
    swap = [(i, i ^ 1) for i in range(8)]
    recv = lax.ppermute(send, "space", swap)
    strips = lax.all_to_all(strips, "space", 0, 0, tiled=True)
    pre, hid, ins, wide = call(
        ready_kernel, "ready",
        [
            shape((8, PAD, 256), BF16), shape((864, ROWS), BF16), shape((256, ROWS), BF16),
            shape((768, 256), BF16),
        ],
        [pltpu.VMEM((ROWS, 256), F32), pltpu.VMEM((ROWS, 128), F32), pltpu.VMEM((256, ROWS), F32)],
        [keep, recv, conv2_weight.transpose(0, 2, 1).reshape(864, 16)],
        2e10, 5e6, limit=SOME,
    )
    act, mine, rest = call(
        grads_kernel, "grads",
        [shape((10 * PAD, 256), BF16), shape((64, 128), F32), shape((64, 128), F32)],
        [
            pltpu.VMEM((10 * PAD, 512), BF16), pltpu.VMEM((3, 2, 480, 256), F32), pltpu.VMEM((3, 256, 256), F32),
            pltpu.VMEM((128, 128), F32), pltpu.VMEM((4, ROWS, 256), F32),
        ],
        [strips, pre, hid, ins, wide], 3e9, 4e6, limit=SOME,
    )
    own, give = call(
        back_kernel, "back", [shape((4, 32, 128), BF16), shape((4, 32, 128), BF16)], [pltpu.VMEM((ROWS, 128), F32), pltpu.VMEM((768, 256), BF16)],
        [act, conv1_weight.transpose(0, 2, 1).reshape(432, 4)], 5e8, 1e6,
    )
    total = mine + lax.ppermute(rest, ALL, cores)
    got = lax.ppermute(give, "space", swap)
    for stage in stages:
        parts = [lax.ppermute(total, ALL, pairs) for pairs in stage]
        total = (total + parts[0]) + (parts[1] + parts[2])
    other = lax.ppermute(total, ALL, cores)
    (input_grad,) = call(tile_kernel, "tile", [shape((4, 8, 8, 128), BF16)], [], [own, got], 1e6, 2e5)
    first, second = call(
        unpack_kernel, "unpack", [shape((4, 16, 27), F32), shape((27, 16, 32), F32)], [pltpu.VMEM((128, 128), F32)],
        [total, other], 1e6, 2e5,
    )
    return input_grad[None, None], first.transpose(2, 0, 1), second


def solution(mesh):
    placed = (
        P("dp", "space", None, None, None, None),
        P("dp", "space", None, None, None, None),
        P("dp", "space", None, None, None),
        P(),
        P(),
    )
    return jax.shard_map(
        body,
        mesh=mesh,
        in_specs=placed,
        out_specs=(P("dp", "space", None, None, None, None), P(), P()),
        check_vma=False,
    )
```

```python
import itertools

import jax
import jax.numpy as jnp
from jax import lax
from jax.experimental import pallas as pl
from jax.experimental.pallas import tpu as pltpu
from jax.sharding import PartitionSpec as P

LEAK = 0.3
STRIP = 64
WIDE = 72
PAD = 80
ROWS = 8 * PAD
FULL = 62
SOME = 20
ALL = ("dp", "space")
F32 = jnp.float32
BF16 = jnp.bfloat16


def iota(shape, dim):
    return lax.broadcasted_iota(jnp.int32, shape, dim)


def one_hot(flags):
    return jnp.where(flags, 1.0, 0.0).astype(BF16)


def dot(a, b):
    return jnp.dot(a, b, preferred_element_type=F32)


def dot_t(a, b):
    return lax.dot_general(a, b, (((1,), (1,)), ((), ())), preferred_element_type=F32)


def call(kernel, name, outs, scratch, args, flops, size, limit=10, far_args=(), far_outs=()):
    def spec(far):
        return pl.BlockSpec(memory_space=pltpu.HBM if far else pltpu.VMEM)

    return pl.pallas_call(
        kernel,
        name=name,
        out_shape=outs,
        in_specs=[spec(i in far_args) for i in range(len(args))],
        out_specs=[spec(i in far_outs) for i in range(len(outs))],
        scratch_shapes=scratch,
        compiler_params=pltpu.CompilerParams(vmem_limit_bytes=limit << 20),
        cost_estimate=pl.CostEstimate(flops=int(flops), bytes_accessed=int(size), transcendentals=0),
    )(*args)


def row_major():
    src, dst = iota((128, 128), 0), iota((128, 128), 1)
    return one_hot((src // 8 == dst % 16) & (src % 8 == dst // 16))


def cut_kernel(
    slab_hbm, pre_hbm, in_hbm, keep_hbm, send_hbm, out_hbm,
    slab_ref, pre_ref, in_ref, keep_ref, send_ref, out_ref, wide_ref, turned_ref, sems, done,
):
    copies = [pltpu.make_async_copy(in_hbm, in_ref, sems.at[0])]
    copies += [
        pltpu.make_async_copy(pre_hbm.at[pl.ds(4 * i, 4)], pre_ref.at[pl.ds(4 * i, 4)], sems.at[5 + i]) for i in range(4)
    ]
    copies += [
        pltpu.make_async_copy(slab_hbm.at[pl.ds(8 * b, 8)], slab_ref.at[pl.ds(8 * b, 8)], sems.at[1 + b]) for b in range(4)
    ]
    for copy in copies:
        copy.start()
    r = lax.rem(lax.axis_index("space"), 2)
    a, x = iota((WIDE, 128), 0), iota((WIDE, 128), 1)
    src, dst = iota((256, 256), 0), iota((256, 256), 1)
    same = one_hot((src // 64 == dst % 4) & (src // 8 % 8 == dst // 32) & (src % 8 == dst // 4 % 8))
    order = row_major()
    gap = jnp.where(a < STRIP, x - a, -9999)
    pick = jnp.concatenate(
        [jnp.where(gap == STRIP * r, 1.0, 0.0), jnp.where(gap == STRIP * (1 - r), 1.0, 0.0)], axis=0
    ).astype(BF16)
    copies[0].wait()
    rows = in_ref[...].astype(F32).reshape(256, 128).astype(BF16)
    got = dot(dot_t(pick, rows).astype(BF16), same)
    for half in range(2):
        keep_ref[8 + half] = got[:WIDE, 128 * half : 128 * half + 128].astype(BF16)
        send_ref[8 + half] = got[WIDE:, 128 * half : 128 * half + 128].astype(BF16)
    gap = jnp.where(a < STRIP + 2, x - a, -9999)
    end = iota((16, 128), 0)
    pick = jnp.concatenate(
        [
            jnp.where(gap == STRIP * r - 1, 1.0, 0.0),
            jnp.where(gap == STRIP * (1 - r) - 1, 1.0, 0.0),
            jnp.where(iota((16, 128), 1) == jnp.where(end == 0, 127, jnp.where(end == 8, 0, -1)), 1.0, 0.0),
        ],
        axis=0,
    ).astype(BF16)
    for copy in copies[1:5]:
        copy.wait()
    planes = [pre_ref[:, z].astype(F32).reshape(128, 128) for z in range(8)]
    got = dot_t(pick, jnp.concatenate(planes, axis=0).astype(BF16)).astype(BF16)
    got = dot(jnp.concatenate([got[:, 128 * z : 128 * z + 128] for z in range(8)], axis=0), order)
    edges = [jnp.zeros((8, 128), F32)] * 2
    for z in range(8):
        at = 160 * z
        keep_ref[z] = got[at : at + WIDE].astype(BF16)
        send_ref[z] = got[at + WIDE : at + 2 * WIDE].astype(BF16)
        for i in range(2):
            edges[i] = jnp.where(iota((8, 128), 0) == z, got[at + 144 + 8 * i : at + 145 + 8 * i], edges[i])
    results = [
        pltpu.make_async_copy(send_ref, send_hbm, done.at[8]), pltpu.make_async_copy(keep_ref, keep_hbm, done.at[9])
    ]
    for copy in results:
        copy.start()

    for copy in copies[5:]:
        copy.wait()
    for b in range(4):
        wide_ref[b] = slab_ref[:, :, 128 * b : 128 * b + 128].astype(F32).reshape(512, 128)
        for y in range(16):
            slot = (y + 1) % 16
            turned_ref[32 * slot : 32 * slot + 32, 128 * b : 128 * b + 128] = wide_ref[
                b, pl.ds(y, 32, stride=16), :
            ].astype(BF16)
    p, x = iota((WIDE, 512), 0), iota((WIDE, 512), 1)
    gap = jnp.where(p < STRIP + 4, x - p, -9999)
    late = iota((8, 128), 0) >= 4
    for pair in range(2):
        strips = [jnp.where(gap == STRIP * t - 2, 1.0, 0.0) for t in range(4 * pair, 4 * pair + 4)]
        cut = dot_t(jnp.concatenate(strips, axis=0).astype(BF16), turned_ref[...])
        for i in range(4):
            t = 4 * pair + i
            out_ref[t, :STRIP] = cut[WIDE * i : WIDE * i + STRIP].astype(BF16)
            last = cut[WIDE * i + STRIP : WIDE * i + WIDE]
            edge = edges[t % 2]
            last = jnp.concatenate(
                [
                    jnp.where(late, pltpu.roll(edge, 4, 0), last[:, :128]),
                    jnp.where(late, edge, last[:, 128:256]),
                    last[:, 256:],
                ],
                axis=1,
            )
            out_ref[t, STRIP:] = last.astype(BF16)
            results.append(pltpu.make_async_copy(out_ref.at[t], out_hbm.at[t], done.at[t]))
            results[-1].start()
    for copy in results:
        copy.wait()


def join(keep_ref, recv_ref, pre_ref, hid_ref, ins_ref, wide_ref, thin_ref, rows_ref):
    r = lax.rem(lax.axis_index("space"), 2)
    left = r == 0
    lane = iota((PAD, 128), 1)
    tail = jnp.zeros((PAD - WIDE, 128), F32)
    own = (iota((PAD, 128), 0) >= 1) & (iota((PAD, 128), 0) <= STRIP)
    for z in range(8):
        mine = jnp.concatenate([keep_ref[z].astype(F32), tail], axis=0)
        other = jnp.concatenate([recv_ref[z].astype(F32), tail], axis=0)
        for part in range(2):
            value = jnp.where(left, mine, other) if part == 0 else jnp.where(left, other, mine)
            pre_ref[z, :, 128 * part : 128 * part + 128] = value.astype(BF16)
            hidden = jnp.where(value > 0, value, LEAK * value)
            wide_ref[PAD * z : PAD * z + PAD, 128 * part : 128 * part + 128] = jnp.where(own, hidden, 0.0)
        mine = jnp.concatenate([keep_ref[8 + z // 4].astype(F32), tail], axis=0)
        other = jnp.concatenate([recv_ref[8 + z // 4].astype(F32), tail], axis=0)
        low, high = jnp.where(left, mine, other), jnp.where(left, other, mine)
        low = pltpu.roll(low, (128 - 32 * (z % 4)) % 128, 1)
        high = pltpu.roll(high, (160 - 32 * (z % 4)) % 128, 1)
        value = jnp.where(lane < 32, low, jnp.where(lane < 64, high, 0.0))
        thin_ref[PAD * z : PAD * z + PAD, :] = value
    for part in range(2):
        turned = wide_ref[:, 128 * part : 128 * part + 128].T
        for kx in range(3):
            shifted = pltpu.roll(turned, 2 - kx, 1) if kx < 2 else turned
            for y in range(8 * part, 8 * part + 8):
                rows = shifted[16 * (y % 8) : 16 * (y % 8) + 16].astype(BF16)
                for slot in {(y + 2) % 16, y + 2}:
                    hid_ref[48 * slot + 16 * kx : 48 * slot + 16 * kx + 16, :] = rows
    turned = thin_ref[...].T[:64]
    rows_ref[...] = jnp.zeros((256, ROWS), F32)
    for kx in range(3):
        shifted = pltpu.roll(turned, 2 - kx, 1) if kx < 2 else turned
        for y in range(16):
            rows_ref[16 * y + 4 * kx : 16 * y + 4 * kx + 4, :] = shifted[4 * y : 4 * y + 4]
    ins_ref[...] = rows_ref[...].astype(BF16)


def lay(terms, rows, kz, ky):
    parts = [terms[rows * (9 * kz + 3 * ky + kx) :][:rows] for kx in range(3)]
    return jnp.where(iota((rows, 128), 1) < 64, parts[0], parts[1]), parts[2]


def band_two(two_ref, wide_ref):
    two = dot(two_ref[...], one_hot(iota((16, 128), 1) % 16 == iota((16, 128), 0)))
    group = iota((32, 128), 1) // 16 % 4
    for kz in range(3):
        terms = [lay(two, 32, kz, ky) for ky in range(3)]
        for slot in range(8):
            for half in range(2):
                block = jnp.zeros((32, 128), F32)
                for ky in range(3):
                    block = jnp.where(group == ky + slot - 2, terms[ky][half], block)
                at = 256 * kz + 32 * slot
                wide_ref[at : at + 32, 128 * half : 128 * half + 128] = block.astype(BF16)


def band_one(one_ref, thin_ref):
    one = dot(one_ref[...], one_hot(iota((4, 128), 1) // 8 % 4 == iota((4, 128), 0)))
    lane = iota((16, 128), 1)
    group = 8 * (lane // 32 % 2) + lane % 8
    for kz in range(3):
        terms = [lay(one, 16, kz, ky) for ky in range(3)]
        for y in range(16):
            for half in range(2):
                block = jnp.zeros((16, 128), F32)
                for ky in range(3):
                    block = jnp.where(group == y + ky - 1, terms[ky][half], block)
                at = 256 * kz + 16 * y
                thin_ref[at : at + 16, 128 * half : 128 * half + 128] = block.astype(BF16)


def ready_kernel(
    keep_ref, recv_ref, two_ref, pre_ref, hid_ref, ins_ref, wide_ref, hidden_ref, inputs_ref, rows_ref
):
    band_two(two_ref, wide_ref)
    join(keep_ref, recv_ref, pre_ref, hid_ref, ins_ref, hidden_ref, inputs_ref, rows_ref)


def planes(ref, kz, low, size):
    return ref[(2 - kz) * PAD : (2 - kz) * PAD + ROWS, low : low + size]


def across(sums):
    pair = sums[:, :128]
    pair = jnp.where(iota((ROWS, 128), 1) < 64, pltpu.roll(pair, ROWS - 2, 0), pltpu.roll(pair, ROWS - 1, 0))
    return pair + pltpu.roll(pair, 64, 1) + sums[:, 128:]


def grads_kernel(
    grad_ref, pre_ref, hid_ref, ins_ref, wide_ref,
    act_s, mine_ref, rest_ref, grad_s, terms_s, first_s, sums_s, raw_s,
):
    space = lax.axis_index("space")
    left = lax.rem(space, 2) == 0
    for block in (0, 9):
        grad_s[PAD * block : PAD * block + PAD, :] = jnp.zeros((PAD, 512), BF16)
        act_s[PAD * block : PAD * block + PAD, :] = jnp.zeros((PAD, 256), BF16)
    for z in range(8):
        at = PAD * (z + 1)
        grad_s[at : at + STRIP, :] = grad_ref[z, :STRIP]
        last = jnp.concatenate([grad_ref[z, STRIP:].astype(F32), jnp.zeros((PAD - WIDE, 512), F32)], axis=0)
        grad_s[at + STRIP : at + PAD, :] = last.astype(BF16)

    wide = [wide_ref[256 * kz : 256 * kz + 256, :] for kz in range(3)]
    none = jnp.zeros((32, 256), BF16)
    top = jnp.concatenate([part for w in wide for part in (none, w[32:])], axis=0)
    bottom = jnp.concatenate([part for w in wide for part in (w[:160], none, w[192:])], axis=0)
    for group in range(4):
        if group < 3:
            sides = [planes(grad_s, kz, 128 * group, 256) for kz in range(3)]
        else:
            sides = [planes(grad_s, kz, low, 128) for kz in range(3) for low in (384, 0)]
        weights = top if group == 0 else bottom if group == 3 else wide_ref[...]
        raw_s[group] = dot(jnp.concatenate(sides, axis=1), weights)
    for kz in range(3):
        for half in range(2):
            terms_s[kz, half] = dot(hid_ref[384 * half : 384 * half + 480, :], planes(grad_s, kz, 256 * half, 256))
    parts = [across(raw_s[group]) for group in range(4)]
    low = iota((ROWS, 128), 1) < 64
    act = jnp.concatenate([jnp.where(low, parts[0], parts[1]), jnp.where(low, parts[2], parts[3])], axis=1)
    row = iota((PAD, 256), 0)
    at = STRIP * space - 1 + row
    inside = (row < STRIP + 2) & (at >= 0) & (at < 512)
    edge_row = row == jnp.where(left, 0, STRIP + 1)
    side = jnp.clip(space // 2 * 2 + jnp.where(left, -2, 2), 0, 6)
    edges = [grad_ref[side + r, STRIP:, :256].astype(F32) for r in range(2)]
    for z in range(8):
        beside = [edges[r][4 + z % 4 : 5 + z % 4, 128 * (z // 4) : 128 * (z // 4) + 128] for r in range(2)]
        pre = jnp.where(edge_row, jnp.concatenate(beside, axis=1), pre_ref[z].astype(F32))
        value = act[PAD * z : PAD * z + PAD] * jnp.where(pre > 0, 1.0, LEAK)
        act_s[PAD * (z + 1) : PAD * (z + 2), :] = jnp.where(inside, value, 0.0).astype(BF16)

    for kz in range(3):
        first_s[kz] = dot(ins_ref[...], planes(act_s, kz, 0, 256))

    cells = 16 * 8 * 16 * 512
    scale = cells**-0.5
    lane = iota((16, 128), 1)
    for kz in range(3):
        for ky in range(3):
            for kx in range(3):
                total = jnp.zeros((16, 128), F32)
                for y in range(16):
                    at = y + ky - 1
                    if 0 <= at < 16:
                        slot = (y + 1) % 16
                        half = slot // 8
                        row = 48 * ((at + 2) % 16 if half == 0 else at - 6) + 16 * kx
                        col = 128 * (slot % 8 // 4)
                        piece = terms_s[kz, half, row : row + 16, col : col + 128]
                        total = total + jnp.where(lane // 32 == slot % 4, piece, 0.0)
                total = total + pltpu.roll(total, 64, 1)
                total = (total + pltpu.roll(total, 32, 1)) * scale
                tap = 9 * kz + 3 * ky + kx
                at = 16 * (tap // 4)
                if tap % 4 == 0:
                    sums_s[at : at + 16, :] = total
                else:
                    sums_s[at : at + 16, :] = jnp.where(lane // 32 == tap % 4, total, sums_s[at : at + 16, :])

    packed = jnp.zeros((16, 128), F32)
    for kz in range(3):
        for ky in range(3):
            total = jnp.zeros((16, 128), F32)
            for y in range(16):
                at = y + ky - 1
                if 0 <= at < 16:
                    piece = first_s[kz, 16 * at : 16 * at + 16, 128 * (y // 8) : 128 * (y // 8) + 128]
                    total = total + jnp.where(lane // 16 == y % 8, piece, 0.0)
            for by in (64, 32, 16):
                total = total + pltpu.roll(total, by, 1)
            total = total * scale
            if 3 * kz + ky < 8:
                packed = jnp.where(lane // 16 == 3 * kz + ky, total, packed)
            else:
                sums_s[96:112, :] = jnp.where(lane // 32 == 3, total, sums_s[96:112, :])
    sums_s[112:128, :] = packed
    first = lax.rem(lax.axis_index("dp"), 2) == 0
    mine_ref[...] = jnp.where(first, sums_s[:64, :], sums_s[64:, :])
    rest_ref[...] = jnp.where(first, sums_s[64:, :], sums_s[:64, :])


def back_kernel(act_s, one_ref, own_ref, give_ref, out_s, thin_ref):
    band_one(one_ref, thin_ref)
    left = lax.rem(lax.axis_index("space"), 2) == 0
    sides = jnp.concatenate([planes(act_s, kz, 0, 256) for kz in range(3)], axis=1)
    out_s[...] = across(dot(sides, thin_ref[...]))
    row, col = iota((64, 128), 0), iota((64, 128), 1)
    eye = one_hot(jnp.where(left, row, (row + 32) % 64) == col)
    for z in range(4):
        pair = jnp.concatenate([out_s[PAD * z : PAD * z + STRIP], out_s[PAD * (z + 4) : PAD * (z + 4) + STRIP]], axis=0)
        pair = dot_t(eye, pair.astype(BF16))
        own_ref[z] = pair[:32].astype(BF16)
        give_ref[z] = pair[32:].astype(BF16)


def tile_kernel(own_ref, recv_ref, out_ref):
    left = lax.rem(lax.axis_index("space"), 2) == 0
    low_lanes = iota((32, 128), 1) < STRIP
    for z in range(4):
        own, recv = own_ref[z].astype(F32), recv_ref[z].astype(F32)
        a, b = jnp.where(left, own, recv), jnp.where(left, recv, own)
        near = jnp.where(low_lanes, a, pltpu.roll(b, STRIP, 1))
        far = jnp.where(low_lanes, pltpu.roll(a, STRIP, 1), b)
        out_ref[:, z] = near.reshape(4, 8, 128).astype(BF16)
        out_ref[:, z + 4] = far.reshape(4, 8, 128).astype(BF16)


def unpack_kernel(mine_ref, rest_ref, one_hbm, two_hbm, one_ref, two_ref, flat_ref, sems):
    first = lax.rem(lax.axis_index("dp"), 2) == 0
    mine, rest = mine_ref[...], rest_ref[...]
    low, high = jnp.where(first, mine, rest), jnp.where(first, rest, mine)
    blocks = [low[16 * q : 16 * q + 16] for q in range(4)] + [high[16 * q : 16 * q + 16] for q in range(4)]
    copies = []
    for q in range(3):
        for k in range(9 * q, 9 * q + 9):
            two_ref[k] = blocks[k // 4][:, 32 * (k % 4) : 32 * (k % 4) + 32]
        copies.append(pltpu.make_async_copy(two_ref.at[pl.ds(9 * q, 9)], two_hbm.at[pl.ds(9 * q, 9)], sems.at[q]))
        copies[-1].start()
    for pair in range(9):
        source, lane = (blocks[7], 16 * pair) if pair < 8 else (blocks[6], 96)
        source = pltpu.roll(source, 128 - lane, 1) if lane else source
        for kx in range(3):
            flat_ref[pl.ds(3 * pair + kx, 4, stride=32), :] = source[4 * kx : 4 * kx + 4]
    turned = flat_ref[...].T
    for c in range(4):
        one_ref[c] = turned[:16, 32 * c : 32 * c + 27]
    copies.append(pltpu.make_async_copy(one_ref, one_hbm, sems.at[3]))
    copies[-1].start()
    for copy in copies:
        copy.wait()


def routes():
    def number(zh, x, core, y, zl):
        return ((zh * 4 + x) * 2 + core) * 8 + y * 2 + zl

    every = list(itertools.product(range(2), range(4), range(2), range(4), range(2)))
    cores = [(number(*d), number(d[0], d[1], 1 - d[2], d[3], d[4])) for d in every]
    along_x = [[(number(*d), number(d[0], d[1] ^ j, *d[2:])) for d in every] for j in (1, 3, 2)]
    along_y = [[(number(*d), number(*d[:3], d[3] ^ j, d[4])) for d in every] for j in (1, 3, 2)]
    along_z = []
    for j in (1, 3, 2):
        pairs = []
        for d in every:
            z = (2 * d[0] + d[4]) ^ j
            pairs.append((number(*d), number(z // 2, d[1], d[2], d[3], z % 2)))
        along_z.append(pairs)
    return cores, [along_x, along_y, along_z]


def body(inputs, pre_act, out_grad, conv1_weight, conv2_weight):
    shape = jax.ShapeDtypeStruct
    cores, stages = routes()
    keep, send, strips = call(
        cut_kernel, "cut",
        [shape((10, WIDE, 128), BF16), shape((10, WIDE, 128), BF16), shape((8, WIDE, 512), BF16)],
        [
            pltpu.VMEM((32, 16, 512), BF16), pltpu.VMEM((16, 8, 8, 128), BF16), pltpu.VMEM((4, 8, 8, 128), BF16),
            pltpu.VMEM((10, WIDE, 128), BF16), pltpu.VMEM((10, WIDE, 128), BF16), pltpu.VMEM((8, WIDE, 512), BF16),
            pltpu.VMEM((4, 512, 128), F32), pltpu.VMEM((512, 512), BF16),
            pltpu.SemaphoreType.DMA((9,)), pltpu.SemaphoreType.DMA((10,)),
        ],
        [out_grad[0, 0], pre_act[0, 0], inputs[0, 0]], 4e8, 2e6, limit=FULL, far_args=(0, 1, 2), far_outs=(0, 1, 2),
    )
    swap = [(i, i ^ 1) for i in range(8)]
    recv = lax.ppermute(send, "space", swap)
    strips = lax.all_to_all(strips, "space", 0, 0, tiled=True)
    pre, hid, ins, wide = call(
        ready_kernel, "ready",
        [
            shape((8, PAD, 256), BF16), shape((864, ROWS), BF16), shape((256, ROWS), BF16),
            shape((768, 256), BF16),
        ],
        [pltpu.VMEM((ROWS, 256), F32), pltpu.VMEM((ROWS, 128), F32), pltpu.VMEM((256, ROWS), F32)],
        [keep, recv, conv2_weight.transpose(0, 2, 1).reshape(864, 16)],
        2e10, 5e6, limit=SOME,
    )
    act, mine, rest = call(
        grads_kernel, "grads",
        [shape((10 * PAD, 256), BF16), shape((64, 128), F32), shape((64, 128), F32)],
        [
            pltpu.VMEM((10 * PAD, 512), BF16), pltpu.VMEM((3, 2, 480, 256), F32), pltpu.VMEM((3, 256, 256), F32),
            pltpu.VMEM((128, 128), F32), pltpu.VMEM((4, ROWS, 256), F32),
        ],
        [strips, pre, hid, ins, wide], 3e9, 4e6, limit=SOME,
    )
    own, give = call(
        back_kernel, "back", [shape((4, 32, 128), BF16), shape((4, 32, 128), BF16)], [pltpu.VMEM((ROWS, 128), F32), pltpu.VMEM((768, 256), BF16)],
        [act, conv1_weight.transpose(0, 2, 1).reshape(432, 4)], 5e8, 1e6,
    )
    total = mine + lax.ppermute(rest, ALL, cores)
    got = lax.ppermute(give, "space", swap)
    for stage in stages:
        parts = [lax.ppermute(total, ALL, pairs) for pairs in stage]
        total = (total + parts[0]) + (parts[1] + parts[2])
    other = lax.ppermute(total, ALL, cores)
    (input_grad,) = call(tile_kernel, "tile", [shape((4, 8, 8, 128), BF16)], [], [own, got], 1e6, 2e5)
    first, second = call(
        unpack_kernel, "unpack", [shape((4, 16, 27), F32), shape((27, 16, 32), F32)],
        [
            pltpu.VMEM((4, 16, 27), F32), pltpu.VMEM((27, 16, 32), F32), pltpu.VMEM((128, 128), F32),
            pltpu.SemaphoreType.DMA((4,)),
        ],
        [total, other], 1e6, 2e5, far_outs=(0, 1),
    )
    return input_grad[None, None], first.transpose(2, 0, 1), second


def solution(mesh):
    placed = (
        P("dp", "space", None, None, None, None),
        P("dp", "space", None, None, None, None),
        P("dp", "space", None, None, None),
        P(),
        P(),
    )
    return jax.shard_map(
        body,
        mesh=mesh,
        in_specs=placed,
        out_specs=(P("dp", "space", None, None, None, None), P(), P()),
        check_vma=False,
    )
```

```python
import itertools

import jax
import jax.numpy as jnp
from jax import lax
from jax.experimental import pallas as pl
from jax.experimental.pallas import tpu as pltpu
from jax.sharding import PartitionSpec as P

LEAK = 0.3
STRIP = 64
WIDE = 72
PAD = 80
ROWS = 8 * PAD
FULL = 62
SOME = 20
ALL = ("dp", "space")
F32 = jnp.float32
BF16 = jnp.bfloat16


def iota(shape, dim):
    return lax.broadcasted_iota(jnp.int32, shape, dim)


def one_hot(flags):
    return jnp.where(flags, 1.0, 0.0).astype(BF16)


def dot(a, b):
    return jnp.dot(a, b, preferred_element_type=F32)


def dot_t(a, b):
    return lax.dot_general(a, b, (((1,), (1,)), ((), ())), preferred_element_type=F32)


def call(kernel, name, outs, scratch, args, flops, size, limit=10, far_args=(), far_outs=()):
    def spec(far):
        return pl.BlockSpec(memory_space=pltpu.HBM if far else pltpu.VMEM)

    return pl.pallas_call(
        kernel,
        name=name,
        out_shape=outs,
        in_specs=[spec(i in far_args) for i in range(len(args))],
        out_specs=[spec(i in far_outs) for i in range(len(outs))],
        scratch_shapes=scratch,
        compiler_params=pltpu.CompilerParams(vmem_limit_bytes=limit << 20),
        cost_estimate=pl.CostEstimate(flops=int(flops), bytes_accessed=int(size), transcendentals=0),
    )(*args)


def row_major():
    src, dst = iota((128, 128), 0), iota((128, 128), 1)
    return one_hot((src // 8 == dst % 16) & (src % 8 == dst // 16))


def cut_kernel(
    slab_hbm, pre_hbm, in_hbm, keep_hbm, send_hbm, out_hbm,
    slab_ref, pre_ref, in_ref, keep_ref, send_ref, out_ref, wide_ref, turned_ref, sems, done,
):
    copies = [pltpu.make_async_copy(in_hbm, in_ref, sems.at[0])]
    copies += [
        pltpu.make_async_copy(pre_hbm.at[:, z], pre_ref.at[z], sems.at[5 + z]) for z in range(8)
    ]
    copies += [
        pltpu.make_async_copy(slab_hbm.at[:, :, pl.ds(128 * b, 128)], slab_ref.at[b], sems.at[1 + b]) for b in range(4)
    ]
    for copy in copies:
        copy.start()
    r = lax.rem(lax.axis_index("space"), 2)
    a, x = iota((WIDE, 128), 0), iota((WIDE, 128), 1)
    src, dst = iota((256, 256), 0), iota((256, 256), 1)
    same = one_hot((src // 64 == dst % 4) & (src // 8 % 8 == dst // 32) & (src % 8 == dst // 4 % 8))
    order = row_major()
    gap = jnp.where(a < STRIP, x - a, -9999)
    pick = jnp.concatenate(
        [jnp.where(gap == STRIP * r, 1.0, 0.0), jnp.where(gap == STRIP * (1 - r), 1.0, 0.0)], axis=0
    ).astype(BF16)
    copies[0].wait()
    rows = in_ref[...].astype(F32).reshape(256, 128).astype(BF16)
    got = dot(dot_t(pick, rows).astype(BF16), same)
    for half in range(2):
        keep_ref[8 + half] = got[:WIDE, 128 * half : 128 * half + 128].astype(BF16)
        send_ref[8 + half] = got[WIDE:, 128 * half : 128 * half + 128].astype(BF16)
    gap = jnp.where(a < STRIP + 2, x - a, -9999)
    end = iota((16, 128), 0)
    pick = jnp.concatenate(
        [
            jnp.where(gap == STRIP * r - 1, 1.0, 0.0),
            jnp.where(gap == STRIP * (1 - r) - 1, 1.0, 0.0),
            jnp.where(iota((16, 128), 1) == jnp.where(end == 0, 127, jnp.where(end == 8, 0, -1)), 1.0, 0.0),
        ],
        axis=0,
    ).astype(BF16)
    for copy in copies[1:9]:
        copy.wait()
    got = dot_t(pick, pre_ref[...].astype(F32).reshape(1024, 128).astype(BF16)).astype(BF16)
    got = dot(jnp.concatenate([got[:, 128 * z : 128 * z + 128] for z in range(8)], axis=0), order)
    edges = [jnp.zeros((8, 128), F32)] * 2
    for z in range(8):
        at = 160 * z
        keep_ref[z] = got[at : at + WIDE].astype(BF16)
        send_ref[z] = got[at + WIDE : at + 2 * WIDE].astype(BF16)
        for i in range(2):
            edges[i] = jnp.where(iota((8, 128), 0) == z, got[at + 144 + 8 * i : at + 145 + 8 * i], edges[i])
    results = [
        pltpu.make_async_copy(send_ref, send_hbm, done.at[8]), pltpu.make_async_copy(keep_ref, keep_hbm, done.at[9])
    ]
    for copy in results:
        copy.start()

    for b in range(4):
        copies[9 + b].wait()
        wide_ref[b] = slab_ref[b].astype(F32).reshape(512, 128)
        for y in range(16):
            slot = (y + 1) % 16
            turned_ref[32 * slot : 32 * slot + 32, 128 * b : 128 * b + 128] = wide_ref[
                b, pl.ds(y, 32, stride=16), :
            ].astype(BF16)
    p, x = iota((WIDE, 512), 0), iota((WIDE, 512), 1)
    gap = jnp.where(p < STRIP + 4, x - p, -9999)
    late = iota((8, 128), 0) >= 4
    for pair in range(2):
        strips = [jnp.where(gap == STRIP * t - 2, 1.0, 0.0) for t in range(4 * pair, 4 * pair + 4)]
        cut = dot_t(jnp.concatenate(strips, axis=0).astype(BF16), turned_ref[...])
        for i in range(4):
            t = 4 * pair + i
            out_ref[t, :STRIP] = cut[WIDE * i : WIDE * i + STRIP].astype(BF16)
            last = cut[WIDE * i + STRIP : WIDE * i + WIDE]
            edge = edges[t % 2]
            last = jnp.concatenate(
                [
                    jnp.where(late, pltpu.roll(edge, 4, 0), last[:, :128]),
                    jnp.where(late, edge, last[:, 128:256]),
                    last[:, 256:],
                ],
                axis=1,
            )
            out_ref[t, STRIP:] = last.astype(BF16)
            results.append(pltpu.make_async_copy(out_ref.at[t], out_hbm.at[t], done.at[t]))
            results[-1].start()
    for copy in results:
        copy.wait()


def join(keep_ref, recv_ref, pre_ref, hid_ref, ins_ref, wide_ref, thin_ref, rows_ref):
    r = lax.rem(lax.axis_index("space"), 2)
    left = r == 0
    lane = iota((PAD, 128), 1)
    tail = jnp.zeros((PAD - WIDE, 128), F32)
    own = (iota((PAD, 128), 0) >= 1) & (iota((PAD, 128), 0) <= STRIP)
    for z in range(8):
        mine = jnp.concatenate([keep_ref[z].astype(F32), tail], axis=0)
        other = jnp.concatenate([recv_ref[z].astype(F32), tail], axis=0)
        for part in range(2):
            value = jnp.where(left, mine, other) if part == 0 else jnp.where(left, other, mine)
            pre_ref[z, :, 128 * part : 128 * part + 128] = value.astype(BF16)
            hidden = jnp.where(value > 0, value, LEAK * value)
            wide_ref[PAD * z : PAD * z + PAD, 128 * part : 128 * part + 128] = jnp.where(own, hidden, 0.0)
        mine = jnp.concatenate([keep_ref[8 + z // 4].astype(F32), tail], axis=0)
        other = jnp.concatenate([recv_ref[8 + z // 4].astype(F32), tail], axis=0)
        low, high = jnp.where(left, mine, other), jnp.where(left, other, mine)
        low = pltpu.roll(low, (128 - 32 * (z % 4)) % 128, 1)
        high = pltpu.roll(high, (160 - 32 * (z % 4)) % 128, 1)
        value = jnp.where(lane < 32, low, jnp.where(lane < 64, high, 0.0))
        thin_ref[PAD * z : PAD * z + PAD, :] = value
    for part in range(2):
        turned = wide_ref[:, 128 * part : 128 * part + 128].T
        for kx in range(3):
            shifted = pltpu.roll(turned, 2 - kx, 1) if kx < 2 else turned
            for y in range(8 * part, 8 * part + 8):
                rows = shifted[16 * (y % 8) : 16 * (y % 8) + 16].astype(BF16)
                for slot in {(y + 2) % 16, y + 2}:
                    hid_ref[48 * slot + 16 * kx : 48 * slot + 16 * kx + 16, :] = rows
    turned = thin_ref[...].T[:64]
    rows_ref[...] = jnp.zeros((256, ROWS), F32)
    for kx in range(3):
        shifted = pltpu.roll(turned, 2 - kx, 1) if kx < 2 else turned
        for y in range(16):
            rows_ref[16 * y + 4 * kx : 16 * y + 4 * kx + 4, :] = shifted[4 * y : 4 * y + 4]
    ins_ref[...] = rows_ref[...].astype(BF16)


def lay(terms, rows, kz, ky):
    parts = [terms[rows * (9 * kz + 3 * ky + kx) :][:rows] for kx in range(3)]
    return jnp.where(iota((rows, 128), 1) < 64, parts[0], parts[1]), parts[2]


def band_two(two_ref, wide_ref):
    two = dot(two_ref[...], one_hot(iota((16, 128), 1) % 16 == iota((16, 128), 0)))
    group = iota((32, 128), 1) // 16 % 4
    for kz in range(3):
        terms = [lay(two, 32, kz, ky) for ky in range(3)]
        for slot in range(8):
            for half in range(2):
                block = jnp.zeros((32, 128), F32)
                for ky in range(3):
                    block = jnp.where(group == ky + slot - 2, terms[ky][half], block)
                at = 256 * kz + 32 * slot
                wide_ref[at : at + 32, 128 * half : 128 * half + 128] = block.astype(BF16)


def band_one(one_ref, thin_ref):
    one = dot(one_ref[...], one_hot(iota((4, 128), 1) // 8 % 4 == iota((4, 128), 0)))
    lane = iota((16, 128), 1)
    group = 8 * (lane // 32 % 2) + lane % 8
    for kz in range(3):
        terms = [lay(one, 16, kz, ky) for ky in range(3)]
        for y in range(16):
            for half in range(2):
                block = jnp.zeros((16, 128), F32)
                for ky in range(3):
                    block = jnp.where(group == y + ky - 1, terms[ky][half], block)
                at = 256 * kz + 16 * y
                thin_ref[at : at + 16, 128 * half : 128 * half + 128] = block.astype(BF16)


def ready_kernel(
    keep_ref, recv_ref, two_ref, pre_ref, hid_ref, ins_ref, wide_ref, hidden_ref, inputs_ref, rows_ref
):
    band_two(two_ref, wide_ref)
    join(keep_ref, recv_ref, pre_ref, hid_ref, ins_ref, hidden_ref, inputs_ref, rows_ref)


def planes(ref, kz, low, size):
    return ref[(2 - kz) * PAD : (2 - kz) * PAD + ROWS, low : low + size]


def across(sums):
    pair = sums[:, :128]
    pair = jnp.where(iota((ROWS, 128), 1) < 64, pltpu.roll(pair, ROWS - 2, 0), pltpu.roll(pair, ROWS - 1, 0))
    return pair + pltpu.roll(pair, 64, 1) + sums[:, 128:]


def grads_kernel(
    grad_ref, pre_ref, hid_ref, ins_ref, wide_ref,
    act_s, mine_ref, rest_ref, grad_s, terms_s, first_s, sums_s, raw_s,
):
    space = lax.axis_index("space")
    left = lax.rem(space, 2) == 0
    for block in (0, 9):
        grad_s[PAD * block : PAD * block + PAD, :] = jnp.zeros((PAD, 512), BF16)
        act_s[PAD * block : PAD * block + PAD, :] = jnp.zeros((PAD, 256), BF16)
    for z in range(8):
        at = PAD * (z + 1)
        grad_s[at : at + STRIP, :] = grad_ref[z, :STRIP]
        last = jnp.concatenate([grad_ref[z, STRIP:].astype(F32), jnp.zeros((PAD - WIDE, 512), F32)], axis=0)
        grad_s[at + STRIP : at + PAD, :] = last.astype(BF16)

    wide = [wide_ref[256 * kz : 256 * kz + 256, :] for kz in range(3)]
    none = jnp.zeros((32, 256), BF16)
    top = jnp.concatenate([part for w in wide for part in (none, w[32:])], axis=0)
    bottom = jnp.concatenate([part for w in wide for part in (w[:160], none, w[192:])], axis=0)
    for group in range(4):
        if group < 3:
            sides = [planes(grad_s, kz, 128 * group, 256) for kz in range(3)]
        else:
            sides = [planes(grad_s, kz, low, 128) for kz in range(3) for low in (384, 0)]
        weights = top if group == 0 else bottom if group == 3 else wide_ref[...]
        raw_s[group] = dot(jnp.concatenate(sides, axis=1), weights)
    for kz in range(3):
        for half in range(2):
            terms_s[kz, half] = dot(hid_ref[384 * half : 384 * half + 480, :], planes(grad_s, kz, 256 * half, 256))
    parts = [across(raw_s[group]) for group in range(4)]
    low = iota((ROWS, 128), 1) < 64
    act = jnp.concatenate([jnp.where(low, parts[0], parts[1]), jnp.where(low, parts[2], parts[3])], axis=1)
    row = iota((PAD, 256), 0)
    at = STRIP * space - 1 + row
    inside = (row < STRIP + 2) & (at >= 0) & (at < 512)
    edge_row = row == jnp.where(left, 0, STRIP + 1)
    side = jnp.clip(space // 2 * 2 + jnp.where(left, -2, 2), 0, 6)
    edges = [grad_ref[side + r, STRIP:, :256].astype(F32) for r in range(2)]
    for z in range(8):
        beside = [edges[r][4 + z % 4 : 5 + z % 4, 128 * (z // 4) : 128 * (z // 4) + 128] for r in range(2)]
        pre = jnp.where(edge_row, jnp.concatenate(beside, axis=1), pre_ref[z].astype(F32))
        value = act[PAD * z : PAD * z + PAD] * jnp.where(pre > 0, 1.0, LEAK)
        act_s[PAD * (z + 1) : PAD * (z + 2), :] = jnp.where(inside, value, 0.0).astype(BF16)

    for kz in range(3):
        first_s[kz] = dot(ins_ref[...], planes(act_s, kz, 0, 256))

    cells = 16 * 8 * 16 * 512
    scale = cells**-0.5
    lane = iota((16, 128), 1)
    for kz in range(3):
        for ky in range(3):
            for kx in range(3):
                total = jnp.zeros((16, 128), F32)
                for y in range(16):
                    at = y + ky - 1
                    if 0 <= at < 16:
                        slot = (y + 1) % 16
                        half = slot // 8
                        row = 48 * ((at + 2) % 16 if half == 0 else at - 6) + 16 * kx
                        col = 128 * (slot % 8 // 4)
                        piece = terms_s[kz, half, row : row + 16, col : col + 128]
                        total = total + jnp.where(lane // 32 == slot % 4, piece, 0.0)
                total = total + pltpu.roll(total, 64, 1)
                total = (total + pltpu.roll(total, 32, 1)) * scale
                tap = 9 * kz + 3 * ky + kx
                at = 16 * (tap // 4)
                if tap % 4 == 0:
                    sums_s[at : at + 16, :] = total
                else:
                    sums_s[at : at + 16, :] = jnp.where(lane // 32 == tap % 4, total, sums_s[at : at + 16, :])

    packed = jnp.zeros((16, 128), F32)
    for kz in range(3):
        for ky in range(3):
            total = jnp.zeros((16, 128), F32)
            for y in range(16):
                at = y + ky - 1
                if 0 <= at < 16:
                    piece = first_s[kz, 16 * at : 16 * at + 16, 128 * (y // 8) : 128 * (y // 8) + 128]
                    total = total + jnp.where(lane // 16 == y % 8, piece, 0.0)
            for by in (64, 32, 16):
                total = total + pltpu.roll(total, by, 1)
            total = total * scale
            if 3 * kz + ky < 8:
                packed = jnp.where(lane // 16 == 3 * kz + ky, total, packed)
            else:
                sums_s[96:112, :] = jnp.where(lane // 32 == 3, total, sums_s[96:112, :])
    sums_s[112:128, :] = packed
    first = lax.rem(lax.axis_index("dp"), 2) == 0
    mine_ref[...] = jnp.where(first, sums_s[:64, :], sums_s[64:, :])
    rest_ref[...] = jnp.where(first, sums_s[64:, :], sums_s[:64, :])


def back_kernel(act_s, one_ref, own_ref, give_ref, out_s, thin_ref):
    band_one(one_ref, thin_ref)
    left = lax.rem(lax.axis_index("space"), 2) == 0
    sides = jnp.concatenate([planes(act_s, kz, 0, 256) for kz in range(3)], axis=1)
    out_s[...] = across(dot(sides, thin_ref[...]))
    row, col = iota((64, 128), 0), iota((64, 128), 1)
    eye = one_hot(jnp.where(left, row, (row + 32) % 64) == col)
    for z in range(4):
        pair = jnp.concatenate([out_s[PAD * z : PAD * z + STRIP], out_s[PAD * (z + 4) : PAD * (z + 4) + STRIP]], axis=0)
        pair = dot_t(eye, pair.astype(BF16))
        own_ref[z] = pair[:32].astype(BF16)
        give_ref[z] = pair[32:].astype(BF16)


def tile_kernel(own_ref, recv_ref, out_ref):
    left = lax.rem(lax.axis_index("space"), 2) == 0
    low_lanes = iota((32, 128), 1) < STRIP
    for z in range(4):
        own, recv = own_ref[z].astype(F32), recv_ref[z].astype(F32)
        a, b = jnp.where(left, own, recv), jnp.where(left, recv, own)
        near = jnp.where(low_lanes, a, pltpu.roll(b, STRIP, 1))
        far = jnp.where(low_lanes, pltpu.roll(a, STRIP, 1), b)
        out_ref[:, z] = near.reshape(4, 8, 128).astype(BF16)
        out_ref[:, z + 4] = far.reshape(4, 8, 128).astype(BF16)


def unpack_kernel(mine_ref, rest_ref, one_ref, two_ref, flat_ref):
    first = lax.rem(lax.axis_index("dp"), 2) == 0
    mine, rest = mine_ref[...], rest_ref[...]
    low, high = jnp.where(first, mine, rest), jnp.where(first, rest, mine)
    blocks = [low[16 * q : 16 * q + 16] for q in range(4)] + [high[16 * q : 16 * q + 16] for q in range(4)]
    for pair in range(9):
        source, lane = (blocks[7], 16 * pair) if pair < 8 else (blocks[6], 96)
        source = pltpu.roll(source, 128 - lane, 1) if lane else source
        for kx in range(3):
            flat_ref[pl.ds(3 * pair + kx, 4, stride=32), :] = source[4 * kx : 4 * kx + 4]
    for k in range(27):
        two_ref[k] = blocks[k // 4][:, 32 * (k % 4) : 32 * (k % 4) + 32]
    turned = flat_ref[...].T
    for c in range(4):
        one_ref[c] = turned[:16, 32 * c : 32 * c + 27]


def routes():
    def number(zh, x, core, y, zl):
        return ((zh * 4 + x) * 2 + core) * 8 + y * 2 + zl

    every = list(itertools.product(range(2), range(4), range(2), range(4), range(2)))
    cores = [(number(*d), number(d[0], d[1], 1 - d[2], d[3], d[4])) for d in every]
    along_x = [[(number(*d), number(d[0], d[1] ^ j, *d[2:])) for d in every] for j in (1, 3, 2)]
    along_y = [[(number(*d), number(*d[:3], d[3] ^ j, d[4])) for d in every] for j in (1, 3, 2)]
    along_z = []
    for j in (1, 3, 2):
        pairs = []
        for d in every:
            z = (2 * d[0] + d[4]) ^ j
            pairs.append((number(*d), number(z // 2, d[1], d[2], d[3], z % 2)))
        along_z.append(pairs)
    return cores, [along_z, along_y, along_x]


def body(inputs, pre_act, out_grad, conv1_weight, conv2_weight):
    shape = jax.ShapeDtypeStruct
    cores, stages = routes()
    keep, send, strips = call(
        cut_kernel, "cut",
        [shape((10, WIDE, 128), BF16), shape((10, WIDE, 128), BF16), shape((8, WIDE, 512), BF16)],
        [
            pltpu.VMEM((4, 32, 16, 128), BF16), pltpu.VMEM((8, 16, 8, 128), BF16), pltpu.VMEM((4, 8, 8, 128), BF16),
            pltpu.VMEM((10, WIDE, 128), BF16), pltpu.VMEM((10, WIDE, 128), BF16), pltpu.VMEM((8, WIDE, 512), BF16),
            pltpu.VMEM((4, 512, 128), F32), pltpu.VMEM((512, 512), BF16),
            pltpu.SemaphoreType.DMA((13,)), pltpu.SemaphoreType.DMA((10,)),
        ],
        [out_grad[0, 0], pre_act[0, 0], inputs[0, 0]], 4e8, 2e6, limit=FULL, far_args=(0, 1, 2), far_outs=(0, 1, 2),
    )
    swap = [(i, i ^ 1) for i in range(8)]
    recv = lax.ppermute(send, "space", swap)
    strips = lax.all_to_all(strips, "space", 0, 0, tiled=True)
    pre, hid, ins, wide = call(
        ready_kernel, "ready",
        [
            shape((8, PAD, 256), BF16), shape((864, ROWS), BF16), shape((256, ROWS), BF16),
            shape((768, 256), BF16),
        ],
        [pltpu.VMEM((ROWS, 256), F32), pltpu.VMEM((ROWS, 128), F32), pltpu.VMEM((256, ROWS), F32)],
        [keep, recv, conv2_weight.transpose(0, 2, 1).reshape(864, 16)],
        2e10, 5e6, limit=SOME,
    )
    act, mine, rest = call(
        grads_kernel, "grads",
        [shape((10 * PAD, 256), BF16), shape((64, 128), F32), shape((64, 128), F32)],
        [
            pltpu.VMEM((10 * PAD, 512), BF16), pltpu.VMEM((3, 2, 480, 256), F32), pltpu.VMEM((3, 256, 256), F32),
            pltpu.VMEM((128, 128), F32), pltpu.VMEM((4, ROWS, 256), F32),
        ],
        [strips, pre, hid, ins, wide], 3e9, 4e6, limit=SOME,
    )
    own, give = call(
        back_kernel, "back", [shape((4, 32, 128), BF16), shape((4, 32, 128), BF16)], [pltpu.VMEM((ROWS, 128), F32), pltpu.VMEM((768, 256), BF16)],
        [act, conv1_weight.transpose(0, 2, 1).reshape(432, 4)], 5e8, 1e6,
    )
    total = mine + lax.ppermute(rest, ALL, cores)
    got = lax.ppermute(give, "space", swap)
    for stage in stages:
        parts = [lax.ppermute(total, ALL, pairs) for pairs in stage]
        total = (total + parts[0]) + (parts[1] + parts[2])
    other = lax.ppermute(total, ALL, cores)
    (input_grad,) = call(tile_kernel, "tile", [shape((4, 8, 8, 128), BF16)], [], [own, got], 1e6, 2e5)
    first, second = call(
        unpack_kernel, "unpack", [shape((4, 16, 27), F32), shape((27, 16, 32), F32)], [pltpu.VMEM((128, 128), F32)],
        [total, other], 1e6, 2e5,
    )
    return input_grad[None, None], first.transpose(2, 0, 1), second


def solution(mesh):
    placed = (
        P("dp", "space", None, None, None, None),
        P("dp", "space", None, None, None, None),
        P("dp", "space", None, None, None),
        P(),
        P(),
    )
    return jax.shard_map(
        body,
        mesh=mesh,
        in_specs=placed,
        out_specs=(P("dp", "space", None, None, None, None), P(), P()),
        check_vma=False,
    )
```

```python
import itertools

import jax
import jax.numpy as jnp
from jax import lax
from jax.experimental import pallas as pl
from jax.experimental.pallas import tpu as pltpu
from jax.sharding import PartitionSpec as P

LEAK = 0.3
STRIP = 64
WIDE = 72
PAD = 80
ROWS = 8 * PAD
FULL = 62
SOME = 20
ALL = ("dp", "space")
F32 = jnp.float32
BF16 = jnp.bfloat16


def iota(shape, dim):
    return lax.broadcasted_iota(jnp.int32, shape, dim)


def one_hot(flags):
    return jnp.where(flags, 1.0, 0.0).astype(BF16)


def dot(a, b):
    return jnp.dot(a, b, preferred_element_type=F32)


def dot_t(a, b):
    return lax.dot_general(a, b, (((1,), (1,)), ((), ())), preferred_element_type=F32)


def call(kernel, name, outs, scratch, args, flops, size, limit=10, far_args=(), far_outs=()):
    def spec(far):
        return pl.BlockSpec(memory_space=pltpu.HBM if far else pltpu.VMEM)

    return pl.pallas_call(
        kernel,
        name=name,
        out_shape=outs,
        in_specs=[spec(i in far_args) for i in range(len(args))],
        out_specs=[spec(i in far_outs) for i in range(len(outs))],
        scratch_shapes=scratch,
        compiler_params=pltpu.CompilerParams(vmem_limit_bytes=limit << 20),
        cost_estimate=pl.CostEstimate(flops=int(flops), bytes_accessed=int(size), transcendentals=0),
    )(*args)


def row_major():
    src, dst = iota((128, 128), 0), iota((128, 128), 1)
    return one_hot((src // 8 == dst % 16) & (src % 8 == dst // 16))


def cut_kernel(
    slab_hbm, pre_hbm, in_hbm, keep_hbm, send_hbm, out_hbm,
    slab_ref, pre_ref, in_ref, keep_ref, send_ref, out_ref, wide_ref, turned_ref, sems, done,
):
    copies = [pltpu.make_async_copy(in_hbm, in_ref, sems.at[0])]
    copies += [
        pltpu.make_async_copy(pre_hbm.at[:, z], pre_ref.at[z], sems.at[5 + z]) for z in range(8)
    ]
    copies += [
        pltpu.make_async_copy(slab_hbm.at[:, :, pl.ds(128 * b, 128)], slab_ref.at[b], sems.at[1 + b]) for b in range(4)
    ]
    for copy in copies:
        copy.start()
    r = lax.rem(lax.axis_index("space"), 2)
    a, x = iota((WIDE, 128), 0), iota((WIDE, 128), 1)
    src, dst = iota((256, 256), 0), iota((256, 256), 1)
    same = one_hot((src // 64 == dst % 4) & (src // 8 % 8 == dst // 32) & (src % 8 == dst // 4 % 8))
    order = row_major()
    gap = jnp.where(a < STRIP, x - a, -9999)
    pick = jnp.concatenate(
        [jnp.where(gap == STRIP * r, 1.0, 0.0), jnp.where(gap == STRIP * (1 - r), 1.0, 0.0)], axis=0
    ).astype(BF16)
    copies[0].wait()
    rows = in_ref[...].astype(F32).reshape(256, 128).astype(BF16)
    got = dot(dot_t(pick, rows).astype(BF16), same)
    for half in range(2):
        keep_ref[8 + half] = got[:WIDE, 128 * half : 128 * half + 128].astype(BF16)
        send_ref[8 + half] = got[WIDE:, 128 * half : 128 * half + 128].astype(BF16)
    gap = jnp.where(a < STRIP + 2, x - a, -9999)
    end = iota((16, 128), 0)
    pick = jnp.concatenate(
        [
            jnp.where(gap == STRIP * r - 1, 1.0, 0.0),
            jnp.where(gap == STRIP * (1 - r) - 1, 1.0, 0.0),
            jnp.where(iota((16, 128), 1) == jnp.where(end == 0, 127, jnp.where(end == 8, 0, -1)), 1.0, 0.0),
        ],
        axis=0,
    ).astype(BF16)
    for copy in copies[1:9]:
        copy.wait()
    got = dot_t(pick, pre_ref[...].astype(F32).reshape(1024, 128).astype(BF16)).astype(BF16)
    got = dot(jnp.concatenate([got[:, 128 * z : 128 * z + 128] for z in range(8)], axis=0), order)
    edges = [jnp.zeros((8, 128), F32)] * 2
    for z in range(8):
        at = 160 * z
        keep_ref[z] = got[at : at + WIDE].astype(BF16)
        send_ref[z] = got[at + WIDE : at + 2 * WIDE].astype(BF16)
        for i in range(2):
            edges[i] = jnp.where(iota((8, 128), 0) == z, got[at + 144 + 8 * i : at + 145 + 8 * i], edges[i])
    results = [
        pltpu.make_async_copy(send_ref, send_hbm, done.at[8]), pltpu.make_async_copy(keep_ref, keep_hbm, done.at[9])
    ]
    for copy in results:
        copy.start()

    for b in range(4):
        copies[9 + b].wait()
        wide_ref[b] = slab_ref[b].astype(F32).reshape(512, 128)
        for y in range(16):
            slot = (y + 1) % 16
            turned_ref[32 * slot : 32 * slot + 32, 128 * b : 128 * b + 128] = wide_ref[
                b, pl.ds(y, 32, stride=16), :
            ].astype(BF16)
    p, x = iota((WIDE, 512), 0), iota((WIDE, 512), 1)
    gap = jnp.where(p < STRIP + 4, x - p, -9999)
    late = iota((8, 128), 0) >= 4
    for pair in range(2):
        strips = [jnp.where(gap == STRIP * t - 2, 1.0, 0.0) for t in range(4 * pair, 4 * pair + 4)]
        cut = dot_t(jnp.concatenate(strips, axis=0).astype(BF16), turned_ref[...])
        for i in range(4):
            t = 4 * pair + i
            out_ref[t, :STRIP] = cut[WIDE * i : WIDE * i + STRIP].astype(BF16)
            last = cut[WIDE * i + STRIP : WIDE * i + WIDE]
            edge = edges[t % 2]
            last = jnp.concatenate(
                [
                    jnp.where(late, pltpu.roll(edge, 4, 0), last[:, :128]),
                    jnp.where(late, edge, last[:, 128:256]),
                    last[:, 256:],
                ],
                axis=1,
            )
            out_ref[t, STRIP:] = last.astype(BF16)
            results.append(pltpu.make_async_copy(out_ref.at[t], out_hbm.at[t], done.at[t]))
            results[-1].start()
    for copy in results:
        copy.wait()


def join(keep_ref, recv_ref, pre_ref, hid_ref, ins_ref, wide_ref, thin_ref, rows_ref):
    r = lax.rem(lax.axis_index("space"), 2)
    left = r == 0
    lane = iota((PAD, 128), 1)
    tail = jnp.zeros((PAD - WIDE, 128), F32)
    own = (iota((PAD, 128), 0) >= 1) & (iota((PAD, 128), 0) <= STRIP)
    for z in range(8):
        mine = jnp.concatenate([keep_ref[z].astype(F32), tail], axis=0)
        other = jnp.concatenate([recv_ref[z].astype(F32), tail], axis=0)
        for part in range(2):
            value = jnp.where(left, mine, other) if part == 0 else jnp.where(left, other, mine)
            pre_ref[z, :, 128 * part : 128 * part + 128] = value.astype(BF16)
            hidden = jnp.where(value > 0, value, LEAK * value)
            wide_ref[PAD * z : PAD * z + PAD, 128 * part : 128 * part + 128] = jnp.where(own, hidden, 0.0)
        mine = jnp.concatenate([keep_ref[8 + z // 4].astype(F32), tail], axis=0)
        other = jnp.concatenate([recv_ref[8 + z // 4].astype(F32), tail], axis=0)
        low, high = jnp.where(left, mine, other), jnp.where(left, other, mine)
        low = pltpu.roll(low, (128 - 32 * (z % 4)) % 128, 1)
        high = pltpu.roll(high, (160 - 32 * (z % 4)) % 128, 1)
        value = jnp.where(lane < 32, low, jnp.where(lane < 64, high, 0.0))
        thin_ref[PAD * z : PAD * z + PAD, :] = value
    for part in range(2):
        turned = wide_ref[:, 128 * part : 128 * part + 128].T
        for kx in range(3):
            shifted = pltpu.roll(turned, 2 - kx, 1) if kx < 2 else turned
            for y in range(8 * part, 8 * part + 8):
                rows = shifted[16 * (y % 8) : 16 * (y % 8) + 16].astype(BF16)
                for slot in {(y + 2) % 16, y + 2}:
                    hid_ref[48 * slot + 16 * kx : 48 * slot + 16 * kx + 16, :] = rows
    turned = thin_ref[...].T[:64]
    rows_ref[...] = jnp.zeros((256, ROWS), F32)
    for kx in range(3):
        shifted = pltpu.roll(turned, 2 - kx, 1) if kx < 2 else turned
        for y in range(16):
            rows_ref[16 * y + 4 * kx : 16 * y + 4 * kx + 4, :] = shifted[4 * y : 4 * y + 4]
    ins_ref[...] = rows_ref[...].astype(BF16)


def lay(terms, rows, kz, ky):
    parts = [terms[rows * (9 * kz + 3 * ky + kx) :][:rows] for kx in range(3)]
    return jnp.where(iota((rows, 128), 1) < 64, parts[0], parts[1]), parts[2]


def band_two(two_ref, wide_ref):
    two = dot(two_ref[...], one_hot(iota((16, 128), 1) % 16 == iota((16, 128), 0)))
    group = iota((32, 128), 1) // 16 % 4
    for kz in range(3):
        terms = [lay(two, 32, kz, ky) for ky in range(3)]
        for slot in range(8):
            for half in range(2):
                block = jnp.zeros((32, 128), F32)
                for ky in range(3):
                    block = jnp.where(group == ky + slot - 2, terms[ky][half], block)
                at = 256 * kz + 32 * slot
                wide_ref[at : at + 32, 128 * half : 128 * half + 128] = block.astype(BF16)


def band_one(one_ref, thin_ref):
    one = dot(one_ref[...], one_hot(iota((4, 128), 1) // 8 % 4 == iota((4, 128), 0)))
    lane = iota((16, 128), 1)
    group = 8 * (lane // 32 % 2) + lane % 8
    for kz in range(3):
        terms = [lay(one, 16, kz, ky) for ky in range(3)]
        for y in range(16):
            for half in range(2):
                block = jnp.zeros((16, 128), F32)
                for ky in range(3):
                    block = jnp.where(group == y + ky - 1, terms[ky][half], block)
                at = 256 * kz + 16 * y
                thin_ref[at : at + 16, 128 * half : 128 * half + 128] = block.astype(BF16)


def ready_kernel(
    keep_ref, recv_ref, two_ref, pre_ref, hid_ref, ins_ref, wide_ref, hidden_ref, inputs_ref, rows_ref
):
    band_two(two_ref, wide_ref)
    join(keep_ref, recv_ref, pre_ref, hid_ref, ins_ref, hidden_ref, inputs_ref, rows_ref)


def planes(ref, kz, low, size):
    return ref[(2 - kz) * PAD : (2 - kz) * PAD + ROWS, low : low + size]


def across(sums):
    pair = sums[:, :128]
    pair = jnp.where(iota((ROWS, 128), 1) < 64, pltpu.roll(pair, ROWS - 2, 0), pltpu.roll(pair, ROWS - 1, 0))
    return pair + pltpu.roll(pair, 64, 1) + sums[:, 128:]


def grads_kernel(
    grad_ref, pre_ref, hid_ref, ins_ref, wide_ref,
    act_s, mine_ref, rest_ref, grad_s, terms_s, first_s, sums_s, raw_s,
):
    space = lax.axis_index("space")
    left = lax.rem(space, 2) == 0
    for block in (0, 9):
        grad_s[PAD * block : PAD * block + PAD, :] = jnp.zeros((PAD, 512), BF16)
        act_s[PAD * block : PAD * block + PAD, :] = jnp.zeros((PAD, 256), BF16)
    for z in range(8):
        at = PAD * (z + 1)
        grad_s[at : at + STRIP, :] = grad_ref[z, :STRIP]
        last = jnp.concatenate([grad_ref[z, STRIP:].astype(F32), jnp.zeros((PAD - WIDE, 512), F32)], axis=0)
        grad_s[at + STRIP : at + PAD, :] = last.astype(BF16)

    wide = [wide_ref[256 * kz : 256 * kz + 256, :] for kz in range(3)]
    none = jnp.zeros((32, 256), BF16)
    top = jnp.concatenate([part for w in wide for part in (none, w[32:])], axis=0)
    bottom = jnp.concatenate([part for w in wide for part in (w[:160], none, w[192:])], axis=0)
    for group in range(4):
        if group < 3:
            sides = [planes(grad_s, kz, 128 * group, 256) for kz in range(3)]
        else:
            sides = [planes(grad_s, kz, low, 128) for kz in range(3) for low in (384, 0)]
        weights = top if group == 0 else bottom if group == 3 else wide_ref[...]
        raw_s[group] = dot(jnp.concatenate(sides, axis=1), weights)
    for kz in range(3):
        for half in range(2):
            terms_s[kz, half] = dot(hid_ref[384 * half : 384 * half + 480, :], planes(grad_s, kz, 256 * half, 256))
    parts = [across(raw_s[group]) for group in range(4)]
    low = iota((ROWS, 128), 1) < 64
    act = jnp.concatenate([jnp.where(low, parts[0], parts[1]), jnp.where(low, parts[2], parts[3])], axis=1)
    row = iota((PAD, 256), 0)
    at = STRIP * space - 1 + row
    inside = (row < STRIP + 2) & (at >= 0) & (at < 512)
    edge_row = row == jnp.where(left, 0, STRIP + 1)
    side = jnp.clip(space // 2 * 2 + jnp.where(left, -2, 2), 0, 6)
    edges = [grad_ref[side + r, STRIP:, :256].astype(F32) for r in range(2)]
    for z in range(8):
        beside = [edges[r][4 + z % 4 : 5 + z % 4, 128 * (z // 4) : 128 * (z // 4) + 128] for r in range(2)]
        pre = jnp.where(edge_row, jnp.concatenate(beside, axis=1), pre_ref[z].astype(F32))
        value = act[PAD * z : PAD * z + PAD] * jnp.where(pre > 0, 1.0, LEAK)
        act_s[PAD * (z + 1) : PAD * (z + 2), :] = jnp.where(inside, value, 0.0).astype(BF16)

    for kz in range(3):
        first_s[kz] = dot(ins_ref[...], planes(act_s, kz, 0, 256))

    cells = 16 * 8 * 16 * 512
    scale = cells**-0.5
    lane = iota((16, 128), 1)
    for kz in range(3):
        for ky in range(3):
            for kx in range(3):
                total = jnp.zeros((16, 128), F32)
                for y in range(16):
                    at = y + ky - 1
                    if 0 <= at < 16:
                        slot = (y + 1) % 16
                        half = slot // 8
                        row = 48 * ((at + 2) % 16 if half == 0 else at - 6) + 16 * kx
                        col = 128 * (slot % 8 // 4)
                        piece = terms_s[kz, half, row : row + 16, col : col + 128]
                        total = total + jnp.where(lane // 32 == slot % 4, piece, 0.0)
                total = total + pltpu.roll(total, 64, 1)
                total = (total + pltpu.roll(total, 32, 1)) * scale
                tap = 9 * kz + 3 * ky + kx
                at = 16 * (tap // 4)
                if tap % 4 == 0:
                    sums_s[at : at + 16, :] = total
                else:
                    sums_s[at : at + 16, :] = jnp.where(lane // 32 == tap % 4, total, sums_s[at : at + 16, :])

    packed = jnp.zeros((16, 128), F32)
    for kz in range(3):
        for ky in range(3):
            total = jnp.zeros((16, 128), F32)
            for y in range(16):
                at = y + ky - 1
                if 0 <= at < 16:
                    piece = first_s[kz, 16 * at : 16 * at + 16, 128 * (y // 8) : 128 * (y // 8) + 128]
                    total = total + jnp.where(lane // 16 == y % 8, piece, 0.0)
            for by in (64, 32, 16):
                total = total + pltpu.roll(total, by, 1)
            total = total * scale
            if 3 * kz + ky < 8:
                packed = jnp.where(lane // 16 == 3 * kz + ky, total, packed)
            else:
                sums_s[96:112, :] = jnp.where(lane // 32 == 3, total, sums_s[96:112, :])
    sums_s[112:128, :] = packed
    first = lax.rem(lax.axis_index("dp"), 2) == 0
    mine_ref[...] = jnp.where(first, sums_s[:64, :], sums_s[64:, :])
    rest_ref[...] = jnp.where(first, sums_s[64:, :], sums_s[:64, :])


def back_kernel(act_s, one_ref, own_ref, give_ref, out_s, thin_ref):
    band_one(one_ref, thin_ref)
    left = lax.rem(lax.axis_index("space"), 2) == 0
    sides = jnp.concatenate([planes(act_s, kz, 0, 256) for kz in range(3)], axis=1)
    out_s[...] = across(dot(sides, thin_ref[...]))
    row, col = iota((64, 128), 0), iota((64, 128), 1)
    eye = one_hot(jnp.where(left, row, (row + 32) % 64) == col)
    for z in range(4):
        pair = jnp.concatenate([out_s[PAD * z : PAD * z + STRIP], out_s[PAD * (z + 4) : PAD * (z + 4) + STRIP]], axis=0)
        pair = dot_t(eye, pair.astype(BF16))
        own_ref[z] = pair[:32].astype(BF16)
        give_ref[z] = pair[32:].astype(BF16)


def tile_kernel(own_ref, recv_ref, out_ref):
    left = lax.rem(lax.axis_index("space"), 2) == 0
    low_lanes = iota((32, 128), 1) < STRIP
    for z in range(4):
        own, recv = own_ref[z].astype(F32), recv_ref[z].astype(F32)
        a, b = jnp.where(left, own, recv), jnp.where(left, recv, own)
        near = jnp.where(low_lanes, a, pltpu.roll(b, STRIP, 1))
        far = jnp.where(low_lanes, pltpu.roll(a, STRIP, 1), b)
        out_ref[:, z] = near.reshape(4, 8, 128).astype(BF16)
        out_ref[:, z + 4] = far.reshape(4, 8, 128).astype(BF16)


def unpack_kernel(mine_ref, rest_ref, one_ref, two_ref, flat_ref):
    first = lax.rem(lax.axis_index("dp"), 2) == 0
    mine, rest = mine_ref[...], rest_ref[...]
    low, high = jnp.where(first, mine, rest), jnp.where(first, rest, mine)
    blocks = [low[16 * q : 16 * q + 16] for q in range(4)] + [high[16 * q : 16 * q + 16] for q in range(4)]
    for pair in range(9):
        source, lane = (blocks[7], 16 * pair) if pair < 8 else (blocks[6], 96)
        source = pltpu.roll(source, 128 - lane, 1) if lane else source
        for kx in range(3):
            flat_ref[pl.ds(3 * pair + kx, 4, stride=32), :] = source[4 * kx : 4 * kx + 4]
    for k in range(27):
        two_ref[k] = blocks[k // 4][:, 32 * (k % 4) : 32 * (k % 4) + 32]
    turned = flat_ref[...].T
    for c in range(4):
        one_ref[c] = turned[:16, 32 * c : 32 * c + 27]


def routes():
    def number(zh, x, core, y, zl):
        return ((zh * 4 + x) * 2 + core) * 8 + y * 2 + zl

    every = list(itertools.product(range(2), range(4), range(2), range(4), range(2)))
    cores = [(number(*d), number(d[0], d[1], 1 - d[2], d[3], d[4])) for d in every]
    along_x = [[(number(*d), number(d[0], d[1] ^ j, *d[2:])) for d in every] for j in (1, 3, 2)]
    along_y = [[(number(*d), number(*d[:3], d[3] ^ j, d[4])) for d in every] for j in (1, 3, 2)]
    along_z = []
    for j in (1, 3, 2):
        pairs = []
        for d in every:
            z = (2 * d[0] + d[4]) ^ j
            pairs.append((number(*d), number(z // 2, d[1], d[2], d[3], z % 2)))
        along_z.append(pairs)
    return cores, [along_z, along_y, along_x]


def body(inputs, pre_act, out_grad, conv1_weight, conv2_weight):
    shape = jax.ShapeDtypeStruct
    cores, stages = routes()
    keep, send, strips = call(
        cut_kernel, "cut",
        [shape((10, WIDE, 128), BF16), shape((10, WIDE, 128), BF16), shape((8, WIDE, 512), BF16)],
        [
            pltpu.VMEM((4, 32, 16, 128), BF16), pltpu.VMEM((8, 16, 8, 128), BF16), pltpu.VMEM((4, 8, 8, 128), BF16),
            pltpu.VMEM((10, WIDE, 128), BF16), pltpu.VMEM((10, WIDE, 128), BF16), pltpu.VMEM((8, WIDE, 512), BF16),
            pltpu.VMEM((4, 512, 128), F32), pltpu.VMEM((512, 512), BF16),
            pltpu.SemaphoreType.DMA((13,)), pltpu.SemaphoreType.DMA((10,)),
        ],
        [out_grad[0, 0], pre_act[0, 0], inputs[0, 0]], 4e8, 2e6, limit=FULL, far_args=(0, 1, 2), far_outs=(0, 1, 2),
    )
    swap = [(i, i ^ 1) for i in range(8)]
    recv = lax.ppermute(send, "space", swap)
    strips = lax.all_to_all(strips, "space", 0, 0, tiled=True)
    pre, hid, ins, wide = call(
        ready_kernel, "ready",
        [
            shape((8, PAD, 256), BF16), shape((864, ROWS), BF16), shape((256, ROWS), BF16),
            shape((768, 256), BF16),
        ],
        [pltpu.VMEM((ROWS, 256), F32), pltpu.VMEM((ROWS, 128), F32), pltpu.VMEM((256, ROWS), F32)],
        [keep, recv, conv2_weight.transpose(0, 2, 1).reshape(864, 16)],
        2e10, 5e6, limit=SOME,
    )
    act, mine, rest = call(
        grads_kernel, "grads",
        [shape((10 * PAD, 256), BF16), shape((64, 128), F32), shape((64, 128), F32)],
        [
            pltpu.VMEM((10 * PAD, 512), BF16), pltpu.VMEM((3, 2, 480, 256), F32), pltpu.VMEM((3, 256, 256), F32),
            pltpu.VMEM((128, 128), F32), pltpu.VMEM((4, ROWS, 256), F32),
        ],
        [strips, pre, hid, ins, wide], 3e9, 4e6, limit=SOME,
    )
    own, give = call(
        back_kernel, "back", [shape((4, 32, 128), BF16), shape((4, 32, 128), BF16)], [pltpu.VMEM((ROWS, 128), F32), pltpu.VMEM((768, 256), BF16)],
        [act, conv1_weight.transpose(0, 2, 1).reshape(432, 4)], 5e8, 1e6,
    )
    total = mine + lax.ppermute(rest, ALL, cores)
    for stage in stages:
        parts = [lax.ppermute(total, ALL, pairs) for pairs in stage]
        total = (total + parts[0]) + (parts[1] + parts[2])
        if stage is stages[0]:
            total, give = lax.optimization_barrier((total, give))
    got = lax.ppermute(give, "space", swap)
    other = lax.ppermute(total, ALL, cores)
    (input_grad,) = call(tile_kernel, "tile", [shape((4, 8, 8, 128), BF16)], [], [own, got], 1e6, 2e5)
    first, second = call(
        unpack_kernel, "unpack", [shape((4, 16, 27), F32), shape((27, 16, 32), F32)], [pltpu.VMEM((128, 128), F32)],
        [total, other], 1e6, 2e5,
    )
    return input_grad[None, None], first.transpose(2, 0, 1), second


def solution(mesh):
    placed = (
        P("dp", "space", None, None, None, None),
        P("dp", "space", None, None, None, None),
        P("dp", "space", None, None, None),
        P(),
        P(),
    )
    return jax.shard_map(
        body,
        mesh=mesh,
        in_specs=placed,
        out_specs=(P("dp", "space", None, None, None, None), P(), P()),
        check_vma=False,
    )
```

```python
import itertools

import jax
import jax.numpy as jnp
from jax import lax
from jax.experimental import pallas as pl
from jax.experimental.pallas import tpu as pltpu
from jax.sharding import PartitionSpec as P

LEAK = 0.3
STRIP = 64
WIDE = 72
PAD = 80
ROWS = 8 * PAD
FULL = 62
SOME = 20
ALL = ("dp", "space")
F32 = jnp.float32
BF16 = jnp.bfloat16


def iota(shape, dim):
    return lax.broadcasted_iota(jnp.int32, shape, dim)


def one_hot(flags):
    return jnp.where(flags, 1.0, 0.0).astype(BF16)


def dot(a, b):
    return jnp.dot(a, b, preferred_element_type=F32)


def dot_t(a, b):
    return lax.dot_general(a, b, (((1,), (1,)), ((), ())), preferred_element_type=F32)


def call(kernel, name, outs, scratch, args, flops, size, limit=10, far_args=(), far_outs=()):
    def spec(far):
        return pl.BlockSpec(memory_space=pltpu.HBM if far else pltpu.VMEM)

    return pl.pallas_call(
        kernel,
        name=name,
        out_shape=outs,
        in_specs=[spec(i in far_args) for i in range(len(args))],
        out_specs=[spec(i in far_outs) for i in range(len(outs))],
        scratch_shapes=scratch,
        compiler_params=pltpu.CompilerParams(vmem_limit_bytes=limit << 20),
        cost_estimate=pl.CostEstimate(flops=int(flops), bytes_accessed=int(size), transcendentals=0),
    )(*args)


def row_major():
    src, dst = iota((128, 128), 0), iota((128, 128), 1)
    return one_hot((src // 8 == dst % 16) & (src % 8 == dst // 16))


def cut_kernel(
    slab_hbm, pre_hbm, in_hbm, keep_hbm, send_hbm, out_hbm,
    slab_ref, pre_ref, in_ref, keep_ref, send_ref, out_ref, wide_ref, turned_ref, sems, done,
):
    copies = [pltpu.make_async_copy(in_hbm, in_ref, sems.at[0])]
    copies += [
        pltpu.make_async_copy(pre_hbm.at[:, z], pre_ref.at[z], sems.at[5 + z]) for z in range(8)
    ]
    copies += [
        pltpu.make_async_copy(slab_hbm.at[:, :, pl.ds(128 * b, 128)], slab_ref.at[b], sems.at[1 + b]) for b in range(4)
    ]
    for copy in copies:
        copy.start()
    r = lax.rem(lax.axis_index("space"), 2)
    a, x = iota((WIDE, 128), 0), iota((WIDE, 128), 1)
    src, dst = iota((256, 256), 0), iota((256, 256), 1)
    same = one_hot((src // 64 == dst % 4) & (src // 8 % 8 == dst // 32) & (src % 8 == dst // 4 % 8))
    order = row_major()
    gap = jnp.where(a < STRIP, x - a, -9999)
    pick = jnp.concatenate(
        [jnp.where(gap == STRIP * r, 1.0, 0.0), jnp.where(gap == STRIP * (1 - r), 1.0, 0.0)], axis=0
    ).astype(BF16)
    copies[0].wait()
    rows = in_ref[...].astype(F32).reshape(256, 128).astype(BF16)
    got = dot(dot_t(pick, rows).astype(BF16), same)
    for half in range(2):
        keep_ref[8 + half] = got[:WIDE, 128 * half : 128 * half + 128].astype(BF16)
        send_ref[8 + half] = got[WIDE:, 128 * half : 128 * half + 128].astype(BF16)
    gap = jnp.where(a < STRIP + 2, x - a, -9999)
    end = iota((16, 128), 0)
    pick = jnp.concatenate(
        [
            jnp.where(gap == STRIP * r - 1, 1.0, 0.0),
            jnp.where(gap == STRIP * (1 - r) - 1, 1.0, 0.0),
            jnp.where(iota((16, 128), 1) == jnp.where(end == 0, 127, jnp.where(end == 8, 0, -1)), 1.0, 0.0),
        ],
        axis=0,
    ).astype(BF16)
    for copy in copies[1:9]:
        copy.wait()
    got = dot_t(pick, pre_ref[...].astype(F32).reshape(1024, 128).astype(BF16)).astype(BF16)
    got = dot(jnp.concatenate([got[:, 128 * z : 128 * z + 128] for z in range(8)], axis=0), order)
    edges = [jnp.zeros((8, 128), F32)] * 2
    for z in range(8):
        at = 160 * z
        keep_ref[z] = got[at : at + WIDE].astype(BF16)
        send_ref[z] = got[at + WIDE : at + 2 * WIDE].astype(BF16)
        for i in range(2):
            edges[i] = jnp.where(iota((8, 128), 0) == z, got[at + 144 + 8 * i : at + 145 + 8 * i], edges[i])
    results = [
        pltpu.make_async_copy(send_ref, send_hbm, done.at[8]), pltpu.make_async_copy(keep_ref, keep_hbm, done.at[9])
    ]
    for copy in results:
        copy.start()

    for b in range(4):
        copies[9 + b].wait()
        wide_ref[b] = slab_ref[b].astype(F32).reshape(512, 128)
        for y in range(16):
            slot = (y + 1) % 16
            turned_ref[32 * slot : 32 * slot + 32, 128 * b : 128 * b + 128] = wide_ref[
                b, pl.ds(y, 32, stride=16), :
            ].astype(BF16)
    p, x = iota((WIDE, 512), 0), iota((WIDE, 512), 1)
    gap = jnp.where(p < STRIP + 4, x - p, -9999)
    late = iota((8, 128), 0) >= 4
    for pair in range(2):
        strips = [jnp.where(gap == STRIP * t - 2, 1.0, 0.0) for t in range(4 * pair, 4 * pair + 4)]
        cut = dot_t(jnp.concatenate(strips, axis=0).astype(BF16), turned_ref[...])
        for i in range(4):
            t = 4 * pair + i
            out_ref[t, :STRIP] = cut[WIDE * i : WIDE * i + STRIP].astype(BF16)
            last = cut[WIDE * i + STRIP : WIDE * i + WIDE]
            edge = edges[t % 2]
            last = jnp.concatenate(
                [
                    jnp.where(late, pltpu.roll(edge, 4, 0), last[:, :128]),
                    jnp.where(late, edge, last[:, 128:256]),
                    last[:, 256:],
                ],
                axis=1,
            )
            out_ref[t, STRIP:] = last.astype(BF16)
            results.append(pltpu.make_async_copy(out_ref.at[t], out_hbm.at[t], done.at[t]))
            results[-1].start()
    for copy in results:
        copy.wait()


def join(keep_ref, recv_ref, pre_ref, hid_ref, ins_ref, wide_ref, thin_ref, rows_ref):
    r = lax.rem(lax.axis_index("space"), 2)
    left = r == 0
    lane = iota((PAD, 128), 1)
    tail = jnp.zeros((PAD - WIDE, 128), F32)
    own = (iota((PAD, 128), 0) >= 1) & (iota((PAD, 128), 0) <= STRIP)
    for z in range(8):
        mine = jnp.concatenate([keep_ref[z].astype(F32), tail], axis=0)
        other = jnp.concatenate([recv_ref[z].astype(F32), tail], axis=0)
        for part in range(2):
            value = jnp.where(left, mine, other) if part == 0 else jnp.where(left, other, mine)
            pre_ref[z, :, 128 * part : 128 * part + 128] = value.astype(BF16)
            hidden = jnp.where(value > 0, value, LEAK * value)
            wide_ref[PAD * z : PAD * z + PAD, 128 * part : 128 * part + 128] = jnp.where(own, hidden, 0.0)
        mine = jnp.concatenate([keep_ref[8 + z // 4].astype(F32), tail], axis=0)
        other = jnp.concatenate([recv_ref[8 + z // 4].astype(F32), tail], axis=0)
        low, high = jnp.where(left, mine, other), jnp.where(left, other, mine)
        low = pltpu.roll(low, (128 - 32 * (z % 4)) % 128, 1)
        high = pltpu.roll(high, (160 - 32 * (z % 4)) % 128, 1)
        value = jnp.where(lane < 32, low, jnp.where(lane < 64, high, 0.0))
        thin_ref[PAD * z : PAD * z + PAD, :] = value
    for part in range(2):
        turned = wide_ref[:, 128 * part : 128 * part + 128].T
        for kx in range(3):
            shifted = pltpu.roll(turned, 2 - kx, 1) if kx < 2 else turned
            for y in range(8 * part, 8 * part + 8):
                rows = shifted[16 * (y % 8) : 16 * (y % 8) + 16].astype(BF16)
                for slot in {(y + 2) % 16, y + 2}:
                    hid_ref[48 * slot + 16 * kx : 48 * slot + 16 * kx + 16, :] = rows
    turned = thin_ref[...].T[:64]
    rows_ref[...] = jnp.zeros((256, ROWS), F32)
    for kx in range(3):
        shifted = pltpu.roll(turned, 2 - kx, 1) if kx < 2 else turned
        for y in range(16):
            rows_ref[16 * y + 4 * kx : 16 * y + 4 * kx + 4, :] = shifted[4 * y : 4 * y + 4]
    ins_ref[...] = rows_ref[...].astype(BF16)


def lay(terms, rows, kz, ky):
    parts = [terms[rows * (9 * kz + 3 * ky + kx) :][:rows] for kx in range(3)]
    return jnp.where(iota((rows, 128), 1) < 64, parts[0], parts[1]), parts[2]


def band_two(two_ref, wide_ref):
    two = dot(two_ref[...], one_hot(iota((16, 128), 1) % 16 == iota((16, 128), 0)))
    group = iota((32, 128), 1) // 16 % 4
    for kz in range(3):
        terms = [lay(two, 32, kz, ky) for ky in range(3)]
        for slot in range(8):
            for half in range(2):
                block = jnp.zeros((32, 128), F32)
                for ky in range(3):
                    block = jnp.where(group == ky + slot - 2, terms[ky][half], block)
                at = 256 * kz + 32 * slot
                wide_ref[at : at + 32, 128 * half : 128 * half + 128] = block.astype(BF16)


def band_one(one_ref, thin_ref):
    one = dot(one_ref[...], one_hot(iota((4, 128), 1) // 8 % 4 == iota((4, 128), 0)))
    lane = iota((16, 128), 1)
    group = 8 * (lane // 32 % 2) + lane % 8
    for kz in range(3):
        terms = [lay(one, 16, kz, ky) for ky in range(3)]
        for y in range(16):
            for half in range(2):
                block = jnp.zeros((16, 128), F32)
                for ky in range(3):
                    block = jnp.where(group == y + ky - 1, terms[ky][half], block)
                at = 256 * kz + 16 * y
                thin_ref[at : at + 16, 128 * half : 128 * half + 128] = block.astype(BF16)


def ready_kernel(
    keep_ref, recv_ref, two_ref, pre_ref, hid_ref, ins_ref, wide_ref, hidden_ref, inputs_ref, rows_ref
):
    band_two(two_ref, wide_ref)
    join(keep_ref, recv_ref, pre_ref, hid_ref, ins_ref, hidden_ref, inputs_ref, rows_ref)


def planes(ref, kz, low, size):
    return ref[(2 - kz) * PAD : (2 - kz) * PAD + ROWS, low : low + size]


def across(sums):
    pair = sums[:, :128]
    pair = jnp.where(iota((ROWS, 128), 1) < 64, pltpu.roll(pair, ROWS - 2, 0), pltpu.roll(pair, ROWS - 1, 0))
    return pair + pltpu.roll(pair, 64, 1) + sums[:, 128:]


def grads_kernel(
    grad_ref, pre_ref, hid_ref, ins_ref, wide_ref,
    act_s, mine_ref, rest_ref, grad_s, terms_s, first_s, sums_s, raw_s,
):
    space = lax.axis_index("space")
    left = lax.rem(space, 2) == 0
    for block in (0, 9):
        grad_s[PAD * block : PAD * block + PAD, :] = jnp.zeros((PAD, 512), BF16)
        act_s[PAD * block : PAD * block + PAD, :] = jnp.zeros((PAD, 256), BF16)
    for z in range(8):
        at = PAD * (z + 1)
        grad_s[at : at + STRIP, :] = grad_ref[z, :STRIP]
        last = jnp.concatenate([grad_ref[z, STRIP:].astype(F32), jnp.zeros((PAD - WIDE, 512), F32)], axis=0)
        grad_s[at + STRIP : at + PAD, :] = last.astype(BF16)

    wide = [wide_ref[256 * kz : 256 * kz + 256, :] for kz in range(3)]
    none = jnp.zeros((32, 256), BF16)
    top = jnp.concatenate([part for w in wide for part in (none, w[32:])], axis=0)
    bottom = jnp.concatenate([part for w in wide for part in (w[:160], none, w[192:])], axis=0)
    for group in range(4):
        if group < 3:
            sides = [planes(grad_s, kz, 128 * group, 256) for kz in range(3)]
        else:
            sides = [planes(grad_s, kz, low, 128) for kz in range(3) for low in (384, 0)]
        weights = top if group == 0 else bottom if group == 3 else wide_ref[...]
        raw_s[group] = dot(jnp.concatenate(sides, axis=1), weights)
    for kz in range(3):
        for half in range(2):
            terms_s[kz, half] = dot(hid_ref[384 * half : 384 * half + 480, :], planes(grad_s, kz, 256 * half, 256))
    parts = [across(raw_s[group]) for group in range(4)]
    low = iota((ROWS, 128), 1) < 64
    act = jnp.concatenate([jnp.where(low, parts[0], parts[1]), jnp.where(low, parts[2], parts[3])], axis=1)
    row = iota((PAD, 256), 0)
    at = STRIP * space - 1 + row
    inside = (row < STRIP + 2) & (at >= 0) & (at < 512)
    edge_row = row == jnp.where(left, 0, STRIP + 1)
    side = jnp.clip(space // 2 * 2 + jnp.where(left, -2, 2), 0, 6)
    edges = [grad_ref[side + r, STRIP:, :256].astype(F32) for r in range(2)]
    for z in range(8):
        beside = [edges[r][4 + z % 4 : 5 + z % 4, 128 * (z // 4) : 128 * (z // 4) + 128] for r in range(2)]
        pre = jnp.where(edge_row, jnp.concatenate(beside, axis=1), pre_ref[z].astype(F32))
        value = act[PAD * z : PAD * z + PAD] * jnp.where(pre > 0, 1.0, LEAK)
        act_s[PAD * (z + 1) : PAD * (z + 2), :] = jnp.where(inside, value, 0.0).astype(BF16)

    for kz in range(3):
        first_s[kz] = dot(ins_ref[...], planes(act_s, kz, 0, 256))

    cells = 16 * 8 * 16 * 512
    scale = cells**-0.5
    lane = iota((16, 128), 1)
    for kz in range(3):
        for ky in range(3):
            for kx in range(3):
                total = jnp.zeros((16, 128), F32)
                for y in range(16):
                    at = y + ky - 1
                    if 0 <= at < 16:
                        slot = (y + 1) % 16
                        half = slot // 8
                        row = 48 * ((at + 2) % 16 if half == 0 else at - 6) + 16 * kx
                        col = 128 * (slot % 8 // 4)
                        piece = terms_s[kz, half, row : row + 16, col : col + 128]
                        total = total + jnp.where(lane // 32 == slot % 4, piece, 0.0)
                total = total + pltpu.roll(total, 64, 1)
                total = (total + pltpu.roll(total, 32, 1)) * scale
                tap = 9 * kz + 3 * ky + kx
                at = 16 * (tap // 4)
                if tap % 4 == 0:
                    sums_s[at : at + 16, :] = total
                else:
                    sums_s[at : at + 16, :] = jnp.where(lane // 32 == tap % 4, total, sums_s[at : at + 16, :])

    packed = jnp.zeros((16, 128), F32)
    for kz in range(3):
        for ky in range(3):
            total = jnp.zeros((16, 128), F32)
            for y in range(16):
                at = y + ky - 1
                if 0 <= at < 16:
                    piece = first_s[kz, 16 * at : 16 * at + 16, 128 * (y // 8) : 128 * (y // 8) + 128]
                    total = total + jnp.where(lane // 16 == y % 8, piece, 0.0)
            for by in (64, 32, 16):
                total = total + pltpu.roll(total, by, 1)
            total = total * scale
            if 3 * kz + ky < 8:
                packed = jnp.where(lane // 16 == 3 * kz + ky, total, packed)
            else:
                sums_s[96:112, :] = jnp.where(lane // 32 == 3, total, sums_s[96:112, :])
    sums_s[112:128, :] = packed
    first = lax.rem(lax.axis_index("dp"), 2) == 0
    mine_ref[...] = jnp.where(first, sums_s[:64, :], sums_s[64:, :])
    rest_ref[...] = jnp.where(first, sums_s[64:, :], sums_s[:64, :])


def back_kernel(act_s, one_ref, own_ref, give_ref, out_s, thin_ref):
    band_one(one_ref, thin_ref)
    left = lax.rem(lax.axis_index("space"), 2) == 0
    sides = jnp.concatenate([planes(act_s, kz, 0, 256) for kz in range(3)], axis=1)
    out_s[...] = across(dot(sides, thin_ref[...]))
    row, col = iota((64, 128), 0), iota((64, 128), 1)
    eye = one_hot(jnp.where(left, row, (row + 32) % 64) == col)
    for z in range(4):
        pair = jnp.concatenate([out_s[PAD * z : PAD * z + STRIP], out_s[PAD * (z + 4) : PAD * (z + 4) + STRIP]], axis=0)
        pair = dot_t(eye, pair.astype(BF16))
        own_ref[z] = pair[:32].astype(BF16)
        give_ref[z] = pair[32:].astype(BF16)


def tile_kernel(own_ref, recv_ref, out_ref):
    left = lax.rem(lax.axis_index("space"), 2) == 0
    low_lanes = iota((32, 128), 1) < STRIP
    for z in range(4):
        own, recv = own_ref[z].astype(F32), recv_ref[z].astype(F32)
        a, b = jnp.where(left, own, recv), jnp.where(left, recv, own)
        near = jnp.where(low_lanes, a, pltpu.roll(b, STRIP, 1))
        far = jnp.where(low_lanes, pltpu.roll(a, STRIP, 1), b)
        out_ref[:, z] = near.reshape(4, 8, 128).astype(BF16)
        out_ref[:, z + 4] = far.reshape(4, 8, 128).astype(BF16)


def unpack_kernel(mine_ref, rest_ref, one_ref, two_ref, flat_ref):
    first = lax.rem(lax.axis_index("dp"), 2) == 0
    mine, rest = mine_ref[...], rest_ref[...]
    low, high = jnp.where(first, mine, rest), jnp.where(first, rest, mine)
    blocks = [low[16 * q : 16 * q + 16] for q in range(4)] + [high[16 * q : 16 * q + 16] for q in range(4)]
    for pair in range(9):
        source, lane = (blocks[7], 16 * pair) if pair < 8 else (blocks[6], 96)
        source = pltpu.roll(source, 128 - lane, 1) if lane else source
        for kx in range(3):
            flat_ref[pl.ds(3 * pair + kx, 4, stride=32), :] = source[4 * kx : 4 * kx + 4]
    for k in range(27):
        two_ref[k] = blocks[k // 4][:, 32 * (k % 4) : 32 * (k % 4) + 32]
    turned = flat_ref[...].T
    for c in range(4):
        one_ref[c] = turned[:16, 32 * c : 32 * c + 27]


def routes():
    def number(zh, x, core, y, zl):
        return ((zh * 4 + x) * 2 + core) * 8 + y * 2 + zl

    every = list(itertools.product(range(2), range(4), range(2), range(4), range(2)))
    cores = [(number(*d), number(d[0], d[1], 1 - d[2], d[3], d[4])) for d in every]
    along_x = [[(number(*d), number(d[0], d[1] ^ j, *d[2:])) for d in every] for j in (1, 3, 2)]
    along_y = [[(number(*d), number(*d[:3], d[3] ^ j, d[4])) for d in every] for j in (1, 3, 2)]
    along_z = []
    for j in (1, 3, 2):
        pairs = []
        for d in every:
            z = (2 * d[0] + d[4]) ^ j
            pairs.append((number(*d), number(z // 2, d[1], d[2], d[3], z % 2)))
        along_z.append(pairs)
    return cores, [along_y, along_z, along_x]


def body(inputs, pre_act, out_grad, conv1_weight, conv2_weight):
    shape = jax.ShapeDtypeStruct
    cores, stages = routes()
    keep, send, strips = call(
        cut_kernel, "cut",
        [shape((10, WIDE, 128), BF16), shape((10, WIDE, 128), BF16), shape((8, WIDE, 512), BF16)],
        [
            pltpu.VMEM((4, 32, 16, 128), BF16), pltpu.VMEM((8, 16, 8, 128), BF16), pltpu.VMEM((4, 8, 8, 128), BF16),
            pltpu.VMEM((10, WIDE, 128), BF16), pltpu.VMEM((10, WIDE, 128), BF16), pltpu.VMEM((8, WIDE, 512), BF16),
            pltpu.VMEM((4, 512, 128), F32), pltpu.VMEM((512, 512), BF16),
            pltpu.SemaphoreType.DMA((13,)), pltpu.SemaphoreType.DMA((10,)),
        ],
        [out_grad[0, 0], pre_act[0, 0], inputs[0, 0]], 4e8, 2e6, limit=FULL, far_args=(0, 1, 2), far_outs=(0, 1, 2),
    )
    swap = [(i, i ^ 1) for i in range(8)]
    recv = lax.ppermute(send, "space", swap)
    strips = lax.all_to_all(strips, "space", 0, 0, tiled=True)
    pre, hid, ins, wide = call(
        ready_kernel, "ready",
        [
            shape((8, PAD, 256), BF16), shape((864, ROWS), BF16), shape((256, ROWS), BF16),
            shape((768, 256), BF16),
        ],
        [pltpu.VMEM((ROWS, 256), F32), pltpu.VMEM((ROWS, 128), F32), pltpu.VMEM((256, ROWS), F32)],
        [keep, recv, conv2_weight.transpose(0, 2, 1).reshape(864, 16)],
        2e10, 5e6, limit=SOME,
    )
    act, mine, rest = call(
        grads_kernel, "grads",
        [shape((10 * PAD, 256), BF16), shape((64, 128), F32), shape((64, 128), F32)],
        [
            pltpu.VMEM((10 * PAD, 512), BF16), pltpu.VMEM((3, 2, 480, 256), F32), pltpu.VMEM((3, 256, 256), F32),
            pltpu.VMEM((128, 128), F32), pltpu.VMEM((4, ROWS, 256), F32),
        ],
        [strips, pre, hid, ins, wide], 3e9, 4e6, limit=SOME,
    )
    own, give = call(
        back_kernel, "back", [shape((4, 32, 128), BF16), shape((4, 32, 128), BF16)], [pltpu.VMEM((ROWS, 128), F32), pltpu.VMEM((768, 256), BF16)],
        [act, conv1_weight.transpose(0, 2, 1).reshape(432, 4)], 5e8, 1e6,
    )
    total = mine + lax.ppermute(rest, ALL, cores)
    got = lax.ppermute(give, "space", swap)
    for stage in stages:
        parts = [lax.ppermute(total, ALL, pairs) for pairs in stage]
        total = (total + parts[0]) + (parts[1] + parts[2])
    other = lax.ppermute(total, ALL, cores)
    (input_grad,) = call(tile_kernel, "tile", [shape((4, 8, 8, 128), BF16)], [], [own, got], 1e6, 2e5)
    first, second = call(
        unpack_kernel, "unpack", [shape((4, 16, 27), F32), shape((27, 16, 32), F32)], [pltpu.VMEM((128, 128), F32)],
        [total, other], 1e6, 2e5,
    )
    return input_grad[None, None], first.transpose(2, 0, 1), second


def solution(mesh):
    placed = (
        P("dp", "space", None, None, None, None),
        P("dp", "space", None, None, None, None),
        P("dp", "space", None, None, None),
        P(),
        P(),
    )
    return jax.shard_map(
        body,
        mesh=mesh,
        in_specs=placed,
        out_specs=(P("dp", "space", None, None, None, None), P(), P()),
        check_vma=False,
    )
```
